32 devices in a mesh: dp: 4 (over y, core), tensor: 8 (over z, x).
Axes of the slice: x: 2, y: 2, z: 4, core: 2. Of those that a mesh axis runs over, the one named last changes fastest.
Arguments:
- layer_inputs: bfloat16 [4, 1536, 2048], P(None, 'dp'), may hold values from -6 to 6
- history: bfloat16 [3, 1536, 2048], P(None, None, 'dp'), may hold values from -6 to 6
- seq_ids: int32 [1536], P('dp'), may hold values from -1 to 14, as said below
- norms_master: float32 [9, 2048], P(None, 'dp'), may hold values from -4 to 4
- norms_first: float32 [9, 2048], P(None, 'dp'), may hold values from -1 to 1
- norms_second: float32 [9, 2048], P(None, 'dp'), may hold values from 0 to 1
- attend_in_master: float32 [3, 2048, 2048], P(None, 'dp', 'tensor'), may hold values from -1 to 1
- attend_in_first: float32 [3, 2048, 2048], P(None, 'dp', 'tensor'), may hold values from -1 to 1
- attend_in_second: float32 [3, 2048, 2048], P(None, 'dp', 'tensor'), may hold values from 0 to 1
- attend_out_master: float32 [2048, 2048], P('tensor', 'dp'), may hold values from -4 to 4
- attend_out_first: float32 [2048, 2048], P('tensor', 'dp'), may hold values from -1 to 1
- attend_out_second: float32 [2048, 2048], P('tensor', 'dp'), may hold values from 0 to 1
- expand_master: float32 [2048, 8192], P('dp', 'tensor'), may hold values from -1 to 1
- expand_first: float32 [2048, 8192], P('dp', 'tensor'), may hold values from -1 to 1
- expand_second: float32 [2048, 8192], P('dp', 'tensor'), may hold values from 0 to 1
- project_master: float32 [8192, 2048], P('tensor', 'dp'), may hold values from -1 to 1
- project_first: float32 [8192, 2048], P('tensor', 'dp'), may hold values from -1 to 1
- project_second: float32 [8192, 2048], P('tensor', 'dp'), may hold values from 0 to 1
- mixer_in_master: float32 [2048, 36], P('dp'), may hold values from -0.125 to 0.125
- mixer_in_first: float32 [2048, 36], P('dp'), may hold values from -1 to 1
- mixer_in_second: float32 [2048, 36], P('dp'), may hold values from 0 to 1
- mixer_out_master: float32 [16, 36], P('dp'), may hold values from -1 to 1
- mixer_out_first: float32 [16, 36], P('dp'), may hold values from -1 to 1
- mixer_out_second: float32 [16, 36], P('dp'), may hold values from 0 to 1
- next_cotangent: bfloat16 [4, 1536, 2048], P(None, 'dp'), may hold values from -16 to 16
- grad_entry: bfloat16 [1536, 2048], P(None, 'dp'), may hold values from -16 to 16
Outputs:
- next_inputs: bfloat16 [4, 1536, 2048], P(None, 'dp')
- new_entry: bfloat16 [1536, 2048], P(None, 'dp')
- grad_inputs: bfloat16 [4, 1536, 2048], P(None, 'dp')
- grad_history: bfloat16 [3, 1536, 2048], P(None, None, 'dp')
- norms_new: float32 [9, 2048], P(None, 'dp')
- norms_first_new: float32 [9, 2048], P(None, 'dp')
- norms_second_new: float32 [9, 2048], P(None, 'dp')
- attend_in_new: float32 [3, 2048, 2048], P(None, 'dp', 'tensor')
- attend_in_first_new: float32 [3, 2048, 2048], P(None, 'dp', 'tensor')
- attend_in_second_new: float32 [3, 2048, 2048], P(None, 'dp', 'tensor')
- attend_in_copy: bfloat16 [3, 2048, 2048], P(None, 'dp', 'tensor')
- attend_out_new: float32 [2048, 2048], P('tensor', 'dp')
- attend_out_first_new: float32 [2048, 2048], P('tensor', 'dp')
- attend_out_second_new: float32 [2048, 2048], P('tensor', 'dp')
- attend_out_copy: bfloat16 [2048, 2048], P('tensor', 'dp')
- expand_new: float32 [2048, 8192], P('dp', 'tensor')
- expand_first_new: float32 [2048, 8192], P('dp', 'tensor')
- expand_second_new: float32 [2048, 8192], P('dp', 'tensor')
- expand_copy: bfloat16 [2048, 8192], P('dp', 'tensor')
- project_new: float32 [8192, 2048], P('tensor', 'dp')
- project_first_new: float32 [8192, 2048], P('tensor', 'dp')
- project_second_new: float32 [8192, 2048], P('tensor', 'dp')
- project_copy: bfloat16 [8192, 2048], P('tensor', 'dp')
- mixer_in_new: float32 [2048, 36], P('dp')
- mixer_in_first_new: float32 [2048, 36], P('dp')
- mixer_in_second_new: float32 [2048, 36], P('dp')
- mixer_in_copy: bfloat16 [2048, 36], P('dp')
- mixer_out_new: float32 [16, 36], P('dp')
- mixer_out_first_new: float32 [16, 36], P('dp')
- mixer_out_second_new: float32 [16, 36], P('dp')
- mixer_out_copy: bfloat16 [16, 36], P('dp')
- grad_norm: float32 [], replicated
The draws below stay inside these ranges and needn't reach their ends.
Inputs may be any that keep to these rules, and one draw needn't show every extreme that they name: `seq_ids`: slots 384 k to 384 (k + 1) - 1 form bucket k. In a bucket the ids of real tokens come first, never fall, and lie in 4 k to 4 k + 2; equal ids are consecutive; the rest of the bucket is padding with id -1. The share of real tokens rises from about a third in bucket 0 to all of the last bucket.
All inputs are finite; a program needn't handle non-finite values.
Results may differ from the reference program's by a relative error of at most 0.018.
The reference program's roundings to bfloat16 on the way count: a program that leaves them out, or rounds other values in their place, can miss the bound.
Values may be sent and summed in bfloat16 or wider, within the bound.
No kernel may reach another device: no remote copies, remote signals or barrier semaphores. Data moves between devices by JAX's collectives and lax.ppermute only.
A program may use at most 256 MiB of HBM per device.

```python
import math
import jax
import jax.numpy as jnp
from jax import lax

D = 2048
HEADS = 16
HDIM = 128
FF = 8192
MIXH = 36
ROT = 32
STORED = 3
STEP = 10
TOK_DEV = 384
MIX = 4
BUCKETS = 4
TOKENS = 1536


clip_level = 1.0


beta_first = 0.9


beta_second = 0.95


def ramp(count, start, stop):
    return start + (stop - start) * jnp.arange(count).astype(jnp.float32) / max(count - 1, 1)


def ramped_normal(key, shape, fan_in, axis, start, stop):
    values = jax.random.normal(key, shape, jnp.float32) / math.sqrt(fan_in)
    view = [1] * len(shape)
    view[axis] = shape[axis]
    return values * ramp(shape[axis], start, stop).reshape(view)


def entry_level(multiple):
    count = 4 * D * D + 2 * D * FF + 9 * D + D * MIXH + 4 * MIX * MIXH
    return multiple * clip_level / math.sqrt(count)


def first_draw(key, shape, level):
    sign_key, size_key = jax.random.split(key)
    signs = jnp.where(jax.random.bernoulli(sign_key, 0.5, shape), 1.0, -1.0)
    magnitude = jnp.exp(jax.random.uniform(size_key, shape, jnp.float32, math.log(0.5), math.log(2.0)))
    return (signs * magnitude * level * (1.0 - beta_first) / beta_first).astype(jnp.float32)


def second_draw(key, shape, level):
    base_key, spread_key = jax.random.split(key)
    base = jax.random.uniform(base_key, shape, jnp.float32, 1.0, 4.0)
    spread = jnp.exp(jax.random.uniform(spread_key, shape, jnp.float32, math.log(0.5), math.log(2.0)))
    return (base * spread * level * level * (1.0 - beta_second) / beta_second).astype(jnp.float32)


def draw_seq_ids(key, part):
    key = jax.random.fold_in(key, 5)
    drop_key, first_key, second_key = jax.random.split(key, 3)
    bucket = jnp.arange(BUCKETS, dtype=jnp.int32)
    target = TOK_DEV // 3 + (TOK_DEV - TOK_DEV // 3) * bucket // (BUCKETS - 1)
    shortfall = jax.random.randint(drop_key, (BUCKETS,), 0, TOK_DEV // 8 + 1)
    filled = jnp.where(bucket == BUCKETS - 1, TOK_DEV, target - shortfall)
    first_cut = 1 + jax.random.randint(first_key, (BUCKETS,), 0, 1 << 20) % (filled - 1)
    second_cut = 1 + jax.random.randint(second_key, (BUCKETS,), 0, 1 << 20) % (filled - 1)
    lower = jnp.minimum(first_cut, second_cut)
    upper = jnp.maximum(first_cut, second_cut)
    slot = jnp.arange(TOK_DEV, dtype=jnp.int32)[None, :]
    segment = (slot >= lower[:, None]).astype(jnp.int32) + (slot >= upper[:, None]).astype(jnp.int32)
    ids = jnp.where(slot < filled[:, None], 4 * bucket[:, None] + segment, -1)
    return ids.reshape(TOKENS).astype(jnp.int32)


def draw_norms_master(key, part):
    key = jax.random.fold_in(key, 7)
    gain_key, bias_key = jax.random.split(key)
    start, stop = (0.6, 1.8)
    biases = 0.3 * jax.random.normal(bias_key, (4, D), jnp.float32)
    gains = ramp(D, start, stop)[None, :] * jax.random.uniform(gain_key, (5, D), jnp.float32, 0.8, 1.2)
    return jnp.concatenate([gains[0:4], biases, gains[4:5]], axis=0).astype(jnp.float32)


def weight_ends():
    return (0.5, 1.5)


def draw_attend_in_master(key, part):
    key = jax.random.fold_in(key, 11)
    pair_key, value_key = jax.random.split(key)
    start, stop = weight_ends()
    pair = jax.random.normal(pair_key, (2, D, D), jnp.float32) / math.sqrt(D)
    values = ramped_normal(value_key, (1, D, D), D, 2, start, stop)
    return jnp.concatenate([pair, values], axis=0).astype(jnp.float32)


def draw_attend_out_master(key, part):
    key = jax.random.fold_in(key, 13)
    start, stop = weight_ends()
    values = ramped_normal(key, (D, D), D // 32, 0, start, stop)
    return jnp.clip(values, -4.0, 4.0).astype(jnp.float32)


def draw_expand_master(key, part):
    key = jax.random.fold_in(key, 17)
    start, stop = weight_ends()
    return ramped_normal(key, (D, FF), D, 1, start, stop).astype(jnp.float32)


def draw_project_master(key, part):
    key = jax.random.fold_in(key, 19)
    start, stop = weight_ends()
    return ramped_normal(key, (FF, D), FF, 0, start, stop).astype(jnp.float32)


def cotangent_draw(key, shape):
    start, stop = (0.6, 1.8)
    values = jax.random.normal(key, shape, jnp.float32)
    view = [1] * len(shape)
    view[-1] = shape[-1]
    return (values * ramp(shape[-1], start, stop).reshape(view)).astype(jnp.float32)


def draw_next_cotangent(key, part):
    key = jax.random.fold_in(key, 23)
    return cotangent_draw(key, (4, TOKENS, D)).astype(jnp.bfloat16)


def draw_grad_entry(key, part):
    key = jax.random.fold_in(key, 29)
    return cotangent_draw(key, (TOKENS, D)).astype(jnp.bfloat16)


def draw_norms_first(key, part):
    key = jax.random.fold_in(key, 31)
    return first_draw(key, (9, D), entry_level(1.0))


def draw_norms_second(key, part):
    key = jax.random.fold_in(key, 37)
    return second_draw(key, (9, D), entry_level(1.0))


def draw_attend_in_first(key, part):
    key = jax.random.fold_in(key, 41)
    return first_draw(key, (3, D, D), entry_level(1.0))


def draw_attend_in_second(key, part):
    key = jax.random.fold_in(key, 43)
    return second_draw(key, (3, D, D), entry_level(1.0))


def draw_attend_out_first(key, part):
    key = jax.random.fold_in(key, 47)
    return first_draw(key, (D, D), entry_level(1.0))


def draw_attend_out_second(key, part):
    key = jax.random.fold_in(key, 53)
    return second_draw(key, (D, D), entry_level(1.0))


def draw_expand_first(key, part):
    key = jax.random.fold_in(key, 59)
    return first_draw(key, (D, FF), entry_level(0.35))


def draw_expand_second(key, part):
    key = jax.random.fold_in(key, 61)
    return second_draw(key, (D, FF), entry_level(0.35))


def draw_project_first(key, part):
    key = jax.random.fold_in(key, 67)
    return first_draw(key, (FF, D), entry_level(1.0))


def draw_project_second(key, part):
    key = jax.random.fold_in(key, 71)
    return second_draw(key, (FF, D), entry_level(1.0))


def draw_mixer_in_first(key, part):
    key = jax.random.fold_in(key, 73)
    return first_draw(key, (D, MIXH), entry_level(1.0))


def draw_mixer_in_second(key, part):
    key = jax.random.fold_in(key, 79)
    return second_draw(key, (D, MIXH), entry_level(1.0))


def draw_mixer_out_first(key, part):
    key = jax.random.fold_in(key, 83)
    return first_draw(key, (4 * MIX, MIXH), entry_level(3.0))


def draw_mixer_out_second(key, part):
    key = jax.random.fold_in(key, 89)
    return second_draw(key, (4 * MIX, MIXH), entry_level(3.0))


def level_of(rng, dims, cuts, low, top_value):
    level, own = 1.0, jax.random.fold_in(rng, 6)
    for axis_at, shards_of in cuts:
        heights = jnp.exp(jax.random.uniform(jax.random.fold_in(own, axis_at), (shards_of,), jnp.float32, low / len(cuts), top_value / len(cuts)))
        level = level * jnp.repeat(heights, dims[axis_at] // shards_of).reshape([-1 if axis == axis_at else 1 for axis in range(len(dims))])
    return level


def scatter_about(own_key, extent, width, reach, cuts=(), kind=jnp.bfloat16):
    entries = jax.random.normal(own_key, extent, jnp.float32) * width
    if len(cuts) > 0:
        entries = level_of(own_key, extent, cuts, -0.22, 0.18) * entries
    return jnp.clip(entries, min=-reach, max=reach).astype(kind)


def setup_inputs(seed: int = 0) -> dict:
    seeds = jax.random.split(jax.random.key(seed), 27)
    return {
        "layer_inputs": scatter_about(seeds[0], (4, TOKENS, D), 1.0, 6.0, ((1, 4),)),
        "history": scatter_about(seeds[1], (STORED, TOKENS, D), 1.0, 6.0, ((2, 4),)),
        "seq_ids": draw_seq_ids(jax.random.fold_in(seeds[26], 71), 0),
        "norms_master": draw_norms_master(jax.random.fold_in(seeds[26], 71), 0),
        "norms_first": draw_norms_first(jax.random.fold_in(seeds[26], 71), 0),
        "norms_second": draw_norms_second(jax.random.fold_in(seeds[26], 71), 0),
        "attend_in_master": draw_attend_in_master(jax.random.fold_in(seeds[26], 71), 0),
        "attend_in_first": draw_attend_in_first(jax.random.fold_in(seeds[26], 71), 0),
        "attend_in_second": draw_attend_in_second(jax.random.fold_in(seeds[26], 71), 0),
        "attend_out_master": draw_attend_out_master(jax.random.fold_in(seeds[26], 71), 0),
        "attend_out_first": draw_attend_out_first(jax.random.fold_in(seeds[26], 71), 0),
        "attend_out_second": draw_attend_out_second(jax.random.fold_in(seeds[26], 71), 0),
        "expand_master": draw_expand_master(jax.random.fold_in(seeds[26], 71), 0),
        "expand_first": draw_expand_first(jax.random.fold_in(seeds[26], 71), 0),
        "expand_second": draw_expand_second(jax.random.fold_in(seeds[26], 71), 0),
        "project_master": draw_project_master(jax.random.fold_in(seeds[26], 71), 0),
        "project_first": draw_project_first(jax.random.fold_in(seeds[26], 71), 0),
        "project_second": draw_project_second(jax.random.fold_in(seeds[26], 71), 0),
        "mixer_in_master": scatter_about(seeds[18], (D, MIXH), D ** -0.5, 0.125, ((0, 4),), jnp.float32),
        "mixer_in_first": draw_mixer_in_first(jax.random.fold_in(seeds[26], 71), 0),
        "mixer_in_second": draw_mixer_in_second(jax.random.fold_in(seeds[26], 71), 0),
        "mixer_out_master": scatter_about(seeds[21], (4 * MIX, MIXH), MIXH ** -0.5, 1.0, ((0, 4),), jnp.float32),
        "mixer_out_first": draw_mixer_out_first(jax.random.fold_in(seeds[26], 71), 0),
        "mixer_out_second": draw_mixer_out_second(jax.random.fold_in(seeds[26], 71), 0),
        "next_cotangent": draw_next_cotangent(jax.random.fold_in(seeds[26], 71), 0),
        "grad_entry": draw_grad_entry(jax.random.fold_in(seeds[26], 71), 0),
    }


@jax.custom_vjp
def low(v):
    return lax.optimization_barrier(v.astype(jnp.bfloat16)).astype(jnp.float32)

@jax.custom_vjp
def low_back(v):
    return v

def low_keep(v):
    return (low(v), None)

def low_pass(kept, grad):
    return (grad,)

def back_keep(v):
    return (v, None)

def back_low(kept, grad):
    return (low(grad),)
low.defvjp(low_keep, low_pass)
low_back.defvjp(back_keep, back_low)
highest = lax.Precision.HIGHEST
norm_epsilon = 1e-05
mixer_epsilon = 1e-06
clip_level = 1.0
beta_first = 0.9
beta_second = 0.95
adam_epsilon = 1e-08
weight_decay = 0.1

def layer_norm(values, gain_rows, bias_rows):
    centred = values - lax.optimization_barrier(jnp.mean(values, axis=-1, keepdims=True))
    spread = lax.optimization_barrier(jnp.mean(centred * centred, axis=-1, keepdims=True))
    return centred * lax.rsqrt(spread + norm_epsilon) * gain_rows + bias_rows

def rotate(vectors, cosine, sine_table):
    half = ROT // 2
    first_half = vectors[..., :half]
    second_half = vectors[..., half:ROT]
    return jnp.concatenate([first_half * cosine - second_half * sine_table, second_half * cosine + first_half * sine_table, vectors[..., ROT:]], axis=-1)

def angles(bucket_ids):
    same_seq = bucket_ids[:, None] == bucket_ids[None, :]
    order = jnp.arange(bucket_ids.shape[0])
    earlier = order[None, :] < order[:, None]
    position = lax.optimization_barrier(jnp.sum(jnp.where(same_seq & earlier, 1, 0), axis=1)).astype(jnp.float32)
    freqs = 10000.0 ** (-2.0 * jnp.arange(ROT // 2).astype(jnp.float32) / ROT)
    angle = position[:, None] * freqs[None, :]
    allowed = same_seq & (order[None, :] <= order[:, None])
    return (jnp.cos(angle), jnp.sin(angle), allowed)

def attend_block(bucket_data):
    query_raw, key_raw, value_low, bucket_ids = bucket_data
    cosine, sine_table, allowed = angles(bucket_ids)
    query = low(rotate(jnp.swapaxes(query_raw, 0, 1), cosine, sine_table))
    key_rows = low(rotate(jnp.swapaxes(key_raw, 0, 1), cosine, sine_table))
    value_rows = jnp.swapaxes(value_low, 0, 1)
    head_scale = HDIM ** (-0.5)
    scores = jnp.einsum('hqd,hkd->hqk', query, key_rows, precision=highest) * head_scale
    scores = low_back(jnp.where(allowed[None], scores, -1e+30))
    row_max = lax.optimization_barrier(jnp.max(scores, axis=-1, keepdims=True))
    log_total = jnp.log(lax.optimization_barrier(jnp.sum(jnp.exp(scores - row_max), axis=-1, keepdims=True))) + row_max
    prob_low = low(jnp.exp(scores - log_total))
    mixed = jnp.einsum('hqk,hkd->qhd', prob_low, value_rows, precision=highest)
    return mixed.reshape(TOK_DEV, HEADS * HDIM)

def adam_step(master, first_moment, second_moment, gradient, factor, step_rate, decay_rate):
    scaled = gradient * factor
    first_new = beta_first * first_moment + (1.0 - beta_first) * scaled
    second_new = beta_second * second_moment + (1.0 - beta_second) * scaled * scaled
    first_hat = first_new / (1.0 - beta_first ** STEP)
    second_hat = second_new / (1.0 - beta_second ** STEP)
    master_new = master - step_rate * (first_hat / (jnp.sqrt(second_hat) + adam_epsilon) + decay_rate * master)
    return (master_new, first_new, second_new)

def reference(layer_inputs, history, seq_ids, norms_master, norms_first, norms_second, attend_in_master, attend_in_first, attend_in_second, attend_out_master, attend_out_first, attend_out_second, expand_master, expand_first, expand_second, project_master, project_first, project_second, mixer_in_master, mixer_in_first, mixer_in_second, mixer_out_master, mixer_out_first, mixer_out_second, next_cotangent, grad_entry):
    bucket_ids = seq_ids.reshape(BUCKETS, TOK_DEV)
    valid = (seq_ids >= 0).astype(jnp.float32)[:, None]

    def forward(input_vals, history_vals, norms_vals, attend_in_vals, attend_out_vals, expand_vals, project_vals, mixer_in_vals, mixer_out_vals):
        norm_copy = low(norms_vals)
        normed = low(layer_norm(input_vals, norm_copy[0:4][:, None, :], norm_copy[4:8][:, None, :]))
        proj = jnp.einsum('ctd,cde->cte', normed[0:3], low(attend_in_vals), precision=highest)
        query_raw = low_back(proj[0])
        key_raw = low_back(proj[1])
        value_low = low_back(low(proj[2]))
        head_shape = (BUCKETS, TOK_DEV, HEADS, HDIM)
        heads_all = lax.map(jax.checkpoint(attend_block), (query_raw.reshape(head_shape), key_raw.reshape(head_shape), value_low.reshape(head_shape), bucket_ids))
        heads_out = low_back(low(heads_all.reshape(TOKENS, D)))
        upper = low_back(jnp.dot(normed[3], low(expand_vals), precision=highest))
        hidden = low(jax.nn.gelu(upper, approximate=False))
        branch = low_back(jnp.dot(heads_out, low(attend_out_vals), precision=highest) + jnp.dot(hidden, low(project_vals), precision=highest))
        newest = input_vals[3] + valid * branch
        mix_scale = lax.rsqrt(lax.optimization_barrier(jnp.mean(newest * newest, axis=-1, keepdims=True)) + mixer_epsilon)
        mix_normed = low(newest * mix_scale * norm_copy[8])
        mix_pre = low_back(jnp.dot(mix_normed, low(mixer_in_vals), precision=highest))
        mix_act = low(jax.nn.gelu(mix_pre, approximate=False))
        mix_weights = low_back(jnp.dot(mix_act, low(mixer_out_vals).T, precision=highest)).reshape(TOKENS, 4, MIX)
        layers = [history_vals[layer_index] for layer_index in range(STORED)] + [newest]
        next_vals = mix_weights[:, :, 0].T[:, :, None] * layers[0][None]
        for layer_index in range(1, MIX):
            next_vals = next_vals + mix_weights[:, :, layer_index].T[:, :, None] * layers[layer_index][None]
        return (next_vals, newest)
    outputs, pullback = jax.vjp(forward, layer_inputs.astype(jnp.float32), history.astype(jnp.float32), norms_master, attend_in_master, attend_out_master, expand_master, project_master, mixer_in_master, mixer_out_master)
    next_vals, newest = outputs
    gradients = pullback((next_cotangent.astype(jnp.float32), grad_entry.astype(jnp.float32)))
    grad_in, grad_hist = (gradients[0], gradients[1])
    weight_grads = gradients[2:]
    total = sum((jnp.sum(gradient * gradient) for gradient in weight_grads))
    grad_norm = jnp.sqrt(total)
    factor = jnp.minimum(1.0, clip_level / grad_norm)
    wide_rate = 2.0 / math.sqrt(D)
    norms_out = adam_step(norms_master, norms_first, norms_second, weight_grads[0], factor, 1.0, 0.0)
    attend_in_out = adam_step(attend_in_master, attend_in_first, attend_in_second, weight_grads[1], factor, wide_rate, weight_decay)
    attend_out_out = adam_step(attend_out_master, attend_out_first, attend_out_second, weight_grads[2], factor, wide_rate, weight_decay)
    expand_out = adam_step(expand_master, expand_first, expand_second, weight_grads[3], factor, wide_rate, weight_decay)
    project_out = adam_step(project_master, project_first, project_second, weight_grads[4], factor, 2.0 / math.sqrt(FF), weight_decay)
    mixer_in_out = adam_step(mixer_in_master, mixer_in_first, mixer_in_second, weight_grads[5], factor, wide_rate, weight_decay)
    mixer_out_out = adam_step(mixer_out_master, mixer_out_first, mixer_out_second, weight_grads[6], factor, 2.0 / math.sqrt(MIXH), weight_decay)
    return (next_vals.astype(jnp.bfloat16), newest.astype(jnp.bfloat16), grad_in.astype(jnp.bfloat16), grad_hist.astype(jnp.bfloat16), norms_out[0], norms_out[1], norms_out[2], attend_in_out[0], attend_in_out[1], attend_in_out[2], attend_in_out[0].astype(jnp.bfloat16), attend_out_out[0], attend_out_out[1], attend_out_out[2], attend_out_out[0].astype(jnp.bfloat16), expand_out[0], expand_out[1], expand_out[2], expand_out[0].astype(jnp.bfloat16), project_out[0], project_out[1], project_out[2], project_out[0].astype(jnp.bfloat16), mixer_in_out[0], mixer_in_out[1], mixer_in_out[2], mixer_in_out[0].astype(jnp.bfloat16), mixer_out_out[0], mixer_out_out[1], mixer_out_out[2], mixer_out_out[0].astype(jnp.bfloat16), grad_norm)
```

```python
import math

import jax
import jax.numpy as jnp
from jax import lax
from jax.sharding import PartitionSpec as P

D = 2048
HDIM = 128
FF = 8192
MIXH = 36
ROT = 32
STEP = 10


norm_epsilon = 1e-05
mixer_epsilon = 1e-06
clip_level = 1.0
beta_first = 0.9
beta_second = 0.95
adam_epsilon = 1e-08
weight_decay = 0.1


def exact_gelu(values):
    return jax.nn.gelu(values, approximate=False)


def gelu_grad(values, upstream):
    unused, pullback = jax.vjp(exact_gelu, values)
    return pullback(upstream)[0]


def rotate(vectors, cosine, sine_table):
    half = ROT // 2
    first_half = vectors[..., :half]
    second_half = vectors[..., half:ROT]
    return jnp.concatenate(
        [
            first_half * cosine - second_half * sine_table,
            second_half * cosine + first_half * sine_table,
            vectors[..., ROT:],
        ],
        axis=-1,
    )


def angles(bucket_ids):
    same_seq = bucket_ids[:, None] == bucket_ids[None, :]
    order = jnp.arange(bucket_ids.shape[0])
    earlier = order[None, :] < order[:, None]
    position = jnp.sum(jnp.where(same_seq & earlier, 1, 0), axis=1).astype(jnp.float32)
    freqs = 10000.0 ** (-2.0 * jnp.arange(ROT // 2).astype(jnp.float32) / ROT)
    angle = position[:, None] * freqs[None, :]
    allowed = same_seq & (order[None, :] <= order[:, None])
    return (jnp.cos(angle), jnp.sin(angle), allowed)


def score_block(query, key_rows, allowed):
    head_scale = HDIM ** (-0.5)
    scores = (
        jnp.einsum("hqd,hkd->hqk", query, key_rows, preferred_element_type=jnp.float32) * head_scale
    )
    return jnp.where(allowed[None], scores, -1e30)


def norm_back(grad_rows, unit_rows, inverse_rows, gain_rows):
    scaled = grad_rows * gain_rows
    mean_scaled = jnp.mean(scaled, axis=-1, keepdims=True)
    mean_cross = jnp.mean(scaled * unit_rows, axis=-1, keepdims=True)
    return inverse_rows * (scaled - mean_scaled - unit_rows * mean_cross)


def contract_rows(left, right):
    return lax.dot_general(
        left, right, (((0,), (0,)), ((), ())), preferred_element_type=jnp.float32
    )


def contract_cols(left, right):
    return lax.dot_general(
        left, right, (((1,), (1,)), ((), ())), preferred_element_type=jnp.float32
    )


def adam_step(master, first_moment, second_moment, gradient, factor, step_rate, decay_rate):
    scaled = gradient * factor
    first_new = beta_first * first_moment + (1.0 - beta_first) * scaled
    second_new = beta_second * second_moment + (1.0 - beta_second) * scaled * scaled
    first_hat = first_new / (1.0 - beta_first**STEP)
    second_hat = second_new / (1.0 - beta_second**STEP)
    master_new = master - step_rate * (
        first_hat / (jnp.sqrt(second_hat) + adam_epsilon) + decay_rate * master
    )
    return (master_new, first_new, second_new)


def bits_of(size):
    return [1 << index for index in range(size.bit_length() - 1)]


def swap(values, axis, mask):
    size = lax.axis_size(axis)
    return lax.ppermute(values, axis, [(source, source ^ mask) for source in range(size)])


def gather_pieces(piece, axis):
    size = lax.axis_size(axis)
    pieces = {0: piece}
    for bit in reversed(bits_of(size)):
        for known in list(pieces):
            pieces[known | bit] = swap(pieces[known], axis, bit)
    return [pieces[index] for index in range(size)]


def exchange_pieces(pieces, axis):
    return [pieces[0]] + [swap(pieces[mask], axis, mask) for mask in range(1, len(pieces))]


def reduce_pieces(pieces, axis, send_type):
    kept = dict(enumerate(pieces))
    for bit in bits_of(len(pieces)):
        for index in sorted(kept, reverse=True):
            if index & bit:
                moved = swap(kept.pop(index).astype(send_type), axis, bit)
                kept[index ^ bit] = kept[index ^ bit].astype(jnp.float32) + moved.astype(jnp.float32)
    return kept[0]


def butterfly(values, axis):
    for bit in bits_of(lax.axis_size(axis)):
        values = values + swap(values, axis, bit)
    return values


def share_index(axis):
    size = lax.axis_size(axis)
    here = lax.axis_index(axis)
    place = 0
    for bit in bits_of(size):
        place = place * 2 + (here & bit) // bit
    return place


def scatter_rows(values, axis, row_axis):
    here = lax.axis_index(axis)
    low_type = values.dtype
    for bit in bits_of(lax.axis_size(axis)):
        half = values.shape[row_axis] // 2
        side = (here & bit) // bit
        kept = lax.dynamic_slice_in_dim(values, side * half, half, row_axis)
        given = lax.dynamic_slice_in_dim(values, (1 - side) * half, half, row_axis)
        moved = swap(given.astype(low_type), axis, bit)
        values = kept.astype(jnp.float32) + moved.astype(jnp.float32)
        if bit * 2 < lax.axis_size(axis):
            values = values.astype(low_type)
    return values


def gather_rows(values, axis, row_axis):
    here = lax.axis_index(axis)
    for bit in reversed(bits_of(lax.axis_size(axis))):
        side = (here & bit) // bit
        moved = swap(values, axis, bit)
        half = values.shape[row_axis]
        shape = list(values.shape)
        shape[row_axis] = half * 2
        joined = lax.dynamic_update_slice_in_dim(
            jnp.zeros(shape, values.dtype), values, side * half, row_axis
        )
        values = lax.dynamic_update_slice_in_dim(joined, moved, (1 - side) * half, row_axis)
    return values


def body(
    layer_inputs,
    history,
    seq_ids,
    norms_master,
    norms_first,
    norms_second,
    attend_in_master,
    attend_in_first,
    attend_in_second,
    attend_out_master,
    attend_out_first,
    attend_out_second,
    expand_master,
    expand_first,
    expand_second,
    project_master,
    project_first,
    project_second,
    mixer_in_master,
    mixer_in_first,
    mixer_in_second,
    mixer_out_master,
    mixer_out_first,
    mixer_out_second,
    next_cotangent,
    grad_entry,
):
    bf16_type = jnp.bfloat16
    float_type = jnp.float32
    tensor_size = lax.axis_size("tensor")
    owners = lax.axis_size("dp")
    me = lax.axis_index("dp")
    tokens_here = layer_inputs.shape[1]
    share_rows = tokens_here // tensor_size
    share_start = share_index("tensor") * share_rows
    cols = norms_master.shape[1]
    mixers = mixer_out_master.shape[0]

    def own_rows(values, axis):
        return lax.dynamic_slice_in_dim(values, share_start, share_rows, axis)

    def block_of(values, index):
        return lax.dynamic_slice_in_dim(values, (me ^ index) * cols, cols, values.ndim - 1)

    def reorder(pieces):
        stacked = jnp.stack(pieces)
        return jnp.concatenate(
            [lax.dynamic_index_in_dim(stacked, me ^ index, 0, False) for index in range(owners)],
            axis=-1,
        )

    def split(values):
        return [values[..., index * cols : (index + 1) * cols] for index in range(owners)]

    small = jnp.concatenate(
        [
            norms_master,
            mixer_in_master.T,
            jnp.pad(mixer_out_master, ((0, 0), (0, cols - MIXH))),
        ],
        axis=0,
    ).astype(bf16_type)
    small_pieces = gather_pieces(small, "dp")
    attend_in_pieces = gather_pieces(attend_in_master.astype(bf16_type), "dp")
    expand_pieces = gather_pieces(expand_master.astype(bf16_type), "dp")
    project_pieces = gather_pieces(project_master.astype(bf16_type), "dp")
    attend_out_pieces = gather_pieces(attend_out_master.astype(bf16_type), "dp")

    stacked_entry = jnp.concatenate([history, grad_entry[None]], axis=0)
    early_rows = [
        lax.dynamic_slice_in_dim(
            stacked_entry, (me ^ index) * tokens_here + share_start, share_rows, 1
        )
        for index in range(owners)
    ]
    early = reorder(exchange_pieces(early_rows, "dp"))
    stored_share = early[:-1]
    entry_back = early[-1].astype(float_type)
    stored = gather_rows(stored_share, "tensor", 1)

    norm_pieces = [piece[0:9].astype(float_type) for piece in small_pieces]
    small_whole = reorder([piece[0 : 9 + MIXH] for piece in small_pieces])
    norm_vals = small_whole[0:9].astype(float_type)
    mixer_in_low = small_whole[9:]
    mixer_out_stack = jnp.stack([piece[9 + MIXH :, 0:MIXH] for piece in small_pieces])
    mixer_out_low = jnp.concatenate(
        [lax.dynamic_index_in_dim(mixer_out_stack, me ^ index, 0, False) for index in range(owners)]
    )

    input_vals = layer_inputs.astype(float_type)
    mean_vals = jnp.mean(input_vals, axis=-1, keepdims=True)
    centred = input_vals - mean_vals
    inverse = lax.rsqrt(jnp.mean(centred * centred, axis=-1, keepdims=True) + norm_epsilon)
    normed_pieces = [
        (
            (block_of(layer_inputs, index).astype(float_type) - mean_vals)
            * inverse
            * norm_pieces[index][0:4][:, None, :]
            + norm_pieces[index][4:8][:, None, :]
        ).astype(bf16_type)
        for index in range(owners)
    ]
    proj = sum(
        jnp.einsum(
            "ctd,cde->cte", normed[0:3], weights, preferred_element_type=float_type
        )
        for normed, weights in zip(normed_pieces, attend_in_pieces)
    )
    local_heads = proj.shape[2] // HDIM
    split_heads = jnp.transpose(proj.reshape(3, tokens_here, local_heads, HDIM), (0, 2, 1, 3))
    cosine, sine_table, allowed = angles(seq_ids)
    query = rotate(split_heads[0], cosine, sine_table).astype(bf16_type)
    key_rows = rotate(split_heads[1], cosine, sine_table).astype(bf16_type)
    value_rows = split_heads[2].astype(bf16_type)
    scores = score_block(query, key_rows, allowed)
    row_max = jnp.max(scores, axis=-1, keepdims=True)
    log_total = jnp.log(jnp.sum(jnp.exp(scores - row_max), axis=-1, keepdims=True)) + row_max
    prob_low = jnp.exp(scores - log_total).astype(bf16_type)
    heads_mixed = jnp.einsum(
        "hqk,hkd->qhd", prob_low, value_rows, preferred_element_type=float_type
    )
    heads_out = heads_mixed.reshape(tokens_here, local_heads * HDIM).astype(bf16_type)
    upper = sum(
        jnp.dot(normed[3], weights, preferred_element_type=float_type)
        for normed, weights in zip(normed_pieces, expand_pieces)
    )
    hidden = exact_gelu(upper).astype(bf16_type)
    partial_branch = jnp.concatenate(
        [
            (
                jnp.dot(heads_out, out_weights, preferred_element_type=float_type)
                + jnp.dot(hidden, weights, preferred_element_type=float_type)
            ).astype(bf16_type)
            for out_weights, weights in zip(attend_out_pieces, project_pieces)
        ],
        axis=-1,
    )
    branch = reorder(split(scatter_rows(partial_branch, "tensor", 0)))

    valid = (own_rows(seq_ids, 0) >= 0).astype(float_type)[:, None]
    input_share = own_rows(layer_inputs, 1).astype(float_type)
    newest = input_share[3] + valid * branch
    mix_scale = lax.rsqrt(jnp.mean(newest * newest, axis=-1, keepdims=True) + mixer_epsilon)
    mix_normed = (newest * mix_scale * norm_vals[8]).astype(bf16_type)
    mix_pre = contract_cols(mix_normed, mixer_in_low)
    mix_act = exact_gelu(mix_pre).astype(bf16_type)
    layer_count = stored.shape[0] + 1
    mix_share = contract_cols(mix_act, mixer_out_low)
    mix_weights = mix_share.reshape(share_rows, 4, layer_count)
    layers = [stored_share[index].astype(float_type) for index in range(layer_count - 1)] + [newest]
    grad_out = own_rows(next_cotangent, 1).astype(float_type)
    weight_terms = jnp.stack(
        [jnp.sum(grad_out * layer_vals[None], axis=-1) for layer_vals in layers], axis=-1
    )
    grad_weights = (
        jnp.transpose(weight_terms, (1, 0, 2))
        .reshape(share_rows, 4 * layer_count)
        .astype(bf16_type)
    )
    newest_back = jnp.sum(mix_weights[:, :, layer_count - 1].T[:, :, None] * grad_out, axis=0)
    grad_mixer_out = contract_rows(grad_weights, mix_act)
    grad_mix_act = jnp.dot(grad_weights, mixer_out_low, preferred_element_type=float_type)
    grad_mix_pre = gelu_grad(mix_pre, grad_mix_act).astype(bf16_type)
    grad_mixer_in = contract_rows(grad_mix_pre, mix_normed)
    grad_mix_normed = jnp.dot(grad_mix_pre, mixer_in_low, preferred_element_type=float_type)
    scaled_mix = grad_mix_normed * norm_vals[8]
    grad_newest = (
        newest_back
        + entry_back
        + mix_scale * scaled_mix
        - newest * mix_scale**3 * jnp.mean(scaled_mix * newest, axis=-1, keepdims=True)
    )
    mixer_gain = jnp.sum(grad_mix_normed * newest * mix_scale, axis=0)
    branch_share = (valid * grad_newest).astype(bf16_type)
    grad_branch = split(
        gather_rows(
            jnp.concatenate([block_of(branch_share, index) for index in range(owners)], axis=-1),
            "tensor",
            0,
        )
    )

    newest_low = gather_rows(newest.astype(bf16_type), "tensor", 0)
    mix_whole = gather_rows(mix_share, "tensor", 0).reshape(tokens_here, 4, layer_count)
    layers_low = [stored[index] for index in range(layer_count - 1)] + [newest_low]
    next_inputs = sum(
        mix_whole[:, :, index].T[:, :, None] * layers_low[index].astype(float_type)[None]
        for index in range(layer_count)
    ).astype(bf16_type)
    entry_pieces = exchange_pieces(
        [block_of(newest_low, index) for index in range(owners)], "dp"
    )
    history_pieces = exchange_pieces(
        [
            jnp.stack(
                [
                    jnp.sum(
                        mix_whole[:, :, layer].T[:, :, None]
                        * block_of(next_cotangent, index).astype(float_type),
                        axis=0,
                    )
                    for layer in range(layer_count - 1)
                ]
            ).astype(bf16_type)
            for index in range(owners)
        ],
        "dp",
    )
    new_entry = jnp.zeros(grad_entry.shape, bf16_type)
    grad_history = jnp.zeros(history.shape, bf16_type)
    for index in range(owners):
        first_row = (me ^ index) * tokens_here
        new_entry = lax.dynamic_update_slice_in_dim(new_entry, entry_pieces[index], first_row, 0)
        grad_history = lax.dynamic_update_slice_in_dim(
            grad_history, history_pieces[index], first_row, 1
        )

    grad_heads = sum(
        contract_cols(grads, weights) for grads, weights in zip(grad_branch, attend_out_pieces)
    ).astype(bf16_type)
    grad_hidden = sum(
        contract_cols(grads, weights) for grads, weights in zip(grad_branch, project_pieces)
    )
    grad_upper = gelu_grad(upper, grad_hidden).astype(bf16_type)
    grad_project = reduce_pieces(
        [contract_rows(hidden, grads) for grads in grad_branch], "dp", bf16_type
    )
    grad_attend_out = reduce_pieces(
        [contract_rows(heads_out, grads) for grads in grad_branch], "dp", bf16_type
    )
    grad_expand = reduce_pieces(
        [contract_rows(normed[3], grad_upper) for normed in normed_pieces], "dp", bf16_type
    )
    summed_ffn = scatter_rows(
        jnp.concatenate(
            [contract_cols(grad_upper, weights).astype(bf16_type) for weights in expand_pieces],
            axis=-1,
        ),
        "tensor",
        0,
    )
    head_scale = HDIM ** (-0.5)
    grad_heads_split = jnp.transpose(grad_heads.reshape(tokens_here, local_heads, HDIM), (1, 0, 2))
    prob = jnp.exp(score_block(query, key_rows, allowed) - log_total)
    grad_prob = jnp.einsum(
        "hqd,hkd->hqk", grad_heads_split, value_rows, preferred_element_type=float_type
    )
    row_delta = jnp.sum(prob * grad_prob, axis=-1, keepdims=True)
    grad_scores = (prob * (grad_prob - row_delta)).astype(bf16_type)
    grad_query = (
        jnp.einsum("hqk,hkd->hqd", grad_scores, key_rows, preferred_element_type=float_type)
        * head_scale
    )
    grad_key = (
        jnp.einsum("hqk,hqd->hkd", grad_scores, query, preferred_element_type=float_type)
        * head_scale
    )
    grad_value = jnp.einsum(
        "hqk,hqd->hkd", prob_low, grad_heads_split, preferred_element_type=float_type
    )
    grad_proj = [
        jnp.transpose(grads, (1, 0, 2)).reshape(tokens_here, local_heads * HDIM).astype(bf16_type)
        for grads in (
            rotate(grad_query, cosine, -sine_table),
            rotate(grad_key, cosine, -sine_table),
            grad_value,
        )
    ]
    grad_attend_in = [
        reduce_pieces(
            [contract_rows(normed[index], grad_proj[index]) for normed in normed_pieces],
            "dp",
            bf16_type,
        )
        for index in range(3)
    ]
    summed = [
        scatter_rows(
            jnp.concatenate(
                [
                    contract_cols(grad_proj[index], weights[index]).astype(bf16_type)
                    for weights in attend_in_pieces
                ],
                axis=-1,
            ),
            "tensor",
            0,
        )
        for index in range(3)
    ] + [summed_ffn]
    unit_share = (input_share - own_rows(mean_vals, 1)) * own_rows(inverse, 1)
    inverse_share = own_rows(inverse, 1)
    gain_parts = []
    bias_parts = []
    grad_inputs = []
    for index in range(4):
        grad_rows = reorder(split(summed[index]))
        gain_parts.append(jnp.sum(grad_rows * unit_share[index], axis=0))
        bias_parts.append(jnp.sum(grad_rows, axis=0))
        back = norm_back(grad_rows, unit_share[index], inverse_share[index], norm_vals[index][None])
        if index == 3:
            back = back + grad_newest
        grad_inputs.append(gather_rows(back.astype(bf16_type), "tensor", 0))
    grad_inputs = jnp.stack(grad_inputs)

    early_pack = jnp.concatenate(
        [
            grad_mixer_in,
            jnp.pad(
                grad_mixer_out.reshape(owners, mixers * MIXH), ((0, 0), (0, cols - mixers * MIXH))
            ).reshape(1, owners * cols),
            mixer_gain[None],
        ],
        axis=0,
    )
    late_pack = jnp.stack(gain_parts + bias_parts)
    early_sum = butterfly(
        reduce_pieces([block_of(early_pack, index) for index in range(owners)], "dp", float_type),
        "tensor",
    )
    late_sum = butterfly(
        reduce_pieces([block_of(late_pack, index) for index in range(owners)], "dp", float_type),
        "tensor",
    )
    norm_grad = jnp.concatenate([late_sum, early_sum[MIXH + 1 :]], axis=0)
    grad_mixer_in = early_sum[0:MIXH].T
    grad_mixer_out = early_sum[MIXH, 0 : mixers * MIXH].reshape(mixers, MIXH)
    shard_squares = sum(
        (
            jnp.sum(gradient * gradient)
            for gradient in grad_attend_in + [grad_attend_out, grad_expand, grad_project]
        )
    )
    shared_squares = (
        jnp.sum(norm_grad * norm_grad)
        + jnp.sum(grad_mixer_in * grad_mixer_in)
        + jnp.sum(grad_mixer_out * grad_mixer_out)
    )
    total_squares = butterfly(
        butterfly((shard_squares + shared_squares / tensor_size).reshape(1, 1), "dp"), "tensor"
    )[0, 0]
    reduced = (
        jnp.stack(grad_attend_in),
        grad_attend_out,
        grad_expand,
        grad_project,
        grad_mixer_in,
        grad_mixer_out,
    )
    grad_norm = jnp.sqrt(total_squares)
    factor = jnp.minimum(1.0, clip_level / grad_norm)
    wide_rate = 2.0 / math.sqrt(D)
    norms_out = adam_step(norms_master, norms_first, norms_second, norm_grad, factor, 1.0, 0.0)
    attend_in_out = adam_step(
        attend_in_master,
        attend_in_first,
        attend_in_second,
        reduced[0],
        factor,
        wide_rate,
        weight_decay,
    )
    attend_out_out = adam_step(
        attend_out_master,
        attend_out_first,
        attend_out_second,
        reduced[1],
        factor,
        wide_rate,
        weight_decay,
    )
    expand_out = adam_step(
        expand_master, expand_first, expand_second, reduced[2], factor, wide_rate, weight_decay
    )
    project_out = adam_step(
        project_master,
        project_first,
        project_second,
        reduced[3],
        factor,
        2.0 / math.sqrt(FF),
        weight_decay,
    )
    mixer_in_out = adam_step(
        mixer_in_master,
        mixer_in_first,
        mixer_in_second,
        reduced[4],
        factor,
        wide_rate,
        weight_decay,
    )
    mixer_out_out = adam_step(
        mixer_out_master,
        mixer_out_first,
        mixer_out_second,
        reduced[5],
        factor,
        2.0 / math.sqrt(MIXH),
        weight_decay,
    )
    return (
        next_inputs,
        new_entry,
        grad_inputs,
        grad_history,
        norms_out[0],
        norms_out[1],
        norms_out[2],
        attend_in_out[0],
        attend_in_out[1],
        attend_in_out[2],
        attend_in_out[0].astype(bf16_type),
        attend_out_out[0],
        attend_out_out[1],
        attend_out_out[2],
        attend_out_out[0].astype(bf16_type),
        expand_out[0],
        expand_out[1],
        expand_out[2],
        expand_out[0].astype(bf16_type),
        project_out[0],
        project_out[1],
        project_out[2],
        project_out[0].astype(bf16_type),
        mixer_in_out[0],
        mixer_in_out[1],
        mixer_in_out[2],
        mixer_in_out[0].astype(bf16_type),
        mixer_out_out[0],
        mixer_out_out[1],
        mixer_out_out[2],
        mixer_out_out[0].astype(bf16_type),
        grad_norm,
    )


def solution(mesh):
    in_specs = (
        P(None, "dp", None),
        P(None, None, "dp"),
        P("dp"),
        P(None, "dp"),
        P(None, "dp"),
        P(None, "dp"),
        P(None, "dp", "tensor"),
        P(None, "dp", "tensor"),
        P(None, "dp", "tensor"),
        P("tensor", "dp"),
        P("tensor", "dp"),
        P("tensor", "dp"),
        P("dp", "tensor"),
        P("dp", "tensor"),
        P("dp", "tensor"),
        P("tensor", "dp"),
        P("tensor", "dp"),
        P("tensor", "dp"),
        P("dp", None),
        P("dp", None),
        P("dp", None),
        P("dp", None),
        P("dp", None),
        P("dp", None),
        P(None, "dp", None),
        P(None, "dp"),
    )
    out_specs = (
        P(None, "dp", None),
        P(None, "dp"),
        P(None, "dp", None),
        P(None, None, "dp"),
        P(None, "dp"),
        P(None, "dp"),
        P(None, "dp"),
        P(None, "dp", "tensor"),
        P(None, "dp", "tensor"),
        P(None, "dp", "tensor"),
        P(None, "dp", "tensor"),
        P("tensor", "dp"),
        P("tensor", "dp"),
        P("tensor", "dp"),
        P("tensor", "dp"),
        P("dp", "tensor"),
        P("dp", "tensor"),
        P("dp", "tensor"),
        P("dp", "tensor"),
        P("tensor", "dp"),
        P("tensor", "dp"),
        P("tensor", "dp"),
        P("tensor", "dp"),
        P("dp", None),
        P("dp", None),
        P("dp", None),
        P("dp", None),
        P("dp", None),
        P("dp", None),
        P("dp", None),
        P("dp", None),
        P(),
    )
    return jax.shard_map(body, mesh=mesh, in_specs=in_specs, out_specs=out_specs, check_vma=False)
```

```python
import functools
import math

import jax
import jax.numpy as jnp
from jax import lax
from jax.experimental import pallas as pl
from jax.experimental.pallas import tpu as pltpu
from jax.sharding import PartitionSpec as P

D = 2048
HDIM = 128
FF = 8192
MIXH = 36
ROT = 32
STEP = 10


norm_epsilon = 1e-05
mixer_epsilon = 1e-06
clip_level = 1.0
beta_first = 0.9
beta_second = 0.95
adam_epsilon = 1e-08
weight_decay = 0.1


def exact_gelu(values):
    return jax.nn.gelu(values, approximate=False)


def gelu_grad(values, upstream):
    unused, pullback = jax.vjp(exact_gelu, values)
    return pullback(upstream)[0]


def rotate(vectors, cosine, sine_table):
    half = ROT // 2
    first_half = vectors[..., :half]
    second_half = vectors[..., half:ROT]
    return jnp.concatenate(
        [
            first_half * cosine - second_half * sine_table,
            second_half * cosine + first_half * sine_table,
            vectors[..., ROT:],
        ],
        axis=-1,
    )


def angles(bucket_ids):
    same_seq = bucket_ids[:, None] == bucket_ids[None, :]
    order = jnp.arange(bucket_ids.shape[0])
    earlier = order[None, :] < order[:, None]
    position = jnp.sum(jnp.where(same_seq & earlier, 1, 0), axis=1).astype(jnp.float32)
    freqs = 10000.0 ** (-2.0 * jnp.arange(ROT // 2).astype(jnp.float32) / ROT)
    angle = position[:, None] * freqs[None, :]
    allowed = same_seq & (order[None, :] <= order[:, None])
    return (jnp.cos(angle), jnp.sin(angle), allowed)


def score_block(query, key_rows, allowed):
    head_scale = HDIM ** (-0.5)
    scores = (
        jnp.einsum("hqd,hkd->hqk", query, key_rows, preferred_element_type=jnp.float32) * head_scale
    )
    return jnp.where(allowed[None], scores, -1e30)


def norm_back(grad_rows, unit_rows, inverse_rows, gain_rows):
    scaled = grad_rows * gain_rows
    mean_scaled = jnp.mean(scaled, axis=-1, keepdims=True)
    mean_cross = jnp.mean(scaled * unit_rows, axis=-1, keepdims=True)
    return inverse_rows * (scaled - mean_scaled - unit_rows * mean_cross)


def contract_rows(left, right):
    return lax.dot_general(
        left, right, (((0,), (0,)), ((), ())), preferred_element_type=jnp.float32
    )


def contract_cols(left, right):
    return lax.dot_general(
        left, right, (((1,), (1,)), ((), ())), preferred_element_type=jnp.float32
    )


def adam_step(master, first_moment, second_moment, gradient, factor, step_rate, decay_rate):
    scaled = gradient * factor
    first_new = beta_first * first_moment + (1.0 - beta_first) * scaled
    second_new = beta_second * second_moment + (1.0 - beta_second) * scaled * scaled
    first_hat = first_new / (1.0 - beta_first**STEP)
    second_hat = second_new / (1.0 - beta_second**STEP)
    master_new = master - step_rate * (
        first_hat / (jnp.sqrt(second_hat) + adam_epsilon) + decay_rate * master
    )
    return (master_new, first_new, second_new)


def gelu_parts(values):
    upper_share = 0.5 * (1.0 + lax.erf(values * math.sqrt(0.5)))
    density = jnp.exp(-0.5 * values * values) * (1.0 / math.sqrt(2.0 * math.pi))
    return upper_share, density


def bits_of(size):
    return [1 << index for index in range(size.bit_length() - 1)]


def feature_order(owners):
    order = [0]
    for bit in reversed(bits_of(owners)):
        order = order + [index | bit for index in order]
    return order


def swap(values, axis, mask):
    size = lax.axis_size(axis)
    return lax.ppermute(values, axis, [(source, source ^ mask) for source in range(size)])


def sync(plain, steps):
    held = [vars(item) for item in steps]
    names = [
        [name for name in ("values", "terms", "given") if item.get(name) is not None]
        for item in held
    ]
    plain, inner = lax.optimization_barrier(
        (
            list(plain),
            [[item[name] for name in kinds] for item, kinds in zip(held, names)],
        )
    )
    for item, kinds, values in zip(steps, names, inner):
        for name, value in zip(kinds, values):
            setattr(item, name, value)
    return plain


def gather_half(piece, axis, dim):
    for bit in reversed(bits_of(lax.axis_size(axis))[1:]):
        piece = jnp.concatenate([piece, swap(piece, axis, bit)], axis=dim)
    return piece


def halve(values, dim):
    half = values.shape[dim] // 2
    return (
        lax.slice_in_dim(values, 0, half, axis=dim),
        lax.slice_in_dim(values, half, 2 * half, axis=dim),
    )


class Reduce:
    def __init__(self, kept, given, axis, dim):
        self.terms, self.given, self.axis, self.dim = [kept], given, axis, dim

    def near(self):
        self.terms.append(swap(self.given, self.axis, 1))
        self.given = None

    def prepare(self):
        half = self.terms[-1].shape[self.dim] // 2
        self.given = sum(
            lax.slice_in_dim(term, half, 2 * half, axis=self.dim).astype(jnp.float32)
            for term in self.terms
        ).astype(jnp.bfloat16)

    def far(self):
        for bit in bits_of(lax.axis_size(self.axis))[1:]:
            if self.given is None:
                self.prepare()
            self.terms.append(swap(self.given, self.axis, bit))
            self.given = None

    def squares(self):
        own = self.terms[-1].shape[self.dim]
        return square_sum(
            sum(
                lax.slice_in_dim(term, 0, own, axis=self.dim).astype(jnp.float32)
                for term in self.terms
            )
        )


class Halves:
    def __init__(self, values, axis):
        self.values, self.axis = values, axis

    def hop(self, bit):
        kept, given = halve(self.values, 1)
        self.values = kept + swap(given, self.axis, bit)

    def near(self):
        self.hop(1)

    def far(self):
        for bit in bits_of(lax.axis_size(self.axis))[1:]:
            self.hop(bit)

    def rows(self, axis, bits):
        for bit in bits:
            self.values = self.values + swap(self.values, axis, bit)


def step_both(scatter, stage, gather, gather_stage):
    for bit in scatter.order[stage]:
        kept, given = scatter.split(bit)
        both = jnp.stack([given, gather.values])
        moved = swap(both, scatter.axis, bit)
        scatter.add(kept, moved[0])
        gather.values = gather.join(moved[1], bit)


def square_sum(values):
    return jnp.sum(values * values)


def share_index(axis):
    here = lax.axis_index(axis)
    place = 0
    for bit in bits_of(lax.axis_size(axis)):
        place = place * 2 + (here & bit) // bit
    return place


def unfold_rows(values, axis, dim):
    count = len(bits_of(lax.axis_size(axis)))
    shape = values.shape
    return values.reshape(
        shape[:dim] + (2,) * count + (shape[dim] >> count,) + shape[dim + 1 :]
    )


def fold_rows(values, axis, dim):
    count = len(bits_of(lax.axis_size(axis)))
    shape = values.shape
    return values.reshape(shape[:dim] + (-1,) + shape[dim + count + 1 :])


class Scatter:
    def __init__(self, values, axis, order):
        self.values, self.axis, self.order = unfold_rows(values, axis, 0), axis, list(order)
        self.places = bits_of(lax.axis_size(axis))

    def split(self, bit):
        dim = self.places.index(bit)
        self.places = [place for place in self.places if place != bit]
        side = (lax.axis_index(self.axis) & bit) // bit
        return (
            lax.dynamic_index_in_dim(self.values, side, dim, False),
            lax.dynamic_index_in_dim(self.values, 1 - side, dim, False),
        )

    def add(self, kept, moved):
        values = kept.astype(jnp.float32) + moved.astype(jnp.float32)
        self.values = values.astype(jnp.bfloat16) if self.places else values

    def step(self, stage):
        for bit in self.order[stage]:
            kept, given = self.split(bit)
            self.add(kept, swap(given, self.axis, bit))


class Gather:
    def __init__(self, values, axis, order, dim=0):
        self.values, self.axis, self.order, self.dim = values, axis, list(order), dim
        self.places = []

    def step(self, stage):
        for bit in self.order[stage]:
            moved = swap(self.values, self.axis, bit)
            self.values = self.join(moved, bit)

    def join(self, moved, bit):
        known = self.places + [bit]
        self.places = [place for place in bits_of(lax.axis_size(self.axis)) if place in known]
        dim = self.dim + self.places.index(bit)
        side = (lax.axis_index(self.axis) & bit) // bit
        shape = list(moved.shape)
        shape.insert(dim, 2)
        return jnp.where(
            lax.broadcasted_iota(jnp.int32, shape, dim) == side,
            jnp.expand_dims(self.values, dim),
            jnp.expand_dims(moved, dim),
        )

    def result(self):
        return fold_rows(self.values, self.axis, self.dim)


def stages_of(axis):
    bits = bits_of(lax.axis_size(axis))
    near = len(bits) - 2
    return bits[:near], bits[near : near + 1], bits[near + 1 :]


def adam_kernel(rates, count, flip, factor_ref, *refs):
    term_refs, (master_ref, first_ref, second_ref) = refs[:count], refs[count : count + 3]
    new_ref, first_new_ref, second_new_ref, copy_ref = refs[count + 3 :]
    gradient = sum(term_ref[...].astype(jnp.float32) for term_ref in term_refs)
    if flip:
        gradient = gradient[0].T
    master_new, first_new, second_new = adam_step(
        master_ref[...], first_ref[...], second_ref[...], gradient, factor_ref[0], *rates
    )
    new_ref[...] = master_new
    first_new_ref[...] = first_new
    second_new_ref[...] = second_new
    copy_ref[...] = master_new.astype(jnp.bfloat16)


def adam_call(terms, master, first_moment, second_moment, factor, rates, grid, block, spot):
    flip = spot is not None
    own = pl.BlockSpec(block, lambda *steps: steps[: len(grid)])
    if flip:
        term_specs = [
            pl.BlockSpec((1,) + master.shape[::-1], lambda *steps: (spot, 0, 0)) for term in terms
        ]
    else:
        term_specs = [own] * len(terms)
    wide = jax.ShapeDtypeStruct(master.shape, jnp.float32)
    return pl.pallas_call(
        functools.partial(adam_kernel, rates, len(terms), flip),
        grid=grid,
        in_specs=[pl.BlockSpec(memory_space=pltpu.SMEM)] + term_specs + [own] * 3,
        out_specs=[own] * 4,
        out_shape=[wide, wide, wide, jax.ShapeDtypeStruct(master.shape, jnp.bfloat16)],
        compiler_params=pltpu.CompilerParams(vmem_limit_bytes=60 << 20),
        cost_estimate=pl.CostEstimate(
            flops=20 * master.size, bytes_accessed=32 * master.size, transcendentals=0
        ),
    )(factor.reshape(1), *terms, master, first_moment, second_moment)


def lane_block(place_ref, index, cols):
    return pl.ds(pl.multiple_of(place_ref[index] * cols, cols), cols)


def norm_kernel(owners, place_ref, inputs_ref, gains_ref, biases_ref, kept_ref, given_ref):
    cols = inputs_ref.shape[2] // owners
    values = inputs_ref[0].astype(jnp.float32)
    mean_vals = jnp.mean(values, axis=-1, keepdims=True)
    centred = values - mean_vals
    inverse = lax.rsqrt(jnp.mean(centred * centred, axis=-1, keepdims=True) + norm_epsilon)
    for index in range(owners):
        block = inputs_ref[0, :, lane_block(place_ref, index, cols)].astype(jnp.float32)
        spot = slice(index * cols, (index + 1) * cols)
        normed = (block - mean_vals) * inverse * gains_ref[0, :, spot] + biases_ref[0, :, spot]
        target = kept_ref if index < owners // 2 else given_ref
        near = index % (owners // 2)
        target[0, :, near * cols : (near + 1) * cols] = normed.astype(jnp.bfloat16)


def norm_forward(layer_inputs, gains, biases, place, owners):
    count, tokens, width = layer_inputs.shape
    tile = 128
    half = pl.BlockSpec((1, tile, width // 2), lambda c, i, place_ref: (c, i, 0))
    row = pl.BlockSpec((1, 1, width), lambda c, i, place_ref: (c, 0, 0))
    shape = jax.ShapeDtypeStruct((count, tokens, width // 2), jnp.bfloat16)
    return pl.pallas_call(
        functools.partial(norm_kernel, owners),
        grid_spec=pltpu.PrefetchScalarGridSpec(
            num_scalar_prefetch=1,
            grid=(count, tokens // tile),
            in_specs=[
                pl.BlockSpec((1, tile, width), lambda c, i, place_ref: (c, i, 0)),
                row,
                row,
            ],
            out_specs=[half, half],
        ),
        out_shape=[shape, shape],
        compiler_params=pltpu.CompilerParams(vmem_limit_bytes=56 << 20),
        cost_estimate=pl.CostEstimate(
            flops=10 * count * tokens * width,
            bytes_accessed=4 * count * tokens * width,
            transcendentals=0,
        ),
    )(place, layer_inputs, gains[:, None, :], biases[:, None, :])


def turn(values, cosine, sine_low, sine_high):
    width = values.shape[-1]
    return (
        values * cosine
        + pltpu.roll(values, width - ROT // 2, 1) * sine_low
        + pltpu.roll(values, ROT // 2, 1) * sine_high
    )


def masked_probs(query, key_rows, ids_col, ids_row):
    tokens = query.shape[0]
    scores = lax.dot_general(
        query, key_rows, (((1,), (1,)), ((), ())), preferred_element_type=jnp.float32
    ) * (HDIM ** (-0.5))
    here = lax.broadcasted_iota(jnp.int32, (tokens, tokens), 0)
    there = lax.broadcasted_iota(jnp.int32, (tokens, tokens), 1)
    scores = jnp.where((ids_col == ids_row) & (there <= here), scores, -1e30)
    row_max = jnp.max(scores, axis=-1, keepdims=True)
    log_total = jnp.log(jnp.sum(jnp.exp(scores - row_max), axis=-1, keepdims=True)) + row_max
    return jnp.exp(scores - log_total)


def attend_kernel(proj_ref, cos_ref, low_ref, high_ref, col_ref, row_ref, turned_ref, heads_ref):
    tables = (cos_ref[...], low_ref[...], high_ref[...])
    query = turn(proj_ref[0], *tables).astype(jnp.bfloat16)
    key_rows = turn(proj_ref[1], *tables).astype(jnp.bfloat16)
    value_rows = proj_ref[2].astype(jnp.bfloat16)
    turned_ref[0] = query
    turned_ref[1] = key_rows
    turned_ref[2] = value_rows
    prob = masked_probs(query, key_rows, col_ref[...], row_ref[...]).astype(jnp.bfloat16)
    heads_ref[...] = jnp.dot(prob, value_rows, preferred_element_type=jnp.float32).astype(
        jnp.bfloat16
    )


def attend_back_kernel(
    turned_ref, grads_ref, cos_ref, low_ref, high_ref, col_ref, row_ref, back_ref
):
    query, key_rows, value_rows = turned_ref[0], turned_ref[1], turned_ref[2]
    grads = grads_ref[...]
    prob = masked_probs(query, key_rows, col_ref[...], row_ref[...])
    grad_prob = contract_cols(grads, value_rows)
    row_delta = jnp.sum(prob * grad_prob, axis=-1, keepdims=True)
    grad_scores = (prob * (grad_prob - row_delta)).astype(jnp.bfloat16)
    tables = (cos_ref[...], -low_ref[...], -high_ref[...])
    head_scale = HDIM ** (-0.5)
    grad_query = jnp.dot(grad_scores, key_rows, preferred_element_type=jnp.float32) * head_scale
    grad_key = contract_rows(grad_scores, query) * head_scale
    back_ref[0] = turn(grad_query, *tables).astype(jnp.bfloat16)
    back_ref[1] = turn(grad_key, *tables).astype(jnp.bfloat16)
    back_ref[2] = contract_rows(prob.astype(jnp.bfloat16), grads).astype(jnp.bfloat16)


def attend_specs(tokens):
    table = pl.BlockSpec((tokens, HDIM), lambda head: (0, 0))
    heads = pl.BlockSpec((tokens, HDIM), lambda head: (0, head))
    triple = pl.BlockSpec((3, tokens, HDIM), lambda head: (0, 0, head))
    shared = [
        table,
        table,
        table,
        pl.BlockSpec((tokens, 1), lambda head: (0, 0)),
        pl.BlockSpec((1, tokens), lambda head: (0, 0)),
    ]
    return heads, triple, shared


def attend(proj, tables, ids):
    tokens, width = proj.shape[1:]
    heads, triple, shared = attend_specs(tokens)
    return pl.pallas_call(
        attend_kernel,
        grid=(width // HDIM,),
        in_specs=[triple] + shared,
        out_specs=[triple, heads],
        out_shape=[
            jax.ShapeDtypeStruct((3, tokens, width), jnp.bfloat16),
            jax.ShapeDtypeStruct((tokens, width), jnp.bfloat16),
        ],
        compiler_params=pltpu.CompilerParams(vmem_limit_bytes=32 << 20),
        cost_estimate=pl.CostEstimate(
            flops=4 * tokens * tokens * width,
            bytes_accessed=20 * tokens * width,
            transcendentals=2 * tokens * tokens,
        ),
    )(proj, *tables, ids[:, None], ids[None, :])


def attend_back(turned, grads, tables, ids):
    tokens, width = grads.shape
    heads, triple, shared = attend_specs(tokens)
    return pl.pallas_call(
        attend_back_kernel,
        grid=(width // HDIM,),
        in_specs=[triple, heads] + shared,
        out_specs=triple,
        out_shape=jax.ShapeDtypeStruct((3, tokens, width), jnp.bfloat16),
        compiler_params=pltpu.CompilerParams(vmem_limit_bytes=32 << 20),
        cost_estimate=pl.CostEstimate(
            flops=10 * tokens * tokens * width,
            bytes_accessed=14 * tokens * width,
            transcendentals=2 * tokens * tokens,
        ),
    )(turned, grads, *tables, ids[:, None], ids[None, :])


def mix_kernel(
    branch_ref,
    inputs_ref,
    stored_ref,
    entry_ref,
    cotangent_ref,
    valid_ref,
    gain_ref,
    mixer_in_ref,
    mixer_out_ref,
    newest_ref,
    grad_newest_ref,
    sent_kept_ref,
    sent_given_ref,
    mixer_in_grad_ref,
    mixer_out_grad_ref,
    gain_grad_ref,
):
    valid = valid_ref[...]
    gain = gain_ref[...]
    newest = inputs_ref[...].astype(jnp.float32) + valid * branch_ref[...]
    newest_ref[...] = newest.astype(jnp.bfloat16)
    rows, width = newest.shape
    scale = lax.rsqrt(jnp.mean(newest * newest, axis=-1, keepdims=True) + mixer_epsilon)
    normed = (newest * scale * gain).astype(jnp.bfloat16)
    mix_pre = contract_cols(normed, mixer_in_ref[...])
    phi, density = gelu_parts(mix_pre)
    mix_act = (mix_pre * phi).astype(jnp.bfloat16)
    weights = contract_cols(mix_act, mixer_out_ref[...])
    count = stored_ref.shape[0] + 1
    total = weights.shape[1]
    lane = lax.broadcasted_iota(jnp.int32, (rows, total), 1)
    grad_weights = jnp.zeros((rows, total), jnp.float32)
    newest_back = jnp.zeros((rows, width), jnp.float32)
    for outer in range(total // count):
        upstream = cotangent_ref[outer].astype(jnp.float32)
        for inner in range(count):
            layer = newest if inner == count - 1 else stored_ref[inner].astype(jnp.float32)
            dots = jnp.sum(upstream * layer, axis=-1, keepdims=True)
            grad_weights = jnp.where(lane == outer * count + inner, dots, grad_weights)
        last = outer * count + count - 1
        newest_back = newest_back + weights[:, last : last + 1] * upstream
    grad_weights = grad_weights.astype(jnp.bfloat16)
    mixer_out_grad_ref[...] = contract_rows(grad_weights, mix_act)
    grad_act = jnp.dot(grad_weights, mixer_out_ref[...], preferred_element_type=jnp.float32)
    grad_pre = ((phi + mix_pre * density) * grad_act).astype(jnp.bfloat16)
    mixer_in_grad_ref[...] = contract_rows(grad_pre, normed)
    grad_normed = jnp.dot(grad_pre, mixer_in_ref[...], preferred_element_type=jnp.float32)
    gain_grad_ref[...] = jnp.sum(grad_normed * newest * scale, axis=0, keepdims=True)
    scaled = grad_normed * gain
    grad_newest = (
        newest_back
        + entry_ref[...].astype(jnp.float32)
        + scale * scaled
        - newest * (scale * scale * scale) * jnp.mean(scaled * newest, axis=-1, keepdims=True)
    )
    grad_newest_ref[...] = grad_newest
    sent = (valid * grad_newest).astype(jnp.bfloat16)
    sent_kept_ref[...] = sent[:, 0 : width // 2]
    sent_given_ref[:, 0 : width // 2] = sent[:, width // 2 :]
    high = weights.astype(jnp.bfloat16)
    rest = (weights - high.astype(jnp.float32)).astype(jnp.bfloat16)
    blank = jnp.zeros((rows, 128 - 2 * total), jnp.bfloat16)
    sent_given_ref[:, width // 2 :] = jnp.concatenate([high, rest, blank], axis=1)


def mix(branch, inputs, stored, entry, cotangent, valid, gain, mixer_in, mixer_out):
    rows, width = branch.shape
    hidden_units = mixer_in.shape[0]
    total = mixer_out.shape[0]
    return pl.pallas_call(
        mix_kernel,
        out_shape=[
            jax.ShapeDtypeStruct((rows, width), jnp.bfloat16),
            jax.ShapeDtypeStruct((rows, width), jnp.float32),
            jax.ShapeDtypeStruct((rows, width // 2), jnp.bfloat16),
            jax.ShapeDtypeStruct((rows, width // 2 + 128), jnp.bfloat16),
            jax.ShapeDtypeStruct((hidden_units, width), jnp.float32),
            jax.ShapeDtypeStruct((total, hidden_units), jnp.float32),
            jax.ShapeDtypeStruct((1, width), jnp.float32),
        ],
        compiler_params=pltpu.CompilerParams(vmem_limit_bytes=32 << 20),
        cost_estimate=pl.CostEstimate(
            flops=60 * rows * width, bytes_accessed=30 * rows * width, transcendentals=0
        ),
    )(branch, inputs, stored, entry, cotangent, valid, gain, mixer_in, mixer_out)


def history_kernel(owners, count, place_ref, weights_ref, cotangent_ref, *back_refs):
    cols = back_refs[0].shape[2]
    weights = weights_ref[...]
    for index in range(owners):
        spot = lane_block(place_ref, index, cols)
        upstream = [
            cotangent_ref[outer, :, spot].astype(jnp.float32)
            for outer in range(cotangent_ref.shape[0])
        ]
        for layer in range(count - 1):
            back_refs[index][layer] = sum(
                weights[:, outer * count + layer : outer * count + layer + 1] * upstream[outer]
                for outer in range(len(upstream))
            ).astype(jnp.bfloat16)


def history_back(weights, cotangent, place, owners):
    outer, tokens, width = cotangent.shape
    total = weights.shape[1]
    count = total // outer
    tile = 128
    return pl.pallas_call(
        functools.partial(history_kernel, owners, count),
        grid_spec=pltpu.PrefetchScalarGridSpec(
            num_scalar_prefetch=1,
            grid=(tokens // tile,),
            in_specs=[
                pl.BlockSpec((tile, total), lambda i, place_ref: (i, 0)),
                pl.BlockSpec((outer, tile, width), lambda i, place_ref: (0, i, 0)),
            ],
            out_specs=[
                pl.BlockSpec((count - 1, tile, width // owners), lambda i, place_ref: (0, i, 0))
            ]
            * owners,
        ),
        out_shape=[
            jax.ShapeDtypeStruct((count - 1, tokens, width // owners), jnp.bfloat16)
        ]
        * owners,
        compiler_params=pltpu.CompilerParams(vmem_limit_bytes=56 << 20),
        cost_estimate=pl.CostEstimate(
            flops=8 * outer * tokens * width,
            bytes_accessed=14 * tokens * width,
            transcendentals=0,
        ),
    )(place, weights, cotangent)


def next_kernel(owners, place_ref, weights_ref, newest_ref, *refs):
    stored_refs, next_ref = refs[:-1], refs[-1]
    cols = newest_ref.shape[1] // owners
    weights = weights_ref[...]
    count = len(stored_refs) + 1
    for index in range(owners):
        spot = slice(index * cols, (index + 1) * cols)
        layers = [stored_ref[:, spot].astype(jnp.float32) for stored_ref in stored_refs]
        layers.append(newest_ref[:, spot].astype(jnp.float32))
        for outer in range(next_ref.shape[0]):
            next_ref[outer, :, lane_block(place_ref, index, cols)] = sum(
                weights[:, outer * count + layer : outer * count + layer + 1] * layers[layer]
                for layer in range(count)
            ).astype(jnp.bfloat16)


def next_layer(weights, stored, newest, place, owners):
    tokens, width = newest.shape
    total = weights.shape[1]
    count = len(stored) + 1
    outer = total // count
    tile = 128
    return pl.pallas_call(
        functools.partial(next_kernel, owners),
        grid_spec=pltpu.PrefetchScalarGridSpec(
            num_scalar_prefetch=1,
            grid=(tokens // tile,),
            in_specs=[
                pl.BlockSpec((tile, total), lambda i, place_ref: (i, 0)),
            ]
            + [pl.BlockSpec((tile, width), lambda i, place_ref: (i, 0))] * count,
            out_specs=pl.BlockSpec((outer, tile, width), lambda i, place_ref: (0, i, 0)),
        ),
        out_shape=jax.ShapeDtypeStruct((outer, tokens, width), jnp.bfloat16),
        compiler_params=pltpu.CompilerParams(vmem_limit_bytes=32 << 20),
        cost_estimate=pl.CostEstimate(
            flops=8 * outer * tokens * width,
            bytes_accessed=16 * tokens * width,
            transcendentals=0,
        ),
    )(place, weights, newest, *stored)


def sums_kernel(owners, place_ref, grads_ref, inputs_ref, sums_ref):
    cols = inputs_ref.shape[2] // owners
    values = inputs_ref[0].astype(jnp.float32)
    mean_vals = jnp.mean(values, axis=-1, keepdims=True)
    centred = values - mean_vals
    inverse = lax.rsqrt(jnp.mean(centred * centred, axis=-1, keepdims=True) + norm_epsilon)

    @pl.when(pl.program_id(1) == 0)
    def clear():
        sums_ref[...] = jnp.zeros_like(sums_ref)

    for index in range(owners):
        spot = lane_block(place_ref, index, cols)
        unit = (inputs_ref[0, :, spot].astype(jnp.float32) - mean_vals) * inverse
        grads = grads_ref[0, :, index * cols : (index + 1) * cols].astype(jnp.float32)
        near = slice(index * cols, (index + 1) * cols)
        sums_ref[0, 0:1, near] += jnp.sum(grads * unit, axis=0, keepdims=True)
        sums_ref[0, 1:2, near] += jnp.sum(grads, axis=0, keepdims=True)


def norm_sums(grads, layer_inputs, first, place, owners):
    count, tokens, width = grads.shape
    tile = 128
    return pl.pallas_call(
        functools.partial(sums_kernel, owners),
        grid_spec=pltpu.PrefetchScalarGridSpec(
            num_scalar_prefetch=1,
            grid=(count, tokens // tile),
            in_specs=[
                pl.BlockSpec((1, tile, width), lambda c, i, place_ref: (c, i, 0)),
                pl.BlockSpec((1, tile, width), lambda c, i, place_ref: (c + first, i, 0)),
            ],
            out_specs=pl.BlockSpec((1, 2, width), lambda c, i, place_ref: (c, 0, 0)),
        ),
        out_shape=jax.ShapeDtypeStruct((count, 2, width), jnp.float32),
        compiler_params=pltpu.CompilerParams(vmem_limit_bytes=32 << 20),
        cost_estimate=pl.CostEstimate(
            flops=12 * count * tokens * width,
            bytes_accessed=4 * count * tokens * width,
            transcendentals=0,
        ),
    )(place, grads, layer_inputs)


def back_kernel(owners, place_ref, grads_ref, inputs_ref, gain_ref, extra_ref, out_ref):
    cols = inputs_ref.shape[1] // owners
    values = inputs_ref[...].astype(jnp.float32)
    centred = values - jnp.mean(values, axis=-1, keepdims=True)
    inverse = lax.rsqrt(jnp.mean(centred * centred, axis=-1, keepdims=True) + norm_epsilon)
    back = norm_back(grads_ref[...], centred * inverse, inverse, gain_ref[...])
    if extra_ref is not None:
        back = back + extra_ref[...]
    for index in range(owners):
        spot = slice(index * cols, (index + 1) * cols)
        out_ref[:, lane_block(place_ref, index, cols)] = back[:, spot].astype(jnp.bfloat16)


def back_share(grads, inputs, gain, extra, place, owners):
    rows, width = grads.shape
    kernel = functools.partial(back_kernel, owners)
    if extra is None:
        kernel = lambda place_ref, grads_ref, inputs_ref, gain_ref, out_ref: back_kernel(
            owners, place_ref, grads_ref, inputs_ref, gain_ref, None, out_ref
        )
    whole = pl.BlockSpec((rows, width), lambda i, place_ref: (0, 0))
    given = [grads, inputs, gain] + ([] if extra is None else [extra])
    return pl.pallas_call(
        kernel,
        grid_spec=pltpu.PrefetchScalarGridSpec(
            num_scalar_prefetch=1,
            grid=(1,),
            in_specs=[whole, whole, pl.BlockSpec((1, width), lambda i, place_ref: (0, 0))]
            + ([] if extra is None else [whole]),
            out_specs=whole,
        ),
        out_shape=jax.ShapeDtypeStruct((rows, width), jnp.bfloat16),
        compiler_params=pltpu.CompilerParams(vmem_limit_bytes=32 << 20),
        cost_estimate=pl.CostEstimate(
            flops=15 * rows * width, bytes_accessed=10 * rows * width, transcendentals=0
        ),
    )(place, *given)


def body(
    layer_inputs,
    history,
    seq_ids,
    norms_master,
    norms_first,
    norms_second,
    attend_in_master,
    attend_in_first,
    attend_in_second,
    attend_out_master,
    attend_out_first,
    attend_out_second,
    expand_master,
    expand_first,
    expand_second,
    project_master,
    project_first,
    project_second,
    mixer_in_master,
    mixer_in_first,
    mixer_in_second,
    mixer_out_master,
    mixer_out_first,
    mixer_out_second,
    next_cotangent,
    grad_entry,
):
    bf16_type = jnp.bfloat16
    float_type = jnp.float32
    tensor_size = lax.axis_size("tensor")
    owners = lax.axis_size("dp")
    me = lax.axis_index("dp")
    order = feature_order(owners)
    place = jnp.stack([me ^ index for index in order]).astype(jnp.int32)
    tokens_here, width = layer_inputs.shape[1:]
    share_rows = tokens_here // tensor_size
    share_start = share_index("tensor") * share_rows
    cols = norms_master.shape[1]
    mixers = mixer_out_master.shape[0]

    def own_rows(values, axis):
        return lax.dynamic_slice_in_dim(values, share_start, share_rows, axis)

    def reorder(values):
        return jnp.concatenate(
            [
                lax.dynamic_slice_in_dim(values, (me ^ index) * cols, cols, values.ndim - 1)
                for index in order
            ],
            axis=-1,
        )


    near, side_bits, far = stages_of("tensor")
    out_first = (near, side_bits, far)
    in_first = (side_bits, far, near)
    back_order = (far, side_bits, near)
    cross_order = (near, far, side_bits)

    small = jnp.concatenate(
        [
            norms_master,
            mixer_in_master.T,
            jnp.pad(mixer_out_master, ((0, 0), (0, cols - MIXH))),
        ],
        axis=0,
    ).astype(bf16_type)
    small_half = gather_half(small, "dp", 1)
    attend_low = jnp.concatenate(
        [attend_in_master.astype(bf16_type), attend_out_master.astype(bf16_type).T[None]], axis=0
    )
    small_half, attend_low, history_late, entry_late, expand_late = sync(
        [small_half, attend_low, history, grad_entry, expand_master], []
    )
    attend_kept = gather_half(attend_low, "dp", 1)
    early_rows = [
        jnp.concatenate(
            [
                lax.dynamic_slice_in_dim(
                    values, (me ^ index) * tokens_here + share_start, share_rows, 1
                )
                for values in (history_late, entry_late[None])
            ],
            axis=0,
        )
        for index in order
    ]
    early_rows = [
        rows if index == 0 else swap(rows, "dp", index) for rows, index in zip(early_rows, order)
    ]
    expand_low = expand_late.astype(bf16_type)
    small_given = swap(small_half, "dp", 1)
    small_whole = jnp.concatenate([small_half, small_given], axis=1)
    norm_vals = small_whole[0:9].astype(float_type)
    mixer_in_low = small_whole[9 : 9 + MIXH]
    out_rows = small_whole[9 + MIXH :]
    mixer_out_low = jnp.zeros((owners, mixers, MIXH), bf16_type)
    for spot, index in enumerate(order):
        mixer_out_low = lax.dynamic_update_index_in_dim(
            mixer_out_low, out_rows[:, spot * cols : spot * cols + MIXH], me ^ index, 0
        )
    mixer_out_low = mixer_out_low.reshape(owners * mixers, MIXH)
    normed_kept, normed_given = norm_forward(
        layer_inputs, norm_vals[0:4], norm_vals[4:8], place, owners
    )
    early_rows, attend_kept, normed_kept, normed_given, expand_low, project_late = sync(
        [early_rows, attend_kept, normed_kept, normed_given, expand_low, project_master], []
    )

    early = jnp.concatenate(early_rows, axis=-1)
    stored_share = early[:-1]
    layer_count = stored_share.shape[0] + 1
    stored_most = Gather(stored_share[:-1], "tensor", back_order, 1)
    stored_last = Gather(stored_share[-1:], "tensor", cross_order, 1)
    expand_kept = gather_half(expand_low, "dp", 0)
    attend_given = swap(attend_kept, "dp", 1)
    stored_most.step(0)
    stored_last.step(0)
    proj_kept = jnp.einsum(
        "ctd,cde->cte", normed_kept[0:3], attend_kept[0:3], preferred_element_type=float_type
    )
    cosine, sine_table, unused = angles(seq_ids)
    half = ROT // 2
    tables = (
        jnp.concatenate([cosine, cosine, jnp.ones((tokens_here, HDIM - ROT), float_type)], 1),
        jnp.pad(-sine_table, ((0, 0), (0, HDIM - half))),
        jnp.pad(sine_table, ((0, 0), (half, HDIM - ROT))),
    )
    project_low = project_late.astype(bf16_type)
    expand_kept, attend_given, proj_kept, project_low, tables, layer_late, cotangent_late = sync(
        [
            expand_kept,
            attend_given,
            proj_kept,
            project_low,
            tables,
            layer_inputs,
            next_cotangent,
        ],
        [stored_most, stored_last],
    )

    project_kept = gather_half(project_low, "dp", 1)
    expand_given = swap(expand_kept, "dp", 1)
    stored_most.step(1)
    stored_last.step(1)
    proj = proj_kept + jnp.einsum(
        "ctd,cde->cte", normed_given[0:3], attend_given[0:3], preferred_element_type=float_type
    )
    turned, heads_out = attend(proj, tables, seq_ids)
    upper_kept = jnp.dot(normed_kept[3], expand_kept, preferred_element_type=float_type)
    valid = (own_rows(seq_ids, 0) >= 0).astype(float_type)[:, None]
    input_share = reorder(own_rows(layer_late, 1))
    cotangent_share = reorder(own_rows(cotangent_late, 1))
    (
        project_kept,
        expand_given,
        turned,
        heads_out,
        upper_kept,
        input_share,
        cotangent_share,
    ) = sync(
        [
            project_kept,
            expand_given,
            turned,
            heads_out,
            upper_kept,
            input_share,
            cotangent_share,
        ],
        [stored_most, stored_last],
    )

    out_kept, out_given = attend_kept[3], attend_given[3]
    project_given = swap(project_kept, "dp", 1)
    upper = upper_kept + jnp.dot(normed_given[3], expand_given, preferred_element_type=float_type)
    hidden = exact_gelu(upper).astype(bf16_type)
    branch_kept = Scatter(
        (
            contract_cols(heads_out, out_kept)
            + jnp.dot(hidden, project_kept, preferred_element_type=float_type)
        ).astype(bf16_type),
        "tensor",
        out_first,
    )
    branch_given = Scatter(
        (
            contract_cols(heads_out, out_given)
            + jnp.dot(hidden, project_given, preferred_element_type=float_type)
        ).astype(bf16_type),
        "tensor",
        in_first,
    )
    for stage in range(2):
        branch_kept.step(stage)
        branch_given.step(stage)
    (upper,) = sync([upper], [branch_kept, branch_given])
    branch_kept.step(2)
    branch_given.step(2)
    branch = jnp.concatenate([branch_kept.values, branch_given.values], axis=-1)
    phi, density = gelu_parts(upper)
    slope = phi + upper * density
    branch, slope = sync([branch, slope], [])

    newest, grad_newest, sent_kept, sent_given, grad_mixer_in, grad_mixer_out, mixer_gain = mix(
        branch,
        input_share[3],
        stored_share,
        early[-1],
        cotangent_share,
        valid,
        norm_vals[8:9],
        mixer_in_low,
        mixer_out_low,
    )
    grad_kept = Gather(sent_kept, "tensor", back_order)
    grad_given = Gather(sent_given, "tensor", cross_order)
    for stage in range(3):
        grad_kept.step(stage)
        grad_given.step(stage)
    grad_kept = grad_kept.result()
    received = grad_given.result()
    grad_given = received[:, 0 : width // 2]
    mix_low = received[:, width // 2 :]
    mix_total = 4 * layer_count
    mix_weights = mix_low[:, 0:mix_total].astype(float_type) + mix_low[
        :, mix_total : 2 * mix_total
    ].astype(float_type)
    newest_all = Gather(newest, "tensor", back_order)
    grad_kept, grad_given, mix_weights = sync(
        [grad_kept, grad_given, mix_weights], [newest_all, stored_last, stored_most]
    )

    history_pieces = list(history_back(mix_weights, cotangent_late, place, owners))

    def send_far(pieces, which):
        for spot in which:
            pieces[spot] = swap(pieces[spot], "dp", order[spot])

    far_spots = [spot for spot in range(owners) if order[spot] > 1]
    near_spots = [spot for spot in range(owners) if order[spot] == 1]
    first_far, last_far = far_spots[: len(far_spots) // 2], far_spots[len(far_spots) // 2 :]
    stored_pair = [
        Gather(stored_most.values[index : index + 1], "tensor", back_order, 1)
        for index in range(layer_count - 2)
    ]
    for item in stored_pair:
        item.places = list(stored_most.places)
    for item in stored_pair[:1]:
        item.step(2)
    stored_last.step(2)
    newest_all.step(0)
    grad_hidden = contract_cols(grad_kept, project_kept) + contract_cols(grad_given, project_given)
    grad_upper = (slope * grad_hidden).astype(bf16_type)
    grad_normed_ffn = jnp.concatenate(
        [
            contract_cols(grad_upper, expand_kept).astype(bf16_type),
            contract_cols(grad_upper, expand_given).astype(bf16_type),
        ],
        axis=-1,
    )
    grad_project = Reduce(
        contract_rows(hidden, grad_kept).astype(bf16_type),
        contract_rows(hidden, grad_given).astype(bf16_type),
        "dp",
        1,
    )
    (
        history_pieces,
        grad_normed_ffn,
        grad_upper,
        grad_kept,
        grad_given,
        out_kept,
        out_given,
    ) = sync(
        [history_pieces, grad_normed_ffn, grad_upper, grad_kept, grad_given, out_kept, out_given],
        [newest_all, stored_last, grad_project] + stored_pair,
    )

    newest_all.step(1)
    for item in stored_pair[1:]:
        item.step(2)
    send_far(history_pieces, near_spots)
    grad_project.near()
    grad_heads = (
        jnp.dot(grad_kept, out_kept, preferred_element_type=float_type)
        + jnp.dot(grad_given, out_given, preferred_element_type=float_type)
    ).astype(bf16_type)
    grad_proj = attend_back(turned, grad_heads, tables, seq_ids)
    grad_normed_attend = [
        jnp.concatenate(
            [
                contract_cols(grad_proj[index], weights[index]).astype(bf16_type)
                for weights in (attend_kept, attend_given)
            ],
            axis=-1,
        )
        for index in range(3)
    ]
    attend_grads = [
        jnp.concatenate(
            [
                jnp.einsum(
                    "ctd,cte->cde", normed[0:3], grad_proj, preferred_element_type=float_type
                ).astype(bf16_type),
                contract_rows(grads, heads_out).astype(bf16_type)[None],
            ],
            axis=0,
        )
        for normed, grads in ((normed_kept, grad_kept), (normed_given, grad_given))
    ]
    grad_attend = Reduce(*attend_grads, "dp", 1)
    grad_expand = Reduce(
        contract_rows(normed_kept[3], grad_upper).astype(bf16_type),
        contract_rows(normed_given[3], grad_upper).astype(bf16_type),
        "dp",
        0,
    )
    grad_normed_attend, grad_normed_ffn, history_pieces, layer_late = sync(
        [grad_normed_attend, grad_normed_ffn, history_pieces, layer_late],
        [grad_attend, grad_expand, grad_project, newest_all] + stored_pair,
    )

    summed = [
        Scatter(grad_normed_attend[index], "tensor", out_first) for index in range(3)
    ] + [Scatter(grad_normed_ffn, "tensor", in_first)]
    summed[0].step(0)
    summed[3].step(0)
    send_far(history_pieces, first_far)
    grad_attend.near()
    grad_expand.near()
    sums = [
        norm_sums(grads[None], layer_late, index, place, owners)[0]
        for index, grads in enumerate(grad_normed_attend + [grad_normed_ffn])
    ]
    sums, history_pieces = sync(
        [sums, history_pieces], summed + [newest_all, grad_project, grad_attend, grad_expand]
    )

    norm_pack = jnp.stack(sums)
    own_rows_out = jnp.stack(
        [
            lax.dynamic_index_in_dim(
                grad_mixer_out.reshape(owners, mixers * MIXH), me ^ index, 0, False
            )
            for index in order
        ]
    )
    pack = Halves(
        jnp.concatenate(
            [
                norm_pack[:, 0],
                norm_pack[:, 1],
                mixer_gain,
                grad_mixer_in,
                jnp.pad(own_rows_out, ((0, 0), (0, cols - mixers * MIXH))).reshape(1, width),
            ],
            axis=0,
        ),
        "dp",
    )
    pack.near()
    summed[1].step(0)
    summed[3].step(1)
    summed[3].step(2)
    summed[0].step(1)
    send_far(history_pieces, last_far)
    grad_project.prepare()
    (history_pieces,) = sync(
        [history_pieces], summed + [grad_project, grad_expand, grad_attend, pack]
    )

    def back(index):
        return Gather(
            back_share(
                summed[index].values,
                input_share[index],
                norm_vals[index][None],
                grad_newest if index == 3 else None,
                place,
                owners,
            ),
            "tensor",
            back_order,
        )

    gathered = [None, None, None, back(3)]
    summed[2].step(0)
    summed[1].step(1)
    step_both(summed[0], 2, gathered[3], 0)
    grad_project.far()
    grad_expand.prepare()
    pack.far()
    sync([], summed[0:3] + [gathered[3], grad_expand, grad_project, grad_attend, newest_all, pack])

    gathered[0] = back(0)
    newest_all.step(2)
    step_both(summed[2], 1, gathered[3], 1)
    step_both(summed[1], 2, gathered[0], 0)
    grad_expand.far()
    grad_attend.prepare()
    pack.rows("tensor", near)
    (project_squares,) = sync(
        [grad_project.squares()],
        summed[1:3] + [gathered[0], gathered[3], newest_all, grad_attend, grad_expand, pack],
    )

    gathered[1] = back(1)
    gathered[3].step(2)
    step_both(summed[2], 2, gathered[1], 0)
    gathered[0].step(1)
    grad_attend.far()
    pack.rows("tensor", side_bits)
    newest_whole = newest_all.result()
    newest_stored = [item.result()[0] for item in stored_pair] + [stored_last.result()[0]]
    expand_squares, newest_whole, newest_stored, mix_weights = sync(
        [grad_expand.squares(), newest_whole, newest_stored, mix_weights],
        [summed[2], gathered[0], gathered[1], gathered[3], grad_attend, pack],
    )

    gathered[2] = back(2)
    gathered[0].step(2)
    gathered[2].step(0)
    gathered[1].step(1)
    pack.rows("tensor", far)
    entry_pieces = [newest_whole[:, spot * cols : (spot + 1) * cols] for spot in range(owners)]
    send_far(entry_pieces, first_far)
    next_inputs = next_layer(mix_weights, newest_stored, newest_whole, place, owners)
    attend_squares, entry_pieces, next_inputs = sync(
        [grad_attend.squares(), entry_pieces, next_inputs],
        [gathered[0], gathered[1], gathered[2], pack],
    )

    gathered[1].step(2)
    gathered[2].step(1)
    send_far(entry_pieces, last_far)
    send_far(entry_pieces, near_spots)
    own_pack = pack.values
    norm_grad = own_pack[0:9]
    grad_mixer_in = own_pack[9 : 9 + MIXH].T
    grad_mixer_out = own_pack[9 + MIXH, 0 : mixers * MIXH].reshape(mixers, MIXH)
    shared_squares = (
        square_sum(norm_grad) + square_sum(grad_mixer_in) + square_sum(grad_mixer_out)
    )
    shard_squares = project_squares + expand_squares + attend_squares
    total_squares = (shard_squares + shared_squares / tensor_size).reshape(1, 1)
    for axis, bits in (
        ("dp", bits_of(owners)[:1]),
        ("tensor", side_bits + far),
        ("dp", bits_of(owners)[1:]),
        ("tensor", near),
    ):
        for bit in bits:
            total_squares = total_squares + swap(total_squares, axis, bit)
    total_squares, entry_pieces = sync(
        [total_squares, entry_pieces], [gathered[1], gathered[2]]
    )
    total_squares = total_squares[0, 0]

    gathered[2].step(2)
    grad_norm = jnp.sqrt(total_squares)
    factor = jnp.minimum(1.0, clip_level / grad_norm)
    wide_rate = 2.0 / math.sqrt(D)
    wide = (wide_rate, weight_decay)
    norms_out = adam_step(norms_master, norms_first, norms_second, norm_grad, factor, 1.0, 0.0)
    mixer_in_out = adam_step(
        mixer_in_master,
        mixer_in_first,
        mixer_in_second,
        grad_mixer_in,
        factor,
        wide_rate,
        weight_decay,
    )
    mixer_out_out = adam_step(
        mixer_out_master,
        mixer_out_first,
        mixer_out_second,
        grad_mixer_out,
        factor,
        2.0 / math.sqrt(MIXH),
        weight_decay,
    )
    parts, rows, units = attend_in_master.shape
    attend_in_out = adam_call(
        grad_attend.terms,
        attend_in_master,
        attend_in_first,
        attend_in_second,
        factor,
        wide,
        (parts, 1, 1),
        (1, rows, units),
        None,
    )
    attend_out_out = adam_call(
        grad_attend.terms,
        attend_out_master,
        attend_out_first,
        attend_out_second,
        factor,
        wide,
        (1, 1),
        attend_out_master.shape,
        parts,
    )
    rows, units = expand_master.shape
    expand_out = adam_call(
        grad_expand.terms,
        expand_master,
        expand_first,
        expand_second,
        factor,
        wide,
        (4, 1),
        (rows // 4, units),
        None,
    )
    rows, units = project_master.shape
    project_out = adam_call(
        grad_project.terms,
        project_master,
        project_first,
        project_second,
        factor,
        (2.0 / math.sqrt(FF), weight_decay),
        (4, 1),
        (rows // 4, units),
        None,
    )
    new_entry = jnp.zeros(grad_entry.shape, bf16_type)
    grad_history = jnp.zeros(history.shape, bf16_type)
    for spot, index in enumerate(order):
        first_row = (me ^ index) * tokens_here
        new_entry = lax.dynamic_update_slice_in_dim(new_entry, entry_pieces[spot], first_row, 0)
        grad_history = lax.dynamic_update_slice_in_dim(
            grad_history, history_pieces[spot], first_row, 1
        )
    grad_inputs = jnp.zeros(layer_inputs.shape, bf16_type)
    for index in (3, 0, 1, 2):
        grad_inputs = lax.dynamic_update_index_in_dim(
            grad_inputs, gathered[index].result(), index, 0
        )
    return (
        next_inputs,
        new_entry,
        grad_inputs,
        grad_history,
        norms_out[0],
        norms_out[1],
        norms_out[2],
        attend_in_out[0],
        attend_in_out[1],
        attend_in_out[2],
        attend_in_out[3],
        attend_out_out[0],
        attend_out_out[1],
        attend_out_out[2],
        attend_out_out[3],
        expand_out[0],
        expand_out[1],
        expand_out[2],
        expand_out[3],
        project_out[0],
        project_out[1],
        project_out[2],
        project_out[3],
        mixer_in_out[0],
        mixer_in_out[1],
        mixer_in_out[2],
        mixer_in_out[0].astype(bf16_type),
        mixer_out_out[0],
        mixer_out_out[1],
        mixer_out_out[2],
        mixer_out_out[0].astype(bf16_type),
        grad_norm,
    )


def solution(mesh):
    in_specs = (
        P(None, "dp", None),
        P(None, None, "dp"),
        P("dp"),
        P(None, "dp"),
        P(None, "dp"),
        P(None, "dp"),
        P(None, "dp", "tensor"),
        P(None, "dp", "tensor"),
        P(None, "dp", "tensor"),
        P("tensor", "dp"),
        P("tensor", "dp"),
        P("tensor", "dp"),
        P("dp", "tensor"),
        P("dp", "tensor"),
        P("dp", "tensor"),
        P("tensor", "dp"),
        P("tensor", "dp"),
        P("tensor", "dp"),
        P("dp", None),
        P("dp", None),
        P("dp", None),
        P("dp", None),
        P("dp", None),
        P("dp", None),
        P(None, "dp", None),
        P(None, "dp"),
    )
    out_specs = (
        P(None, "dp", None),
        P(None, "dp"),
        P(None, "dp", None),
        P(None, None, "dp"),
        P(None, "dp"),
        P(None, "dp"),
        P(None, "dp"),
        P(None, "dp", "tensor"),
        P(None, "dp", "tensor"),
        P(None, "dp", "tensor"),
        P(None, "dp", "tensor"),
        P("tensor", "dp"),
        P("tensor", "dp"),
        P("tensor", "dp"),
        P("tensor", "dp"),
        P("dp", "tensor"),
        P("dp", "tensor"),
        P("dp", "tensor"),
        P("dp", "tensor"),
        P("tensor", "dp"),
        P("tensor", "dp"),
        P("tensor", "dp"),
        P("tensor", "dp"),
        P("dp", None),
        P("dp", None),
        P("dp", None),
        P("dp", None),
        P("dp", None),
        P("dp", None),
        P("dp", None),
        P("dp", None),
        P(),
    )
    return jax.shard_map(body, mesh=mesh, in_specs=in_specs, out_specs=out_specs, check_vma=False)
```

```python
import functools
import math

import jax
import jax.numpy as jnp
from jax import lax
from jax.experimental import pallas as pl
from jax.experimental.pallas import tpu as pltpu
from jax.sharding import PartitionSpec as P

D = 2048
HDIM = 128
FF = 8192
MIXH = 36
ROT = 32
STEP = 10


norm_epsilon = 1e-05
mixer_epsilon = 1e-06
clip_level = 1.0
beta_first = 0.9
beta_second = 0.95
adam_epsilon = 1e-08
weight_decay = 0.1


def exact_gelu(values):
    return jax.nn.gelu(values, approximate=False)


def gelu_grad(values, upstream):
    unused, pullback = jax.vjp(exact_gelu, values)
    return pullback(upstream)[0]


def rotate(vectors, cosine, sine_table):
    half = ROT // 2
    first_half = vectors[..., :half]
    second_half = vectors[..., half:ROT]
    return jnp.concatenate(
        [
            first_half * cosine - second_half * sine_table,
            second_half * cosine + first_half * sine_table,
            vectors[..., ROT:],
        ],
        axis=-1,
    )


def angles(bucket_ids):
    same_seq = bucket_ids[:, None] == bucket_ids[None, :]
    order = jnp.arange(bucket_ids.shape[0])
    earlier = order[None, :] < order[:, None]
    position = jnp.sum(jnp.where(same_seq & earlier, 1, 0), axis=1).astype(jnp.float32)
    freqs = 10000.0 ** (-2.0 * jnp.arange(ROT // 2).astype(jnp.float32) / ROT)
    angle = position[:, None] * freqs[None, :]
    allowed = same_seq & (order[None, :] <= order[:, None])
    return (jnp.cos(angle), jnp.sin(angle), allowed)


def score_block(query, key_rows, allowed):
    head_scale = HDIM ** (-0.5)
    scores = (
        jnp.einsum("hqd,hkd->hqk", query, key_rows, preferred_element_type=jnp.float32) * head_scale
    )
    return jnp.where(allowed[None], scores, -1e30)


def norm_back(grad_rows, unit_rows, inverse_rows, gain_rows):
    scaled = grad_rows * gain_rows
    mean_scaled = jnp.mean(scaled, axis=-1, keepdims=True)
    mean_cross = jnp.mean(scaled * unit_rows, axis=-1, keepdims=True)
    return inverse_rows * (scaled - mean_scaled - unit_rows * mean_cross)


def contract_rows(left, right):
    return lax.dot_general(
        left, right, (((0,), (0,)), ((), ())), preferred_element_type=jnp.float32
    )


def contract_cols(left, right):
    return lax.dot_general(
        left, right, (((1,), (1,)), ((), ())), preferred_element_type=jnp.float32
    )


def adam_step(master, first_moment, second_moment, gradient, factor, step_rate, decay_rate):
    scaled = gradient * factor
    first_new = beta_first * first_moment + (1.0 - beta_first) * scaled
    second_new = beta_second * second_moment + (1.0 - beta_second) * scaled * scaled
    first_hat = first_new / (1.0 - beta_first**STEP)
    second_hat = second_new / (1.0 - beta_second**STEP)
    master_new = master - step_rate * (
        first_hat / (jnp.sqrt(second_hat) + adam_epsilon) + decay_rate * master
    )
    return (master_new, first_new, second_new)


def gelu_parts(values):
    upper_share = 0.5 * (1.0 + lax.erf(values * math.sqrt(0.5)))
    density = jnp.exp(-0.5 * values * values) * (1.0 / math.sqrt(2.0 * math.pi))
    return upper_share, density


def bits_of(size):
    return [1 << index for index in range(size.bit_length() - 1)]


def feature_order(owners):
    order = [0]
    for bit in reversed(bits_of(owners)):
        order = order + [index | bit for index in order]
    return order


def swap(values, axis, mask):
    size = lax.axis_size(axis)
    return lax.ppermute(values, axis, [(source, source ^ mask) for source in range(size)])


def sync(plain, steps):
    held = [vars(item) for item in steps]
    names = [
        [name for name in ("values", "terms", "given", "moved") if item.get(name) is not None]
        for item in held
    ]
    plain, inner = lax.optimization_barrier(
        (
            list(plain),
            [[item[name] for name in kinds] for item, kinds in zip(held, names)],
        )
    )
    for item, kinds, values in zip(steps, names, inner):
        for name, value in zip(kinds, values):
            setattr(item, name, value)
    return plain


def gather_half(piece, axis, dim):
    for bit in reversed(bits_of(lax.axis_size(axis))[1:]):
        piece = jnp.concatenate([piece, swap(piece, axis, bit)], axis=dim)
    return piece


def halve(values, dim):
    half = values.shape[dim] // 2
    return (
        lax.slice_in_dim(values, 0, half, axis=dim),
        lax.slice_in_dim(values, half, 2 * half, axis=dim),
    )


class Reduce:
    def __init__(self, kept, given, axis, dim):
        self.terms, self.given, self.axis, self.dim = [kept], given, axis, dim

    def near(self):
        self.terms.append(swap(self.given, self.axis, 1))
        self.given = None

    def prepare(self):
        half = self.terms[-1].shape[self.dim] // 2
        self.given = sum(
            lax.slice_in_dim(term, half, 2 * half, axis=self.dim).astype(jnp.float32)
            for term in self.terms
        ).astype(jnp.bfloat16)

    def far(self):
        for bit in bits_of(lax.axis_size(self.axis))[1:]:
            if self.given is None:
                self.prepare()
            self.terms.append(swap(self.given, self.axis, bit))
            self.given = None

    def own(self):
        own = self.terms[-1].shape[self.dim]
        return sum(
            lax.slice_in_dim(term, 0, own, axis=self.dim).astype(jnp.float32)
            for term in self.terms
        )

    def squares(self):
        return square_sum(self.own())


class Halves:
    def __init__(self, values, axis):
        self.values, self.axis = values, axis

    def hop(self, bit):
        kept, given = halve(self.values, 1)
        self.values = kept + swap(given, self.axis, bit)

    def near(self):
        self.hop(1)

    def far(self):
        for bit in bits_of(lax.axis_size(self.axis))[1:]:
            self.hop(bit)

    def rows(self, axis, bits):
        for bit in bits:
            self.values = self.values + swap(self.values, axis, bit)


def step_both(scatter, stage, gather, gather_stage):
    for bit in scatter.order[stage]:
        given = scatter.split(bit)
        gather.settle()
        moved = swap(jnp.stack([given, gather.values]), scatter.axis, bit)
        scatter.moved, gather.moved, gather.bit = moved[0], moved[1], bit


def square_sum(values):
    return jnp.sum(values * values)


def share_index(axis):
    here = lax.axis_index(axis)
    place = 0
    for bit in bits_of(lax.axis_size(axis)):
        place = place * 2 + (here & bit) // bit
    return place


def unfold_rows(values, axis, dim):
    count = len(bits_of(lax.axis_size(axis)))
    shape = values.shape
    return values.reshape(
        shape[:dim] + (2,) * count + (shape[dim] >> count,) + shape[dim + 1 :]
    )


def fold_rows(values, axis, dim):
    count = len(bits_of(lax.axis_size(axis)))
    shape = values.shape
    return values.reshape(shape[:dim] + (-1,) + shape[dim + count + 1 :])


class Scatter:
    def __init__(self, values, axis, order):
        self.values, self.axis, self.order = unfold_rows(values, axis, 0), axis, list(order)
        self.places = bits_of(lax.axis_size(axis))
        self.moved = None

    def split(self, bit):
        self.settle()
        dim = self.places.index(bit)
        self.places = [place for place in self.places if place != bit]
        side = (lax.axis_index(self.axis) & bit) // bit
        given = lax.dynamic_index_in_dim(self.values, 1 - side, dim, False)
        self.values = lax.dynamic_index_in_dim(self.values, side, dim, False)
        return given

    def settle(self):
        if self.moved is not None:
            values = self.values.astype(jnp.float32) + self.moved.astype(jnp.float32)
            self.values = values.astype(jnp.bfloat16) if self.places else values
            self.moved = None

    def step(self, stage):
        for bit in self.order[stage]:
            self.moved = swap(self.split(bit), self.axis, bit)

    def result(self):
        self.settle()
        return self.values


class Gather:
    def __init__(self, values, axis, order, dim=0):
        self.values, self.axis, self.order, self.dim = values, axis, list(order), dim
        self.places, self.moved, self.bit = [], None, None

    def step(self, stage):
        for bit in self.order[stage]:
            self.settle()
            self.moved, self.bit = swap(self.values, self.axis, bit), bit

    def settle(self):
        if self.moved is None:
            return
        known = self.places + [self.bit]
        self.places = [place for place in bits_of(lax.axis_size(self.axis)) if place in known]
        dim = self.dim + self.places.index(self.bit)
        side = (lax.axis_index(self.axis) & self.bit) // self.bit
        shape = list(self.moved.shape)
        shape.insert(dim, 2)
        self.values = jnp.where(
            lax.broadcasted_iota(jnp.int32, shape, dim) == side,
            jnp.expand_dims(self.values, dim),
            jnp.expand_dims(self.moved, dim),
        )
        self.moved = None

    def place_last(self, whole, index):
        spot = bits_of(lax.axis_size(self.axis)).index(self.bit)
        side = (lax.axis_index(self.axis) & self.bit) // self.bit
        for values, at in ((self.values, side), (self.moved, 1 - side)):
            block = jnp.expand_dims(values, spot)[None]
            starts = [0] * block.ndim
            starts[0], starts[spot + 1] = index, at
            whole = lax.dynamic_update_slice(whole, block, starts)
        return whole

    def result(self):
        self.settle()
        return fold_rows(self.values, self.axis, self.dim)


def stages_of(axis):
    bits = bits_of(lax.axis_size(axis))
    near = len(bits) - 2
    return bits[:near], bits[near : near + 1], bits[near + 1 :]


def light():
    return pl.CostEstimate(flops=1, bytes_accessed=1, transcendentals=0)


def join_kernel(*refs):
    out_ref = refs[-1]
    cols = refs[0].shape[-1]
    for index, ref in enumerate(refs[:-1]):
        out_ref[:, :, index * cols : (index + 1) * cols] = ref[...]


def join_blocks(blocks):
    shape = blocks[0].shape
    return pl.pallas_call(
        join_kernel,
        out_shape=jax.ShapeDtypeStruct(
            shape[:-1] + (shape[-1] * len(blocks),), blocks[0].dtype
        ),
        cost_estimate=light(),
    )(*blocks)


def outer_kernel(pairs, *refs):
    for left, right, target in pairs:
        left_ref, right_ref = refs[left], refs[right]
        value = contract_rows(left_ref[...].reshape(left_ref.shape[-2:]), right_ref[...])
        refs[target][...] = value.astype(jnp.bfloat16)


def outer_call(operands, specs, pairs, grid, out_rows, out_cols, tile):
    out = pl.BlockSpec((tile, out_cols), lambda i: (i, 0))
    shape = jax.ShapeDtypeStruct((out_rows, out_cols), jnp.bfloat16)
    return pl.pallas_call(
        functools.partial(outer_kernel, pairs),
        grid=grid,
        in_specs=specs,
        out_specs=[out, out],
        out_shape=[shape, shape],
        compiler_params=pltpu.CompilerParams(vmem_limit_bytes=16 << 20),
        cost_estimate=light(),
    )(*operands)


def project_grads(hidden, kept, given):
    tokens, units = hidden.shape
    tile = 256
    whole = pl.BlockSpec(kept.shape, lambda i: (0, 0))
    return outer_call(
        (hidden, kept, given),
        [pl.BlockSpec((tokens, tile), lambda i: (0, i)), whole, whole],
        ((0, 1, 3), (0, 2, 4)),
        (units // tile,),
        units,
        kept.shape[1],
        tile,
    )


def expand_grads(kept, given, upper):
    count, tokens, width = kept.shape
    tile = 256
    part = pl.BlockSpec((1, tokens, tile), lambda i: (count - 1, 0, i))
    return outer_call(
        (kept, given, upper),
        [part, part, pl.BlockSpec(upper.shape, lambda i: (0, 0))],
        ((0, 2, 3), (1, 2, 4)),
        (width // tile,),
        width,
        upper.shape[1],
        tile,
    )


def attend_grads_kernel(
    kept_ref, given_ref, back_ref, out_kept_ref, out_given_ref, heads_ref, *outs
):
    last = pl.program_id(0) == pl.num_programs(0) - 1
    for left_ref, other_ref, target_ref in (
        (kept_ref, out_kept_ref, outs[0]),
        (given_ref, out_given_ref, outs[1]),
    ):

        @pl.when(jnp.logical_not(last))
        def inner(left_ref=left_ref, target_ref=target_ref):
            target_ref[0] = contract_rows(left_ref[0], back_ref[0]).astype(jnp.bfloat16)

        @pl.when(last)
        def outer(other_ref=other_ref, target_ref=target_ref):
            target_ref[0] = contract_rows(other_ref[...], heads_ref[...]).astype(jnp.bfloat16)


def attend_grads_call(kept, given, back, out_kept, out_given, heads):
    count, tokens, width = kept.shape
    units = heads.shape[1]
    part = pl.BlockSpec((1, tokens, width), lambda c: (jnp.minimum(c, count - 2), 0, 0))
    whole = pl.BlockSpec((tokens, width), lambda c: (0, 0))
    out = pl.BlockSpec((1, width, units), lambda c: (c, 0, 0))
    shape = jax.ShapeDtypeStruct((count, width, units), jnp.bfloat16)
    return pl.pallas_call(
        attend_grads_kernel,
        grid=(count,),
        in_specs=[
            part,
            part,
            pl.BlockSpec((1, tokens, units), lambda c: (jnp.minimum(c, count - 2), 0, 0)),
            whole,
            whole,
            pl.BlockSpec((tokens, units), lambda c: (0, 0)),
        ],
        out_specs=[out, out],
        out_shape=[shape, shape],
        compiler_params=pltpu.CompilerParams(vmem_limit_bytes=20 << 20),
        cost_estimate=light(),
    )(kept, given, back, out_kept, out_given, heads)


def adam_kernel(rates, count, flip, factor_ref, *refs):
    term_refs, (master_ref, first_ref, second_ref) = refs[:count], refs[count : count + 3]
    new_ref, first_new_ref, second_new_ref, copy_ref = refs[count + 3 :]
    gradient = sum(term_ref[...].astype(jnp.float32) for term_ref in term_refs)
    if flip:
        gradient = gradient[0].T
    master_new, first_new, second_new = adam_step(
        master_ref[...], first_ref[...], second_ref[...], gradient, factor_ref[0], *rates
    )
    new_ref[...] = master_new
    first_new_ref[...] = first_new
    second_new_ref[...] = second_new
    copy_ref[...] = master_new.astype(jnp.bfloat16)


def adam_call(terms, master, first_moment, second_moment, factor, rates, grid, block, spot):
    flip = spot is not None
    own = pl.BlockSpec(block, lambda *steps: steps[: len(grid)])
    if flip:
        term_specs = [
            pl.BlockSpec((1,) + master.shape[::-1], lambda *steps: (spot, 0, 0)) for term in terms
        ]
    else:
        term_specs = [own] * len(terms)
    wide = jax.ShapeDtypeStruct(master.shape, jnp.float32)
    return pl.pallas_call(
        functools.partial(adam_kernel, rates, len(terms), flip),
        grid=grid,
        in_specs=[pl.BlockSpec(memory_space=pltpu.SMEM)] + term_specs + [own] * 3,
        out_specs=[own] * 4,
        out_shape=[wide, wide, wide, jax.ShapeDtypeStruct(master.shape, jnp.bfloat16)],
        compiler_params=pltpu.CompilerParams(vmem_limit_bytes=20 << 20),
        cost_estimate=light(),
    )(factor.reshape(1), *terms, master, first_moment, second_moment)


def lane_block(place_ref, index, cols):
    return pl.ds(pl.multiple_of(place_ref[index] * cols, cols), cols)


def norm_kernel(owners, place_ref, inputs_ref, gains_ref, biases_ref, kept_ref, given_ref):
    cols = inputs_ref.shape[2] // owners
    values = inputs_ref[0].astype(jnp.float32)
    mean_vals = jnp.mean(values, axis=-1, keepdims=True)
    centred = values - mean_vals
    inverse = lax.rsqrt(jnp.mean(centred * centred, axis=-1, keepdims=True) + norm_epsilon)
    for index in range(owners):
        block = inputs_ref[0, :, lane_block(place_ref, index, cols)].astype(jnp.float32)
        spot = slice(index * cols, (index + 1) * cols)
        normed = (block - mean_vals) * inverse * gains_ref[0, :, spot] + biases_ref[0, :, spot]
        target = kept_ref if index < owners // 2 else given_ref
        near = index % (owners // 2)
        target[0, :, near * cols : (near + 1) * cols] = normed.astype(jnp.bfloat16)


def norm_forward(layer_inputs, gains, biases, place, owners):
    count, tokens, width = layer_inputs.shape
    tile = 128
    half = pl.BlockSpec((1, tile, width // 2), lambda c, i, place_ref: (c, i, 0))
    row = pl.BlockSpec((1, 1, width), lambda c, i, place_ref: (c, 0, 0))
    shape = jax.ShapeDtypeStruct((count, tokens, width // 2), jnp.bfloat16)
    return pl.pallas_call(
        functools.partial(norm_kernel, owners),
        grid_spec=pltpu.PrefetchScalarGridSpec(
            num_scalar_prefetch=1,
            grid=(count, tokens // tile),
            in_specs=[
                pl.BlockSpec((1, tile, width), lambda c, i, place_ref: (c, i, 0)),
                row,
                row,
            ],
            out_specs=[half, half],
        ),
        out_shape=[shape, shape],
        compiler_params=pltpu.CompilerParams(vmem_limit_bytes=14 << 20),
        cost_estimate=light(),
    )(place, layer_inputs, gains[:, None, :], biases[:, None, :])


def turn(values, cosine, sine_low, sine_high):
    width = values.shape[-1]
    return (
        values * cosine
        + pltpu.roll(values, width - ROT // 2, 1) * sine_low
        + pltpu.roll(values, ROT // 2, 1) * sine_high
    )


def masked_probs(query, key_rows, ids_col, ids_row):
    tokens = query.shape[0]
    scores = lax.dot_general(
        query, key_rows, (((1,), (1,)), ((), ())), preferred_element_type=jnp.float32
    ) * (HDIM ** (-0.5))
    here = lax.broadcasted_iota(jnp.int32, (tokens, tokens), 0)
    there = lax.broadcasted_iota(jnp.int32, (tokens, tokens), 1)
    scores = jnp.where((ids_col == ids_row) & (there <= here), scores, -1e30)
    row_max = jnp.max(scores, axis=-1, keepdims=True)
    log_total = jnp.log(jnp.sum(jnp.exp(scores - row_max), axis=-1, keepdims=True)) + row_max
    return jnp.exp(scores - log_total)


def attend_kernel(proj_ref, cos_ref, low_ref, high_ref, col_ref, row_ref, turned_ref, heads_ref):
    tables = (cos_ref[...], low_ref[...], high_ref[...])
    query = turn(proj_ref[0], *tables).astype(jnp.bfloat16)
    key_rows = turn(proj_ref[1], *tables).astype(jnp.bfloat16)
    value_rows = proj_ref[2].astype(jnp.bfloat16)
    turned_ref[0] = query
    turned_ref[1] = key_rows
    turned_ref[2] = value_rows
    prob = masked_probs(query, key_rows, col_ref[...], row_ref[...]).astype(jnp.bfloat16)
    heads_ref[...] = jnp.dot(prob, value_rows, preferred_element_type=jnp.float32).astype(
        jnp.bfloat16
    )


def attend_back_kernel(
    turned_ref, grads_ref, cos_ref, low_ref, high_ref, col_ref, row_ref, back_ref
):
    query, key_rows, value_rows = turned_ref[0], turned_ref[1], turned_ref[2]
    grads = grads_ref[...]
    prob = masked_probs(query, key_rows, col_ref[...], row_ref[...])
    grad_prob = contract_cols(grads, value_rows)
    row_delta = jnp.sum(prob * grad_prob, axis=-1, keepdims=True)
    grad_scores = (prob * (grad_prob - row_delta)).astype(jnp.bfloat16)
    tables = (cos_ref[...], -low_ref[...], -high_ref[...])
    head_scale = HDIM ** (-0.5)
    grad_query = jnp.dot(grad_scores, key_rows, preferred_element_type=jnp.float32) * head_scale
    grad_key = contract_rows(grad_scores, query) * head_scale
    back_ref[0] = turn(grad_query, *tables).astype(jnp.bfloat16)
    back_ref[1] = turn(grad_key, *tables).astype(jnp.bfloat16)
    back_ref[2] = contract_rows(prob.astype(jnp.bfloat16), grads).astype(jnp.bfloat16)


def attend_specs(tokens):
    table = pl.BlockSpec((tokens, HDIM), lambda head: (0, 0))
    heads = pl.BlockSpec((tokens, HDIM), lambda head: (0, head))
    triple = pl.BlockSpec((3, tokens, HDIM), lambda head: (0, 0, head))
    shared = [
        table,
        table,
        table,
        pl.BlockSpec((tokens, 1), lambda head: (0, 0)),
        pl.BlockSpec((1, tokens), lambda head: (0, 0)),
    ]
    return heads, triple, shared


def attend(proj, tables, ids):
    tokens, width = proj.shape[1:]
    heads, triple, shared = attend_specs(tokens)
    return pl.pallas_call(
        attend_kernel,
        grid=(width // HDIM,),
        in_specs=[triple] + shared,
        out_specs=[triple, heads],
        out_shape=[
            jax.ShapeDtypeStruct((3, tokens, width), jnp.bfloat16),
            jax.ShapeDtypeStruct((tokens, width), jnp.bfloat16),
        ],
        compiler_params=pltpu.CompilerParams(vmem_limit_bytes=16 << 20),
        cost_estimate=light(),
    )(proj, *tables, ids[:, None], ids[None, :])


def attend_back(turned, grads, tables, ids):
    tokens, width = grads.shape
    heads, triple, shared = attend_specs(tokens)
    return pl.pallas_call(
        attend_back_kernel,
        grid=(width // HDIM,),
        in_specs=[triple, heads] + shared,
        out_specs=triple,
        out_shape=jax.ShapeDtypeStruct((3, tokens, width), jnp.bfloat16),
        compiler_params=pltpu.CompilerParams(vmem_limit_bytes=20 << 20),
        cost_estimate=light(),
    )(turned, grads, *tables, ids[:, None], ids[None, :])


def mix_kernel(
    branch_ref,
    inputs_ref,
    stored_ref,
    entry_ref,
    cotangent_ref,
    valid_ref,
    gain_ref,
    mixer_in_ref,
    mixer_out_ref,
    newest_ref,
    grad_newest_ref,
    sent_kept_ref,
    sent_given_ref,
    mixer_in_grad_ref,
    mixer_out_grad_ref,
    gain_grad_ref,
):
    valid = valid_ref[...]
    gain = gain_ref[...]
    newest = inputs_ref[...].astype(jnp.float32) + valid * branch_ref[...]
    newest_ref[...] = newest.astype(jnp.bfloat16)
    rows, width = newest.shape
    scale = lax.rsqrt(jnp.mean(newest * newest, axis=-1, keepdims=True) + mixer_epsilon)
    normed = (newest * scale * gain).astype(jnp.bfloat16)
    mix_pre = contract_cols(normed, mixer_in_ref[...])
    phi, density = gelu_parts(mix_pre)
    mix_act = (mix_pre * phi).astype(jnp.bfloat16)
    weights = contract_cols(mix_act, mixer_out_ref[...])
    count = stored_ref.shape[0] + 1
    total = weights.shape[1]
    lane = lax.broadcasted_iota(jnp.int32, (rows, total), 1)
    grad_weights = jnp.zeros((rows, total), jnp.float32)
    newest_back = jnp.zeros((rows, width), jnp.float32)
    for outer in range(total // count):
        upstream = cotangent_ref[outer].astype(jnp.float32)
        for inner in range(count):
            layer = newest if inner == count - 1 else stored_ref[inner].astype(jnp.float32)
            dots = jnp.sum(upstream * layer, axis=-1, keepdims=True)
            grad_weights = jnp.where(lane == outer * count + inner, dots, grad_weights)
        last = outer * count + count - 1
        newest_back = newest_back + weights[:, last : last + 1] * upstream
    grad_weights = grad_weights.astype(jnp.bfloat16)
    mixer_out_grad_ref[...] = contract_rows(grad_weights, mix_act)
    grad_act = jnp.dot(grad_weights, mixer_out_ref[...], preferred_element_type=jnp.float32)
    grad_pre = ((phi + mix_pre * density) * grad_act).astype(jnp.bfloat16)
    mixer_in_grad_ref[...] = contract_rows(grad_pre, normed)
    grad_normed = jnp.dot(grad_pre, mixer_in_ref[...], preferred_element_type=jnp.float32)
    gain_grad_ref[...] = jnp.sum(grad_normed * newest * scale, axis=0, keepdims=True)
    scaled = grad_normed * gain
    grad_newest = (
        newest_back
        + entry_ref[...].astype(jnp.float32)
        + scale * scaled
        - newest * (scale * scale * scale) * jnp.mean(scaled * newest, axis=-1, keepdims=True)
    )
    grad_newest_ref[...] = grad_newest
    sent = (valid * grad_newest).astype(jnp.bfloat16)
    sent_kept_ref[...] = sent[:, 0 : width // 2]
    sent_given_ref[:, 0 : width // 2] = sent[:, width // 2 :]
    high = weights.astype(jnp.bfloat16)
    rest = (weights - high.astype(jnp.float32)).astype(jnp.bfloat16)
    blank = jnp.zeros((rows, 128 - 2 * total), jnp.bfloat16)
    sent_given_ref[:, width // 2 :] = jnp.concatenate([high, rest, blank], axis=1)


def mix(branch, inputs, stored, entry, cotangent, valid, gain, mixer_in, mixer_out):
    rows, width = branch.shape
    hidden_units = mixer_in.shape[0]
    total = mixer_out.shape[0]
    return pl.pallas_call(
        mix_kernel,
        out_shape=[
            jax.ShapeDtypeStruct((rows, width), jnp.bfloat16),
            jax.ShapeDtypeStruct((rows, width), jnp.float32),
            jax.ShapeDtypeStruct((rows, width // 2), jnp.bfloat16),
            jax.ShapeDtypeStruct((rows, width // 2 + 128), jnp.bfloat16),
            jax.ShapeDtypeStruct((hidden_units, width), jnp.float32),
            jax.ShapeDtypeStruct((total, hidden_units), jnp.float32),
            jax.ShapeDtypeStruct((1, width), jnp.float32),
        ],
        compiler_params=pltpu.CompilerParams(vmem_limit_bytes=32 << 20),
        cost_estimate=light(),
    )(branch, inputs, stored, entry, cotangent, valid, gain, mixer_in, mixer_out)


def history_kernel(owners, count, place_ref, weights_ref, cotangent_ref, *back_refs):
    cols = back_refs[0].shape[2]
    spots = [
        (target_ref, layer)
        for target_ref in back_refs
        for layer in range(target_ref.shape[0])
    ]
    weights = weights_ref[...]
    for index in range(owners):
        spot = lane_block(place_ref, index, cols)
        upstream = [
            cotangent_ref[outer, :, spot].astype(jnp.float32)
            for outer in range(cotangent_ref.shape[0])
        ]
        for layer in range(count - 1):
            target_ref, near = spots[index * (count - 1) + layer]
            target_ref[near] = sum(
                weights[:, outer * count + layer : outer * count + layer + 1] * upstream[outer]
                for outer in range(len(upstream))
            ).astype(jnp.bfloat16)


def history_back(weights, cotangent, place, owners):
    outer, tokens, width = cotangent.shape
    total = weights.shape[1]
    count = total // outer
    cuts = []
    for index in feature_order(owners):
        cuts += [count - 2, 1] if index > 1 else [count - 1]
    tile = 128
    return pl.pallas_call(
        functools.partial(history_kernel, owners, count),
        grid_spec=pltpu.PrefetchScalarGridSpec(
            num_scalar_prefetch=1,
            grid=(tokens // tile,),
            in_specs=[
                pl.BlockSpec((tile, total), lambda i, place_ref: (i, 0)),
                pl.BlockSpec((outer, tile, width), lambda i, place_ref: (0, i, 0)),
            ],
            out_specs=[
                pl.BlockSpec((layers, tile, width // owners), lambda i, place_ref: (0, i, 0))
                for layers in cuts
            ],
        ),
        out_shape=[
            jax.ShapeDtypeStruct((layers, tokens, width // owners), jnp.bfloat16)
            for layers in cuts
        ],
        compiler_params=pltpu.CompilerParams(vmem_limit_bytes=20 << 20),
        cost_estimate=light(),
    )(place, weights, cotangent)


def next_kernel(owners, place_ref, weights_ref, newest_ref, *refs):
    stored_refs, next_ref = refs[:-1], refs[-1]
    cols = newest_ref.shape[1] // owners
    weights = weights_ref[...]
    count = len(stored_refs) + 1
    for index in range(owners):
        spot = slice(index * cols, (index + 1) * cols)
        layers = [stored_ref[:, spot].astype(jnp.float32) for stored_ref in stored_refs]
        layers.append(newest_ref[:, spot].astype(jnp.float32))
        for outer in range(next_ref.shape[0]):
            next_ref[outer, :, lane_block(place_ref, index, cols)] = sum(
                weights[:, outer * count + layer : outer * count + layer + 1] * layers[layer]
                for layer in range(count)
            ).astype(jnp.bfloat16)


def next_layer(weights, stored, newest, place, owners):
    tokens, width = newest.shape
    total = weights.shape[1]
    count = len(stored) + 1
    outer = total // count
    tile = 128
    return pl.pallas_call(
        functools.partial(next_kernel, owners),
        grid_spec=pltpu.PrefetchScalarGridSpec(
            num_scalar_prefetch=1,
            grid=(tokens // tile,),
            in_specs=[
                pl.BlockSpec((tile, total), lambda i, place_ref: (i, 0)),
            ]
            + [pl.BlockSpec((tile, width), lambda i, place_ref: (i, 0))] * count,
            out_specs=pl.BlockSpec((outer, tile, width), lambda i, place_ref: (0, i, 0)),
        ),
        out_shape=jax.ShapeDtypeStruct((outer, tokens, width), jnp.bfloat16),
        compiler_params=pltpu.CompilerParams(vmem_limit_bytes=24 << 20),
        cost_estimate=light(),
    )(place, weights, newest, *stored)


def sums_kernel(owners, place_ref, grads_ref, inputs_ref, sums_ref):
    cols = inputs_ref.shape[2] // owners
    values = inputs_ref[0].astype(jnp.float32)
    mean_vals = jnp.mean(values, axis=-1, keepdims=True)
    centred = values - mean_vals
    inverse = lax.rsqrt(jnp.mean(centred * centred, axis=-1, keepdims=True) + norm_epsilon)

    @pl.when(pl.program_id(1) == 0)
    def clear():
        sums_ref[...] = jnp.zeros_like(sums_ref)

    for index in range(owners):
        spot = lane_block(place_ref, index, cols)
        unit = (inputs_ref[0, :, spot].astype(jnp.float32) - mean_vals) * inverse
        grads = grads_ref[0, :, index * cols : (index + 1) * cols].astype(jnp.float32)
        near = slice(index * cols, (index + 1) * cols)
        sums_ref[0, 0:1, near] += jnp.sum(grads * unit, axis=0, keepdims=True)
        sums_ref[0, 1:2, near] += jnp.sum(grads, axis=0, keepdims=True)


def norm_sums(grads, layer_inputs, first, place, owners):
    count, tokens, width = grads.shape
    tile = 128
    return pl.pallas_call(
        functools.partial(sums_kernel, owners),
        grid_spec=pltpu.PrefetchScalarGridSpec(
            num_scalar_prefetch=1,
            grid=(count, tokens // tile),
            in_specs=[
                pl.BlockSpec((1, tile, width), lambda c, i, place_ref: (c, i, 0)),
                pl.BlockSpec((1, tile, width), lambda c, i, place_ref: (c + first, i, 0)),
            ],
            out_specs=pl.BlockSpec((1, 2, width), lambda c, i, place_ref: (c, 0, 0)),
        ),
        out_shape=jax.ShapeDtypeStruct((count, 2, width), jnp.float32),
        compiler_params=pltpu.CompilerParams(vmem_limit_bytes=12 << 20),
        cost_estimate=light(),
    )(place, grads, layer_inputs)


def back_kernel(owners, place_ref, grads_ref, inputs_ref, gain_ref, extra_ref, out_ref):
    cols = inputs_ref.shape[1] // owners
    values = inputs_ref[...].astype(jnp.float32)
    centred = values - jnp.mean(values, axis=-1, keepdims=True)
    inverse = lax.rsqrt(jnp.mean(centred * centred, axis=-1, keepdims=True) + norm_epsilon)
    back = norm_back(grads_ref[...], centred * inverse, inverse, gain_ref[...])
    if extra_ref is not None:
        back = back + extra_ref[...]
    for index in range(owners):
        spot = slice(index * cols, (index + 1) * cols)
        out_ref[:, lane_block(place_ref, index, cols)] = back[:, spot].astype(jnp.bfloat16)


def back_share(grads, inputs, gain, extra, place, owners):
    rows, width = grads.shape
    kernel = functools.partial(back_kernel, owners)
    if extra is None:
        kernel = lambda place_ref, grads_ref, inputs_ref, gain_ref, out_ref: back_kernel(
            owners, place_ref, grads_ref, inputs_ref, gain_ref, None, out_ref
        )
    whole = pl.BlockSpec((rows, width), lambda i, place_ref: (0, 0))
    given = [grads, inputs, gain] + ([] if extra is None else [extra])
    return pl.pallas_call(
        kernel,
        grid_spec=pltpu.PrefetchScalarGridSpec(
            num_scalar_prefetch=1,
            grid=(1,),
            in_specs=[whole, whole, pl.BlockSpec((1, width), lambda i, place_ref: (0, 0))]
            + ([] if extra is None else [whole]),
            out_specs=whole,
        ),
        out_shape=jax.ShapeDtypeStruct((rows, width), jnp.bfloat16),
        compiler_params=pltpu.CompilerParams(vmem_limit_bytes=12 << 20),
        cost_estimate=light(),
    )(place, *given)


def body(
    layer_inputs,
    history,
    seq_ids,
    norms_master,
    norms_first,
    norms_second,
    attend_in_master,
    attend_in_first,
    attend_in_second,
    attend_out_master,
    attend_out_first,
    attend_out_second,
    expand_master,
    expand_first,
    expand_second,
    project_master,
    project_first,
    project_second,
    mixer_in_master,
    mixer_in_first,
    mixer_in_second,
    mixer_out_master,
    mixer_out_first,
    mixer_out_second,
    next_cotangent,
    grad_entry,
):
    bf16_type = jnp.bfloat16
    float_type = jnp.float32
    tensor_size = lax.axis_size("tensor")
    owners = lax.axis_size("dp")
    me = lax.axis_index("dp")
    order = feature_order(owners)
    place = jnp.stack([me ^ index for index in order]).astype(jnp.int32)
    tokens_here, width = layer_inputs.shape[1:]
    share_rows = tokens_here // tensor_size
    share_start = share_index("tensor") * share_rows
    cols = norms_master.shape[1]
    mixers = mixer_out_master.shape[0]

    def own_rows(values, axis):
        return lax.dynamic_slice_in_dim(values, share_start, share_rows, axis)

    def reorder(values):
        return jnp.concatenate(
            [
                lax.dynamic_slice_in_dim(values, (me ^ index) * cols, cols, values.ndim - 1)
                for index in order
            ],
            axis=-1,
        )


    near, side_bits, far = stages_of("tensor")
    out_first = (near, side_bits, far)
    in_first = (side_bits, far, near)
    back_order = (far, side_bits, near)
    cross_order = (near, far, side_bits)

    early_rows = [
        jnp.concatenate(
            [
                lax.dynamic_slice_in_dim(
                    values, (me ^ index) * tokens_here + share_start, share_rows, 1
                )
                for values in (history, grad_entry[None])
            ],
            axis=0,
        )
        for index in order
    ]
    early_rows = [
        rows if index == 0 else swap(rows, "dp", index) for rows, index in zip(early_rows, order)
    ]
    norms_half = gather_half(norms_master.astype(bf16_type), "dp", 1)
    attend_low = jnp.concatenate(
        [attend_in_master.astype(bf16_type), attend_out_master.astype(bf16_type).T[None]], axis=0
    )
    norms_half, attend_low, early_rows, expand_late, mixer_in_late, mixer_out_late = sync(
        [norms_half, attend_low, early_rows, expand_master, mixer_in_master, mixer_out_master], []
    )

    attend_kept = gather_half(attend_low, "dp", 1)
    early = join_blocks(early_rows)
    stored_share = early[:-1]
    layer_count = stored_share.shape[0] + 1
    stored_most = Gather(stored_share[:-1], "tensor", back_order, 1)
    stored_last = Gather(stored_share[-1:], "tensor", cross_order, 1)
    stored_most.step(0)
    stored_last.step(0)
    expand_low = expand_late.astype(bf16_type)
    norms_given = swap(norms_half, "dp", 1)
    norm_vals = jnp.concatenate([norms_half, norms_given], axis=1).astype(float_type)
    normed_kept, normed_given = norm_forward(
        layer_inputs, norm_vals[0:4], norm_vals[4:8], place, owners
    )
    attend_kept, normed_kept, normed_given, expand_low, project_late = sync(
        [attend_kept, normed_kept, normed_given, expand_low, project_master],
        [stored_most, stored_last],
    )

    small = jnp.concatenate(
        [mixer_in_late.T, jnp.pad(mixer_out_late, ((0, 0), (0, cols - MIXH)))], axis=0
    ).astype(bf16_type)
    small_half = gather_half(small, "dp", 1)
    expand_kept = gather_half(expand_low, "dp", 0)
    attend_given = swap(attend_kept, "dp", 1)
    stored_most.step(1)
    proj_kept = jnp.einsum(
        "ctd,cde->cte", normed_kept[0:3], attend_kept[0:3], preferred_element_type=float_type
    )
    cosine, sine_table, unused = angles(seq_ids)
    half = ROT // 2
    tables = (
        jnp.concatenate([cosine, cosine, jnp.ones((tokens_here, HDIM - ROT), float_type)], 1),
        jnp.pad(-sine_table, ((0, 0), (0, HDIM - half))),
        jnp.pad(sine_table, ((0, 0), (half, HDIM - ROT))),
    )
    project_low = project_late.astype(bf16_type)
    (
        small_half,
        expand_kept,
        attend_given,
        proj_kept,
        project_low,
        tables,
        layer_late,
        cotangent_late,
    ) = sync(
        [
            small_half,
            expand_kept,
            attend_given,
            proj_kept,
            project_low,
            tables,
            layer_inputs,
            next_cotangent,
        ],
        [stored_most, stored_last],
    )

    small_whole = jnp.concatenate([small_half, swap(small_half, "dp", 1)], axis=1)
    mixer_in_low = small_whole[0:MIXH]
    out_rows = small_whole[MIXH:]
    mixer_out_low = jnp.zeros((owners, mixers, MIXH), bf16_type)
    for spot, index in enumerate(order):
        mixer_out_low = lax.dynamic_update_index_in_dim(
            mixer_out_low, out_rows[:, spot * cols : spot * cols + MIXH], me ^ index, 0
        )
    mixer_out_low = mixer_out_low.reshape(owners * mixers, MIXH)
    project_kept = gather_half(project_low, "dp", 1)
    expand_given = swap(expand_kept, "dp", 1)
    stored_last.step(1)
    stored_most.settle()
    stored_pair = [
        Gather(stored_most.values[index : index + 1], "tensor", back_order, 1)
        for index in range(layer_count - 2)
    ]
    for item in stored_pair:
        item.places = list(stored_most.places)
    for item in stored_pair[:1]:
        item.step(2)
    proj = proj_kept + jnp.einsum(
        "ctd,cde->cte", normed_given[0:3], attend_given[0:3], preferred_element_type=float_type
    )
    turned, heads_out = attend(proj, tables, seq_ids)
    upper_kept = jnp.dot(normed_kept[3], expand_kept, preferred_element_type=float_type)
    valid = (own_rows(seq_ids, 0) >= 0).astype(float_type)[:, None]
    input_share = reorder(own_rows(layer_late, 1))
    cotangent_share = reorder(own_rows(cotangent_late, 1))
    (
        mixer_in_low,
        mixer_out_low,
        project_kept,
        expand_given,
        turned,
        heads_out,
        upper_kept,
        input_share,
        cotangent_share,
    ) = sync(
        [
            mixer_in_low,
            mixer_out_low,
            project_kept,
            expand_given,
            turned,
            heads_out,
            upper_kept,
            input_share,
            cotangent_share,
        ],
        [stored_last] + stored_pair,
    )

    out_kept, out_given = attend_kept[3], attend_given[3]
    project_given = swap(project_kept, "dp", 1)
    upper = upper_kept + jnp.dot(normed_given[3], expand_given, preferred_element_type=float_type)
    phi, density = gelu_parts(upper)
    hidden = exact_gelu(upper).astype(bf16_type)
    slope = phi + upper * density
    branch_kept = Scatter(
        (
            contract_cols(heads_out, out_kept)
            + jnp.dot(hidden, project_kept, preferred_element_type=float_type)
        ).astype(bf16_type),
        "tensor",
        out_first,
    )
    branch_given = Scatter(
        (
            contract_cols(heads_out, out_given)
            + jnp.dot(hidden, project_given, preferred_element_type=float_type)
        ).astype(bf16_type),
        "tensor",
        in_first,
    )
    for stage in range(3):
        branch_kept.step(stage)
        branch_given.step(stage)
    branch = jnp.concatenate([branch_kept.result(), branch_given.result()], axis=-1)
    branch, slope = sync([branch, slope], [])

    newest, grad_newest, sent_kept, sent_given, grad_mixer_in, grad_mixer_out, mixer_gain = mix(
        branch,
        input_share[3],
        stored_share,
        early[-1],
        cotangent_share,
        valid,
        norm_vals[8:9],
        mixer_in_low,
        mixer_out_low,
    )
    grad_kept = Gather(sent_kept, "tensor", back_order)
    grad_given = Gather(sent_given, "tensor", cross_order)
    for stage in range(3):
        grad_kept.step(stage)
        grad_given.step(stage)
    grad_kept = grad_kept.result()
    received = grad_given.result()
    grad_given = received[:, 0 : width // 2]
    mix_low = received[:, width // 2 :]
    mix_total = 4 * layer_count
    mix_weights = mix_low[:, 0:mix_total].astype(float_type) + mix_low[
        :, mix_total : 2 * mix_total
    ].astype(float_type)
    newest_all = Gather(newest, "tensor", back_order)
    grad_kept, grad_given, mix_weights = sync(
        [grad_kept, grad_given, mix_weights], [newest_all, stored_last] + stored_pair
    )

    history_pieces = history_back(mix_weights, cotangent_late, place, owners)
    history_pieces = list(history_pieces)
    history_front, history_last = [], []
    for index in order:
        history_front.append(history_pieces.pop(0))
        history_last.append(history_pieces.pop(0) if index > 1 else None)

    def send_far(pieces, which):
        for spot in which:
            pieces[spot] = swap(pieces[spot], "dp", order[spot])

    far_spots = [spot for spot in range(owners) if order[spot] > 1]
    near_spots = [spot for spot in range(owners) if order[spot] == 1]
    first_far, last_far = far_spots[: len(far_spots) // 2], far_spots[len(far_spots) // 2 :]
    for item in stored_pair[1:]:
        item.step(2)
    stored_last.step(2)
    newest_all.step(0)
    grad_hidden = contract_cols(grad_kept, project_kept) + contract_cols(grad_given, project_given)
    grad_upper = (slope * grad_hidden).astype(bf16_type)
    grad_normed_ffn = jnp.concatenate(
        [
            contract_cols(grad_upper, expand_kept).astype(bf16_type),
            contract_cols(grad_upper, expand_given).astype(bf16_type),
        ],
        axis=-1,
    )
    grad_project = Reduce(*project_grads(hidden, grad_kept, grad_given), "dp", 1)
    (
        history_front,
        history_last,
        grad_normed_ffn,
        grad_upper,
        grad_kept,
        grad_given,
        out_kept,
        out_given,
    ) = sync(
        [
            history_front,
            history_last,
            grad_normed_ffn,
            grad_upper,
            grad_kept,
            grad_given,
            out_kept,
            out_given,
        ],
        [newest_all, stored_last, grad_project] + stored_pair,
    )

    summed = [None, None, None, Scatter(grad_normed_ffn, "tensor", in_first)]
    summed[3].step(0)
    newest_all.step(1)
    send_far(history_front, first_far)
    send_far(history_front, near_spots)
    grad_project.near()
    grad_heads = (
        jnp.dot(grad_kept, out_kept, preferred_element_type=float_type)
        + jnp.dot(grad_given, out_given, preferred_element_type=float_type)
    ).astype(bf16_type)
    grad_proj = attend_back(turned, grad_heads, tables, seq_ids)
    grad_normed_attend = [
        jnp.concatenate(
            [
                contract_cols(grad_proj[index], weights[index]).astype(bf16_type)
                for weights in (attend_kept, attend_given)
            ],
            axis=-1,
        )
        for index in range(3)
    ]
    grad_attend = Reduce(
        *attend_grads_call(normed_kept, normed_given, grad_proj, grad_kept, grad_given, heads_out),
        "dp",
        1,
    )
    grad_expand = Reduce(*expand_grads(normed_kept, normed_given, grad_upper), "dp", 0)
    grad_normed_attend, grad_normed_ffn, history_front, history_last, layer_late = sync(
        [grad_normed_attend, grad_normed_ffn, history_front, history_last, layer_late],
        [grad_attend, grad_expand, grad_project, newest_all, summed[3]] + stored_pair,
    )

    for index in range(3):
        summed[index] = Scatter(grad_normed_attend[index], "tensor", out_first)
    summed[0].step(0)
    summed[3].step(1)
    send_far(history_front, last_far)
    grad_attend.near()
    grad_expand.near()
    all_grads = list(enumerate(grad_normed_attend + [grad_normed_ffn]))
    sums = [
        norm_sums(grads[None], layer_late, index, place, owners)[0] for index, grads in all_grads[:2]
    ]
    grad_project.prepare()
    sums, all_grads[2:], history_front, history_last = sync(
        [sums, [grads for index, grads in all_grads[2:]], history_front, history_last],
        summed + [newest_all, grad_project, grad_attend, grad_expand],
    )

    sums = sums + [
        norm_sums(grads[None], layer_late, index + 2, place, owners)[0]
        for index, grads in enumerate(all_grads[2:])
    ]
    summed[1].step(0)
    summed[3].step(2)
    summed[0].step(1)
    grad_project.far()
    sums, history_front, history_last = sync(
        [sums, history_front, history_last], summed + [grad_project, grad_expand, grad_attend]
    )

    def back(index):
        return Gather(
            back_share(
                summed[index].result(),
                input_share[index],
                norm_vals[index][None],
                grad_newest if index == 3 else None,
                place,
                owners,
            ),
            "tensor",
            back_order,
        )

    gathered = [None, None, None, back(3)]
    summed[2].step(0)
    summed[1].step(1)
    step_both(summed[0], 2, gathered[3], 0)
    norm_pack = jnp.stack(sums)
    own_rows_out = jnp.stack(
        [
            lax.dynamic_index_in_dim(
                grad_mixer_out.reshape(owners, mixers * MIXH), me ^ index, 0, False
            )
            for index in order
        ]
    )
    pack = Halves(
        jnp.concatenate(
            [
                norm_pack[:, 0],
                norm_pack[:, 1],
                mixer_gain,
                grad_mixer_in,
                jnp.pad(own_rows_out, ((0, 0), (0, cols - mixers * MIXH))).reshape(1, width),
            ],
            axis=0,
        ),
        "dp",
    )
    send_far(history_last, far_spots)
    grad_expand.prepare()
    project_squares, history_last = sync(
        [grad_project.squares(), history_last],
        summed[0:3] + [gathered[3], grad_expand, grad_project, grad_attend, newest_all, pack],
    )

    gathered[0] = back(0)
    newest_all.step(2)
    step_both(summed[2], 1, gathered[3], 1)
    step_both(summed[1], 2, gathered[0], 0)
    grad_expand.far()
    grad_attend.prepare()
    pack.near()
    pack.far()
    grad_inputs = jnp.zeros(
        (4,) + (2,) * len(bits_of(tensor_size)) + (share_rows, width), bf16_type
    )
    grad_history = jnp.zeros(history.shape, bf16_type)
    for spot, index in enumerate(order):
        first_row = (me ^ index) * tokens_here
        for pieces, layer in ((history_front, 0), (history_last, layer_count - 2)):
            if pieces[spot] is not None:
                grad_history = lax.dynamic_update_slice(
                    grad_history, pieces[spot], (layer, first_row, 0)
                )
    grad_history, grad_inputs = sync(
        [grad_history, grad_inputs],
        summed[1:3] + [gathered[0], gathered[3], newest_all, grad_attend, grad_expand, pack],
    )

    gathered[1] = back(1)
    gathered[3].step(2)
    step_both(summed[2], 2, gathered[1], 0)
    gathered[0].step(1)
    grad_attend.far()
    pack.rows("tensor", near)
    newest_whole = newest_all.result()
    newest_stored = [item.result()[0] for item in stored_pair] + [stored_last.result()[0]]
    next_inputs = next_layer(mix_weights, newest_stored, newest_whole, place, owners)
    expand_squares, newest_whole, next_inputs = sync(
        [grad_expand.squares(), newest_whole, next_inputs],
        [summed[2], gathered[0], gathered[1], gathered[3], grad_attend, pack],
    )

    gathered[2] = back(2)
    gathered[0].step(2)
    gathered[2].step(0)
    gathered[1].step(1)
    pack.rows("tensor", side_bits)
    pack.rows("tensor", far)
    entry_pieces = [newest_whole[:, spot * cols : (spot + 1) * cols] for spot in range(owners)]
    send_far(entry_pieces, first_far)
    grad_inputs = gathered[3].place_last(grad_inputs, 3)
    shard_squares = project_squares + expand_squares + grad_attend.squares()
    shard_squares, entry_pieces, grad_inputs = sync(
        [shard_squares, entry_pieces, grad_inputs],
        [gathered[0], gathered[1], gathered[2], pack],
    )

    own_pack = pack.values
    norm_grad = own_pack[0:9]
    grad_mixer_in = own_pack[9 : 9 + MIXH].T
    grad_mixer_out = own_pack[9 + MIXH, 0 : mixers * MIXH].reshape(mixers, MIXH)
    shared_squares = (
        square_sum(norm_grad) + square_sum(grad_mixer_in) + square_sum(grad_mixer_out)
    )
    total_squares = jnp.full((1, 128), shard_squares + shared_squares / tensor_size)
    for axis, bits in (
        ("dp", bits_of(owners)[:1]),
        ("tensor", side_bits + far),
        ("dp", bits_of(owners)[1:]),
        ("tensor", near),
    ):
        for bit in bits:
            total_squares = total_squares + swap(total_squares, axis, bit)
    gathered[1].step(2)
    gathered[2].step(1)
    send_far(entry_pieces, last_far)
    send_far(entry_pieces, near_spots)
    grad_inputs = gathered[0].place_last(grad_inputs, 0)
    total_squares, entry_pieces, grad_inputs = sync(
        [total_squares, entry_pieces, grad_inputs], [gathered[1], gathered[2]]
    )
    total_squares = total_squares[0, 0]

    gathered[2].step(2)
    grad_norm = jnp.sqrt(total_squares)
    factor = jnp.minimum(1.0, clip_level / grad_norm)
    wide_rate = 2.0 / math.sqrt(D)
    wide = (wide_rate, weight_decay)
    norms_out = adam_step(norms_master, norms_first, norms_second, norm_grad, factor, 1.0, 0.0)
    mixer_in_out = adam_step(
        mixer_in_master,
        mixer_in_first,
        mixer_in_second,
        grad_mixer_in,
        factor,
        wide_rate,
        weight_decay,
    )
    mixer_out_out = adam_step(
        mixer_out_master,
        mixer_out_first,
        mixer_out_second,
        grad_mixer_out,
        factor,
        2.0 / math.sqrt(MIXH),
        weight_decay,
    )
    parts = attend_in_master.shape[0]
    attend_in_out = adam_step(
        attend_in_master,
        attend_in_first,
        attend_in_second,
        grad_attend.own()[0:parts],
        factor,
        wide_rate,
        weight_decay,
    )
    attend_out_out = adam_call(
        grad_attend.terms,
        attend_out_master,
        attend_out_first,
        attend_out_second,
        factor,
        wide,
        (1, 1),
        attend_out_master.shape,
        parts,
    )
    expand_out = adam_step(
        expand_master,
        expand_first,
        expand_second,
        grad_expand.own(),
        factor,
        wide_rate,
        weight_decay,
    )
    project_out = adam_step(
        project_master,
        project_first,
        project_second,
        grad_project.own(),
        factor,
        2.0 / math.sqrt(FF),
        weight_decay,
    )
    new_entry = jnp.zeros(grad_entry.shape, bf16_type)
    for spot, index in enumerate(order):
        first_row = (me ^ index) * tokens_here
        new_entry = lax.dynamic_update_slice_in_dim(new_entry, entry_pieces[spot], first_row, 0)
    for index in (1, 2):
        grad_inputs = gathered[index].place_last(grad_inputs, index)
    grad_inputs = grad_inputs.reshape(layer_inputs.shape)
    return (
        next_inputs,
        new_entry,
        grad_inputs,
        grad_history,
        norms_out[0],
        norms_out[1],
        norms_out[2],
        attend_in_out[0],
        attend_in_out[1],
        attend_in_out[2],
        attend_in_out[0].astype(bf16_type),
        attend_out_out[0],
        attend_out_out[1],
        attend_out_out[2],
        attend_out_out[3],
        expand_out[0],
        expand_out[1],
        expand_out[2],
        expand_out[0].astype(bf16_type),
        project_out[0],
        project_out[1],
        project_out[2],
        project_out[0].astype(bf16_type),
        mixer_in_out[0],
        mixer_in_out[1],
        mixer_in_out[2],
        mixer_in_out[0].astype(bf16_type),
        mixer_out_out[0],
        mixer_out_out[1],
        mixer_out_out[2],
        mixer_out_out[0].astype(bf16_type),
        grad_norm,
    )


def solution(mesh):
    in_specs = (
        P(None, "dp", None),
        P(None, None, "dp"),
        P("dp"),
        P(None, "dp"),
        P(None, "dp"),
        P(None, "dp"),
        P(None, "dp", "tensor"),
        P(None, "dp", "tensor"),
        P(None, "dp", "tensor"),
        P("tensor", "dp"),
        P("tensor", "dp"),
        P("tensor", "dp"),
        P("dp", "tensor"),
        P("dp", "tensor"),
        P("dp", "tensor"),
        P("tensor", "dp"),
        P("tensor", "dp"),
        P("tensor", "dp"),
        P("dp", None),
        P("dp", None),
        P("dp", None),
        P("dp", None),
        P("dp", None),
        P("dp", None),
        P(None, "dp", None),
        P(None, "dp"),
    )
    out_specs = (
        P(None, "dp", None),
        P(None, "dp"),
        P(None, "dp", None),
        P(None, None, "dp"),
        P(None, "dp"),
        P(None, "dp"),
        P(None, "dp"),
        P(None, "dp", "tensor"),
        P(None, "dp", "tensor"),
        P(None, "dp", "tensor"),
        P(None, "dp", "tensor"),
        P("tensor", "dp"),
        P("tensor", "dp"),
        P("tensor", "dp"),
        P("tensor", "dp"),
        P("dp", "tensor"),
        P("dp", "tensor"),
        P("dp", "tensor"),
        P("dp", "tensor"),
        P("tensor", "dp"),
        P("tensor", "dp"),
        P("tensor", "dp"),
        P("tensor", "dp"),
        P("dp", None),
        P("dp", None),
        P("dp", None),
        P("dp", None),
        P("dp", None),
        P("dp", None),
        P("dp", None),
        P("dp", None),
        P(),
    )
    return jax.shard_map(body, mesh=mesh, in_specs=in_specs, out_specs=out_specs, check_vma=False)
```

```python
import functools
import math

import jax
import jax.numpy as jnp
from jax import lax
from jax.experimental import pallas as pl
from jax.experimental.pallas import tpu as pltpu
from jax.sharding import PartitionSpec as P

D = 2048
HDIM = 128
FF = 8192
MIXH = 36
ROT = 32
STEP = 10


norm_epsilon = 1e-05
mixer_epsilon = 1e-06
clip_level = 1.0
beta_first = 0.9
beta_second = 0.95
adam_epsilon = 1e-08
weight_decay = 0.1


def exact_gelu(values):
    return jax.nn.gelu(values, approximate=False)


def gelu_grad(values, upstream):
    unused, pullback = jax.vjp(exact_gelu, values)
    return pullback(upstream)[0]


def rotate(vectors, cosine, sine_table):
    half = ROT // 2
    first_half = vectors[..., :half]
    second_half = vectors[..., half:ROT]
    return jnp.concatenate(
        [
            first_half * cosine - second_half * sine_table,
            second_half * cosine + first_half * sine_table,
            vectors[..., ROT:],
        ],
        axis=-1,
    )


def angles(bucket_ids):
    same_seq = bucket_ids[:, None] == bucket_ids[None, :]
    order = jnp.arange(bucket_ids.shape[0])
    earlier = order[None, :] < order[:, None]
    position = jnp.sum(jnp.where(same_seq & earlier, 1, 0), axis=1).astype(jnp.float32)
    freqs = 10000.0 ** (-2.0 * jnp.arange(ROT // 2).astype(jnp.float32) / ROT)
    angle = position[:, None] * freqs[None, :]
    allowed = same_seq & (order[None, :] <= order[:, None])
    return (jnp.cos(angle), jnp.sin(angle), allowed)


def score_block(query, key_rows, allowed):
    head_scale = HDIM ** (-0.5)
    scores = (
        jnp.einsum("hqd,hkd->hqk", query, key_rows, preferred_element_type=jnp.float32) * head_scale
    )
    return jnp.where(allowed[None], scores, -1e30)


def norm_back(grad_rows, unit_rows, inverse_rows, gain_rows):
    scaled = grad_rows * gain_rows
    mean_scaled = jnp.mean(scaled, axis=-1, keepdims=True)
    mean_cross = jnp.mean(scaled * unit_rows, axis=-1, keepdims=True)
    return inverse_rows * (scaled - mean_scaled - unit_rows * mean_cross)


def contract_rows(left, right):
    return lax.dot_general(
        left, right, (((0,), (0,)), ((), ())), preferred_element_type=jnp.float32
    )


def contract_cols(left, right):
    return lax.dot_general(
        left, right, (((1,), (1,)), ((), ())), preferred_element_type=jnp.float32
    )


def adam_step(master, first_moment, second_moment, gradient, factor, step_rate, decay_rate):
    scaled = gradient * factor
    first_new = beta_first * first_moment + (1.0 - beta_first) * scaled
    second_new = beta_second * second_moment + (1.0 - beta_second) * scaled * scaled
    first_hat = first_new / (1.0 - beta_first**STEP)
    second_hat = second_new / (1.0 - beta_second**STEP)
    master_new = master - step_rate * (
        first_hat / (jnp.sqrt(second_hat) + adam_epsilon) + decay_rate * master
    )
    return (master_new, first_new, second_new)


def gelu_parts(values):
    upper_share = 0.5 * (1.0 + lax.erf(values * math.sqrt(0.5)))
    density = jnp.exp(-0.5 * values * values) * (1.0 / math.sqrt(2.0 * math.pi))
    return upper_share, density


def bits_of(size):
    return [1 << index for index in range(size.bit_length() - 1)]


def feature_order(owners):
    order = [0]
    for bit in reversed(bits_of(owners)):
        order = order + [index | bit for index in order]
    return order


def swap(values, axis, mask):
    size = lax.axis_size(axis)
    return lax.ppermute(values, axis, [(source, source ^ mask) for source in range(size)])


def sync(plain, steps):
    held = [vars(item) for item in steps]
    names = [
        [name for name in ("values", "terms", "given", "moved") if item.get(name) is not None]
        for item in held
    ]
    plain, inner = lax.optimization_barrier(
        (
            list(plain),
            [[item[name] for name in kinds] for item, kinds in zip(held, names)],
        )
    )
    for item, kinds, values in zip(steps, names, inner):
        for name, value in zip(kinds, values):
            setattr(item, name, value)
    return plain


def gather_half(piece, axis, dim):
    for bit in reversed(bits_of(lax.axis_size(axis))[1:]):
        piece = jnp.concatenate([piece, swap(piece, axis, bit)], axis=dim)
    return piece


def halve(values, dim):
    half = values.shape[dim] // 2
    return (
        lax.slice_in_dim(values, 0, half, axis=dim),
        lax.slice_in_dim(values, half, 2 * half, axis=dim),
    )


class Reduce:
    def __init__(self, kept, given, axis, dim):
        self.terms, self.given, self.axis, self.dim = [kept], given, axis, dim

    def near(self):
        self.terms.append(swap(self.given, self.axis, 1))
        self.given = None

    def prepare(self):
        half = self.terms[-1].shape[self.dim] // 2
        self.given = sum(
            lax.slice_in_dim(term, half, 2 * half, axis=self.dim).astype(jnp.float32)
            for term in self.terms
        ).astype(jnp.bfloat16)

    def far(self):
        for bit in bits_of(lax.axis_size(self.axis))[1:]:
            if self.given is None:
                self.prepare()
            self.terms.append(swap(self.given, self.axis, bit))
            self.given = None

    def own(self):
        own = self.terms[-1].shape[self.dim]
        return sum(
            lax.slice_in_dim(term, 0, own, axis=self.dim).astype(jnp.float32)
            for term in self.terms
        )

    def squares(self):
        return square_sum(self.own())


class Halves:
    def __init__(self, values, axis):
        self.values, self.axis = values, axis

    def hop(self, bit):
        kept, given = halve(self.values, 1)
        self.values = kept + swap(given, self.axis, bit)

    def near(self):
        self.hop(1)

    def far(self):
        for bit in bits_of(lax.axis_size(self.axis))[1:]:
            self.hop(bit)

    def rows(self, axis, bits):
        for bit in bits:
            self.values = self.values + swap(self.values, axis, bit)


def step_both(scatter, stage, gather, gather_stage):
    for bit in scatter.order[stage]:
        given = scatter.split(bit)
        gather.settle()
        moved = swap(jnp.stack([given, gather.values]), scatter.axis, bit)
        scatter.moved, gather.moved, gather.bit = moved[0], moved[1], bit


def square_sum(values):
    return jnp.sum(values * values)


def share_index(axis):
    here = lax.axis_index(axis)
    place = 0
    for bit in bits_of(lax.axis_size(axis)):
        place = place * 2 + (here & bit) // bit
    return place


def unfold_rows(values, axis, dim):
    count = len(bits_of(lax.axis_size(axis)))
    shape = values.shape
    return values.reshape(
        shape[:dim] + (2,) * count + (shape[dim] >> count,) + shape[dim + 1 :]
    )


def fold_rows(values, axis, dim):
    count = len(bits_of(lax.axis_size(axis)))
    shape = values.shape
    return values.reshape(shape[:dim] + (-1,) + shape[dim + count + 1 :])


class Scatter:
    def __init__(self, values, axis, order):
        self.values, self.axis, self.order = unfold_rows(values, axis, 0), axis, list(order)
        self.places = bits_of(lax.axis_size(axis))
        self.moved = None

    def split(self, bit):
        self.settle()
        dim = self.places.index(bit)
        self.places = [place for place in self.places if place != bit]
        side = (lax.axis_index(self.axis) & bit) // bit
        given = lax.dynamic_index_in_dim(self.values, 1 - side, dim, False)
        self.values = lax.dynamic_index_in_dim(self.values, side, dim, False)
        return given

    def settle(self):
        if self.moved is not None:
            values = self.values.astype(jnp.float32) + self.moved.astype(jnp.float32)
            self.values = values.astype(jnp.bfloat16) if self.places else values
            self.moved = None

    def step(self, stage):
        for bit in self.order[stage]:
            self.moved = swap(self.split(bit), self.axis, bit)

    def result(self):
        self.settle()
        return self.values


class Gather:
    def __init__(self, values, axis, order, dim=0):
        self.values, self.axis, self.order, self.dim = values, axis, list(order), dim
        self.places, self.moved, self.bit = [], None, None

    def step(self, stage):
        for bit in self.order[stage]:
            self.settle()
            self.moved, self.bit = swap(self.values, self.axis, bit), bit

    def settle(self):
        if self.moved is None:
            return
        known = self.places + [self.bit]
        self.places = [place for place in bits_of(lax.axis_size(self.axis)) if place in known]
        dim = self.dim + self.places.index(self.bit)
        side = (lax.axis_index(self.axis) & self.bit) // self.bit
        shape = list(self.moved.shape)
        shape.insert(dim, 2)
        self.values = jnp.where(
            lax.broadcasted_iota(jnp.int32, shape, dim) == side,
            jnp.expand_dims(self.values, dim),
            jnp.expand_dims(self.moved, dim),
        )
        self.moved = None

    def place_new(self, count, index):
        spot = bits_of(lax.axis_size(self.axis)).index(self.bit)
        side = (lax.axis_index(self.axis) & self.bit) // self.bit
        whole = place_first(self.values, self.moved, side, spot, count, index)
        shape = self.values.shape[:spot] + (2,) + self.values.shape[spot:]
        return whole.reshape((count,) + shape)

    def place_last(self, whole, index):
        spot = bits_of(lax.axis_size(self.axis)).index(self.bit)
        side = (lax.axis_index(self.axis) & self.bit) // self.bit
        for values, at in ((self.values, side), (self.moved, 1 - side)):
            block = jnp.expand_dims(values, spot)[None]
            starts = [0] * block.ndim
            starts[0], starts[spot + 1] = index, at
            whole = lax.dynamic_update_slice(whole, block, starts)
        return whole

    def result(self):
        self.settle()
        return fold_rows(self.values, self.axis, self.dim)


def stages_of(axis):
    bits = bits_of(lax.axis_size(axis))
    near = len(bits) - 2
    return bits[:near], bits[near : near + 1], bits[near + 1 :]


def light():
    return pl.CostEstimate(flops=1, bytes_accessed=1, transcendentals=0)


def join_kernel(*refs):
    out_ref = refs[-1]
    cols = refs[0].shape[-1]
    for index, ref in enumerate(refs[:-1]):
        out_ref[:, :, index * cols : (index + 1) * cols] = ref[...]


def join_blocks(blocks):
    shape = blocks[0].shape
    return pl.pallas_call(
        join_kernel,
        out_shape=jax.ShapeDtypeStruct(
            shape[:-1] + (shape[-1] * len(blocks),), blocks[0].dtype
        ),
        cost_estimate=light(),
    )(*blocks)


def place_kernel(side_ref, values_ref, moved_ref, out_ref):
    @pl.when(pl.program_id(1) == 0)
    def own():
        out_ref[0, 0, 0] = values_ref[0]

    @pl.when(pl.program_id(1) == 1)
    def other():
        out_ref[0, 0, 0] = moved_ref[0]


def place_first(values, moved, side, spot, count, index):
    front = 2**spot
    rows, width = values.size // values.shape[-1] // front, values.shape[-1]
    part = pl.BlockSpec((1, rows, width), lambda a, g, side_ref: (a, 0, 0))
    return pl.pallas_call(
        place_kernel,
        grid_spec=pltpu.PrefetchScalarGridSpec(
            num_scalar_prefetch=1,
            grid=(front, 2),
            in_specs=[part, part],
            out_specs=pl.BlockSpec(
                (1, 1, 1, rows, width),
                lambda a, g, side_ref: (index, a, (side_ref[0] + g) % 2, 0, 0),
            ),
        ),
        out_shape=jax.ShapeDtypeStruct((count, front, 2, rows, width), values.dtype),
        compiler_params=pltpu.CompilerParams(vmem_limit_bytes=12 << 20),
        cost_estimate=light(),
    )(
        side.reshape(1).astype(jnp.int32),
        values.reshape(front, rows, width),
        moved.reshape(front, rows, width),
    )


def outer_kernel(pairs, *refs):
    for left, right, target in pairs:
        left_ref, right_ref = refs[left], refs[right]
        value = contract_rows(left_ref[...].reshape(left_ref.shape[-2:]), right_ref[...])
        refs[target][...] = value.astype(jnp.bfloat16)


def outer_call(operands, specs, pairs, grid, out_rows, out_cols, tile):
    out = pl.BlockSpec((tile, out_cols), lambda i: (i, 0))
    shape = jax.ShapeDtypeStruct((out_rows, out_cols), jnp.bfloat16)
    return pl.pallas_call(
        functools.partial(outer_kernel, pairs),
        grid=grid,
        in_specs=specs,
        out_specs=[out, out],
        out_shape=[shape, shape],
        compiler_params=pltpu.CompilerParams(vmem_limit_bytes=16 << 20),
        cost_estimate=light(),
    )(*operands)


def project_grads(hidden, kept, given):
    tokens, units = hidden.shape
    tile = 256
    whole = pl.BlockSpec(kept.shape, lambda i: (0, 0))
    return outer_call(
        (hidden, kept, given),
        [pl.BlockSpec((tokens, tile), lambda i: (0, i)), whole, whole],
        ((0, 1, 3), (0, 2, 4)),
        (units // tile,),
        units,
        kept.shape[1],
        tile,
    )


def expand_grads(kept, given, upper):
    count, tokens, width = kept.shape
    tile = 256
    part = pl.BlockSpec((1, tokens, tile), lambda i: (count - 1, 0, i))
    return outer_call(
        (kept, given, upper),
        [part, part, pl.BlockSpec(upper.shape, lambda i: (0, 0))],
        ((0, 2, 3), (1, 2, 4)),
        (width // tile,),
        width,
        upper.shape[1],
        tile,
    )


def attend_grads_kernel(
    kept_ref, given_ref, back_ref, out_kept_ref, out_given_ref, heads_ref, *outs
):
    last = pl.program_id(0) == pl.num_programs(0) - 1
    for left_ref, other_ref, target_ref in (
        (kept_ref, out_kept_ref, outs[0]),
        (given_ref, out_given_ref, outs[1]),
    ):

        @pl.when(jnp.logical_not(last))
        def inner(left_ref=left_ref, target_ref=target_ref):
            target_ref[0] = contract_rows(left_ref[0], back_ref[0]).astype(jnp.bfloat16)

        @pl.when(last)
        def outer(other_ref=other_ref, target_ref=target_ref):
            target_ref[0] = contract_rows(other_ref[...], heads_ref[...]).astype(jnp.bfloat16)


def attend_grads_call(kept, given, back, out_kept, out_given, heads):
    count, tokens, width = kept.shape
    units = heads.shape[1]
    part = pl.BlockSpec((1, tokens, width), lambda c: (jnp.minimum(c, count - 2), 0, 0))
    whole = pl.BlockSpec((tokens, width), lambda c: (0, 0))
    out = pl.BlockSpec((1, width, units), lambda c: (c, 0, 0))
    shape = jax.ShapeDtypeStruct((count, width, units), jnp.bfloat16)
    return pl.pallas_call(
        attend_grads_kernel,
        grid=(count,),
        in_specs=[
            part,
            part,
            pl.BlockSpec((1, tokens, units), lambda c: (jnp.minimum(c, count - 2), 0, 0)),
            whole,
            whole,
            pl.BlockSpec((tokens, units), lambda c: (0, 0)),
        ],
        out_specs=[out, out],
        out_shape=[shape, shape],
        compiler_params=pltpu.CompilerParams(vmem_limit_bytes=20 << 20),
        cost_estimate=light(),
    )(kept, given, back, out_kept, out_given, heads)


def adam_kernel(rates, count, flip, factor_ref, *refs):
    term_refs, (master_ref, first_ref, second_ref) = refs[:count], refs[count : count + 3]
    new_ref, first_new_ref, second_new_ref, copy_ref = refs[count + 3 :]
    gradient = sum(term_ref[...].astype(jnp.float32) for term_ref in term_refs)
    if flip:
        gradient = gradient[0].T
    master_new, first_new, second_new = adam_step(
        master_ref[...], first_ref[...], second_ref[...], gradient, factor_ref[0], *rates
    )
    new_ref[...] = master_new
    first_new_ref[...] = first_new
    second_new_ref[...] = second_new
    copy_ref[...] = master_new.astype(jnp.bfloat16)


def adam_call(terms, master, first_moment, second_moment, factor, rates, grid, block, spot):
    flip = spot is not None
    own = pl.BlockSpec(block, lambda *steps: steps[: len(grid)])
    if flip:
        term_specs = [
            pl.BlockSpec((1,) + master.shape[::-1], lambda *steps: (spot, 0, 0)) for term in terms
        ]
    else:
        term_specs = [own] * len(terms)
    wide = jax.ShapeDtypeStruct(master.shape, jnp.float32)
    return pl.pallas_call(
        functools.partial(adam_kernel, rates, len(terms), flip),
        grid=grid,
        in_specs=[pl.BlockSpec(memory_space=pltpu.SMEM)] + term_specs + [own] * 3,
        out_specs=[own] * 4,
        out_shape=[wide, wide, wide, jax.ShapeDtypeStruct(master.shape, jnp.bfloat16)],
        compiler_params=pltpu.CompilerParams(vmem_limit_bytes=20 << 20),
        cost_estimate=light(),
    )(factor.reshape(1), *terms, master, first_moment, second_moment)


def lane_block(place_ref, index, cols):
    return pl.ds(pl.multiple_of(place_ref[index] * cols, cols), cols)


def norm_kernel(owners, place_ref, inputs_ref, gains_ref, biases_ref, kept_ref, given_ref):
    cols = inputs_ref.shape[2] // owners
    values = inputs_ref[0].astype(jnp.float32)
    mean_vals = jnp.mean(values, axis=-1, keepdims=True)
    centred = values - mean_vals
    inverse = lax.rsqrt(jnp.mean(centred * centred, axis=-1, keepdims=True) + norm_epsilon)
    for index in range(owners):
        block = inputs_ref[0, :, lane_block(place_ref, index, cols)].astype(jnp.float32)
        spot = slice(index * cols, (index + 1) * cols)
        normed = (block - mean_vals) * inverse * gains_ref[0, :, spot] + biases_ref[0, :, spot]
        target = kept_ref if index < owners // 2 else given_ref
        near = index % (owners // 2)
        target[0, :, near * cols : (near + 1) * cols] = normed.astype(jnp.bfloat16)


def norm_forward(layer_inputs, gains, biases, place, owners):
    count, tokens, width = layer_inputs.shape
    tile = 128
    half = pl.BlockSpec((1, tile, width // 2), lambda c, i, place_ref: (c, i, 0))
    row = pl.BlockSpec((1, 1, width), lambda c, i, place_ref: (c, 0, 0))
    shape = jax.ShapeDtypeStruct((count, tokens, width // 2), jnp.bfloat16)
    return pl.pallas_call(
        functools.partial(norm_kernel, owners),
        grid_spec=pltpu.PrefetchScalarGridSpec(
            num_scalar_prefetch=1,
            grid=(count, tokens // tile),
            in_specs=[
                pl.BlockSpec((1, tile, width), lambda c, i, place_ref: (c, i, 0)),
                row,
                row,
            ],
            out_specs=[half, half],
        ),
        out_shape=[shape, shape],
        compiler_params=pltpu.CompilerParams(vmem_limit_bytes=14 << 20),
        cost_estimate=light(),
    )(place, layer_inputs, gains[:, None, :], biases[:, None, :])


def turn(values, cosine, sine_low, sine_high):
    width = values.shape[-1]
    return (
        values * cosine
        + pltpu.roll(values, width - ROT // 2, 1) * sine_low
        + pltpu.roll(values, ROT // 2, 1) * sine_high
    )


def masked_probs(query, key_rows, ids_col, ids_row):
    tokens = query.shape[0]
    scores = lax.dot_general(
        query, key_rows, (((1,), (1,)), ((), ())), preferred_element_type=jnp.float32
    ) * (HDIM ** (-0.5))
    here = lax.broadcasted_iota(jnp.int32, (tokens, tokens), 0)
    there = lax.broadcasted_iota(jnp.int32, (tokens, tokens), 1)
    scores = jnp.where((ids_col == ids_row) & (there <= here), scores, -1e30)
    row_max = jnp.max(scores, axis=-1, keepdims=True)
    log_total = jnp.log(jnp.sum(jnp.exp(scores - row_max), axis=-1, keepdims=True)) + row_max
    return jnp.exp(scores - log_total)


def attend_kernel(proj_ref, cos_ref, low_ref, high_ref, col_ref, row_ref, turned_ref, heads_ref):
    tables = (cos_ref[...], low_ref[...], high_ref[...])
    query = turn(proj_ref[0], *tables).astype(jnp.bfloat16)
    key_rows = turn(proj_ref[1], *tables).astype(jnp.bfloat16)
    value_rows = proj_ref[2].astype(jnp.bfloat16)
    turned_ref[0] = query
    turned_ref[1] = key_rows
    turned_ref[2] = value_rows
    prob = masked_probs(query, key_rows, col_ref[...], row_ref[...]).astype(jnp.bfloat16)
    heads_ref[...] = jnp.dot(prob, value_rows, preferred_element_type=jnp.float32).astype(
        jnp.bfloat16
    )


def attend_back_kernel(
    turned_ref, grads_ref, cos_ref, low_ref, high_ref, col_ref, row_ref, back_ref
):
    query, key_rows, value_rows = turned_ref[0], turned_ref[1], turned_ref[2]
    grads = grads_ref[...]
    prob = masked_probs(query, key_rows, col_ref[...], row_ref[...])
    grad_prob = contract_cols(grads, value_rows)
    row_delta = jnp.sum(prob * grad_prob, axis=-1, keepdims=True)
    grad_scores = (prob * (grad_prob - row_delta)).astype(jnp.bfloat16)
    tables = (cos_ref[...], -low_ref[...], -high_ref[...])
    head_scale = HDIM ** (-0.5)
    grad_query = jnp.dot(grad_scores, key_rows, preferred_element_type=jnp.float32) * head_scale
    grad_key = contract_rows(grad_scores, query) * head_scale
    back_ref[0] = turn(grad_query, *tables).astype(jnp.bfloat16)
    back_ref[1] = turn(grad_key, *tables).astype(jnp.bfloat16)
    back_ref[2] = contract_rows(prob.astype(jnp.bfloat16), grads).astype(jnp.bfloat16)


def attend_specs(tokens):
    table = pl.BlockSpec((tokens, HDIM), lambda head: (0, 0))
    heads = pl.BlockSpec((tokens, HDIM), lambda head: (0, head))
    triple = pl.BlockSpec((3, tokens, HDIM), lambda head: (0, 0, head))
    shared = [
        table,
        table,
        table,
        pl.BlockSpec((tokens, 1), lambda head: (0, 0)),
        pl.BlockSpec((1, tokens), lambda head: (0, 0)),
    ]
    return heads, triple, shared


def attend(proj, tables, ids):
    tokens, width = proj.shape[1:]
    heads, triple, shared = attend_specs(tokens)
    return pl.pallas_call(
        attend_kernel,
        grid=(width // HDIM,),
        in_specs=[triple] + shared,
        out_specs=[triple, heads],
        out_shape=[
            jax.ShapeDtypeStruct((3, tokens, width), jnp.bfloat16),
            jax.ShapeDtypeStruct((tokens, width), jnp.bfloat16),
        ],
        compiler_params=pltpu.CompilerParams(vmem_limit_bytes=16 << 20),
        cost_estimate=light(),
    )(proj, *tables, ids[:, None], ids[None, :])


def attend_back(turned, grads, tables, ids):
    tokens, width = grads.shape
    heads, triple, shared = attend_specs(tokens)
    return pl.pallas_call(
        attend_back_kernel,
        grid=(width // HDIM,),
        in_specs=[triple, heads] + shared,
        out_specs=triple,
        out_shape=jax.ShapeDtypeStruct((3, tokens, width), jnp.bfloat16),
        compiler_params=pltpu.CompilerParams(vmem_limit_bytes=20 << 20),
        cost_estimate=light(),
    )(turned, grads, *tables, ids[:, None], ids[None, :])


def mix_kernel(
    branch_ref,
    inputs_ref,
    stored_ref,
    entry_ref,
    cotangent_ref,
    valid_ref,
    gain_ref,
    mixer_in_ref,
    mixer_out_ref,
    newest_ref,
    grad_newest_ref,
    sent_kept_ref,
    sent_given_ref,
    mixer_in_grad_ref,
    mixer_out_grad_ref,
    gain_grad_ref,
):
    valid = valid_ref[...]
    gain = gain_ref[...]
    newest = inputs_ref[...].astype(jnp.float32) + valid * branch_ref[...]
    newest_ref[...] = newest.astype(jnp.bfloat16)
    rows, width = newest.shape
    scale = lax.rsqrt(jnp.mean(newest * newest, axis=-1, keepdims=True) + mixer_epsilon)
    normed = (newest * scale * gain).astype(jnp.bfloat16)
    mix_pre = contract_cols(normed, mixer_in_ref[...])
    phi, density = gelu_parts(mix_pre)
    mix_act = (mix_pre * phi).astype(jnp.bfloat16)
    weights = contract_cols(mix_act, mixer_out_ref[...])
    count = stored_ref.shape[0] + 1
    total = weights.shape[1]
    lane = lax.broadcasted_iota(jnp.int32, (rows, total), 1)
    grad_weights = jnp.zeros((rows, total), jnp.float32)
    newest_back = jnp.zeros((rows, width), jnp.float32)
    for outer in range(total // count):
        upstream = cotangent_ref[outer].astype(jnp.float32)
        for inner in range(count):
            layer = newest if inner == count - 1 else stored_ref[inner].astype(jnp.float32)
            dots = jnp.sum(upstream * layer, axis=-1, keepdims=True)
            grad_weights = jnp.where(lane == outer * count + inner, dots, grad_weights)
        last = outer * count + count - 1
        newest_back = newest_back + weights[:, last : last + 1] * upstream
    grad_weights = grad_weights.astype(jnp.bfloat16)
    mixer_out_grad_ref[...] = contract_rows(grad_weights, mix_act)
    grad_act = jnp.dot(grad_weights, mixer_out_ref[...], preferred_element_type=jnp.float32)
    grad_pre = ((phi + mix_pre * density) * grad_act).astype(jnp.bfloat16)
    mixer_in_grad_ref[...] = contract_rows(grad_pre, normed)
    grad_normed = jnp.dot(grad_pre, mixer_in_ref[...], preferred_element_type=jnp.float32)
    gain_grad_ref[...] = jnp.sum(grad_normed * newest * scale, axis=0, keepdims=True)
    scaled = grad_normed * gain
    grad_newest = (
        newest_back
        + entry_ref[...].astype(jnp.float32)
        + scale * scaled
        - newest * (scale * scale * scale) * jnp.mean(scaled * newest, axis=-1, keepdims=True)
    )
    grad_newest_ref[...] = grad_newest
    sent = (valid * grad_newest).astype(jnp.bfloat16)
    sent_kept_ref[...] = sent[:, 0 : width // 2]
    sent_given_ref[:, 0 : width // 2] = sent[:, width // 2 :]
    high = weights.astype(jnp.bfloat16)
    rest = (weights - high.astype(jnp.float32)).astype(jnp.bfloat16)
    blank = jnp.zeros((rows, 128 - 2 * total), jnp.bfloat16)
    sent_given_ref[:, width // 2 :] = jnp.concatenate([high, rest, blank], axis=1)


def mix(branch, inputs, stored, entry, cotangent, valid, gain, mixer_in, mixer_out):
    rows, width = branch.shape
    hidden_units = mixer_in.shape[0]
    total = mixer_out.shape[0]
    return pl.pallas_call(
        mix_kernel,
        out_shape=[
            jax.ShapeDtypeStruct((rows, width), jnp.bfloat16),
            jax.ShapeDtypeStruct((rows, width), jnp.float32),
            jax.ShapeDtypeStruct((rows, width // 2), jnp.bfloat16),
            jax.ShapeDtypeStruct((rows, width // 2 + 128), jnp.bfloat16),
            jax.ShapeDtypeStruct((hidden_units, width), jnp.float32),
            jax.ShapeDtypeStruct((total, hidden_units), jnp.float32),
            jax.ShapeDtypeStruct((1, width), jnp.float32),
        ],
        compiler_params=pltpu.CompilerParams(vmem_limit_bytes=32 << 20),
        cost_estimate=light(),
    )(branch, inputs, stored, entry, cotangent, valid, gain, mixer_in, mixer_out)


def history_kernel(owners, count, place_ref, weights_ref, cotangent_ref, *back_refs):
    cols = back_refs[0].shape[2]
    spots = [
        (target_ref, layer)
        for target_ref in back_refs
        for layer in range(target_ref.shape[0])
    ]
    weights = weights_ref[...]
    for index in range(owners):
        spot = lane_block(place_ref, index, cols)
        upstream = [
            cotangent_ref[outer, :, spot].astype(jnp.float32)
            for outer in range(cotangent_ref.shape[0])
        ]
        for layer in range(count - 1):
            target_ref, near = spots[index * (count - 1) + layer]
            target_ref[near] = sum(
                weights[:, outer * count + layer : outer * count + layer + 1] * upstream[outer]
                for outer in range(len(upstream))
            ).astype(jnp.bfloat16)


def history_back(weights, cotangent, place, owners):
    outer, tokens, width = cotangent.shape
    total = weights.shape[1]
    count = total // outer
    cuts = []
    for index in feature_order(owners):
        cuts += [count - 2, 1] if index > 1 else [count - 1]
    tile = 128
    return pl.pallas_call(
        functools.partial(history_kernel, owners, count),
        grid_spec=pltpu.PrefetchScalarGridSpec(
            num_scalar_prefetch=1,
            grid=(tokens // tile,),
            in_specs=[
                pl.BlockSpec((tile, total), lambda i, place_ref: (i, 0)),
                pl.BlockSpec((outer, tile, width), lambda i, place_ref: (0, i, 0)),
            ],
            out_specs=[
                pl.BlockSpec((layers, tile, width // owners), lambda i, place_ref: (0, i, 0))
                for layers in cuts
            ],
        ),
        out_shape=[
            jax.ShapeDtypeStruct((layers, tokens, width // owners), jnp.bfloat16)
            for layers in cuts
        ],
        compiler_params=pltpu.CompilerParams(vmem_limit_bytes=20 << 20),
        cost_estimate=light(),
    )(place, weights, cotangent)


def next_kernel(owners, place_ref, weights_ref, newest_ref, *refs):
    stored_refs, next_ref = refs[:-1], refs[-1]
    cols = newest_ref.shape[1] // owners
    weights = weights_ref[...]
    count = len(stored_refs) + 1
    for index in range(owners):
        spot = slice(index * cols, (index + 1) * cols)
        layers = [stored_ref[:, spot].astype(jnp.float32) for stored_ref in stored_refs]
        layers.append(newest_ref[:, spot].astype(jnp.float32))
        for outer in range(next_ref.shape[0]):
            next_ref[outer, :, lane_block(place_ref, index, cols)] = sum(
                weights[:, outer * count + layer : outer * count + layer + 1] * layers[layer]
                for layer in range(count)
            ).astype(jnp.bfloat16)


def next_layer(weights, stored, newest, place, owners):
    tokens, width = newest.shape
    total = weights.shape[1]
    count = len(stored) + 1
    outer = total // count
    tile = 128
    return pl.pallas_call(
        functools.partial(next_kernel, owners),
        grid_spec=pltpu.PrefetchScalarGridSpec(
            num_scalar_prefetch=1,
            grid=(tokens // tile,),
            in_specs=[
                pl.BlockSpec((tile, total), lambda i, place_ref: (i, 0)),
            ]
            + [pl.BlockSpec((tile, width), lambda i, place_ref: (i, 0))] * count,
            out_specs=pl.BlockSpec((outer, tile, width), lambda i, place_ref: (0, i, 0)),
        ),
        out_shape=jax.ShapeDtypeStruct((outer, tokens, width), jnp.bfloat16),
        compiler_params=pltpu.CompilerParams(vmem_limit_bytes=24 << 20),
        cost_estimate=light(),
    )(place, weights, newest, *stored)


def sums_kernel(owners, place_ref, grads_ref, inputs_ref, sums_ref):
    cols = inputs_ref.shape[2] // owners
    values = inputs_ref[0].astype(jnp.float32)
    mean_vals = jnp.mean(values, axis=-1, keepdims=True)
    centred = values - mean_vals
    inverse = lax.rsqrt(jnp.mean(centred * centred, axis=-1, keepdims=True) + norm_epsilon)

    @pl.when(pl.program_id(1) == 0)
    def clear():
        sums_ref[...] = jnp.zeros_like(sums_ref)

    for index in range(owners):
        spot = lane_block(place_ref, index, cols)
        unit = (inputs_ref[0, :, spot].astype(jnp.float32) - mean_vals) * inverse
        grads = grads_ref[0, :, index * cols : (index + 1) * cols].astype(jnp.float32)
        near = slice(index * cols, (index + 1) * cols)
        sums_ref[0, 0:1, near] += jnp.sum(grads * unit, axis=0, keepdims=True)
        sums_ref[0, 1:2, near] += jnp.sum(grads, axis=0, keepdims=True)


def norm_sums(grads, layer_inputs, first, place, owners):
    count, tokens, width = grads.shape
    tile = 128
    return pl.pallas_call(
        functools.partial(sums_kernel, owners),
        grid_spec=pltpu.PrefetchScalarGridSpec(
            num_scalar_prefetch=1,
            grid=(count, tokens // tile),
            in_specs=[
                pl.BlockSpec((1, tile, width), lambda c, i, place_ref: (c, i, 0)),
                pl.BlockSpec((1, tile, width), lambda c, i, place_ref: (c + first, i, 0)),
            ],
            out_specs=pl.BlockSpec((1, 2, width), lambda c, i, place_ref: (c, 0, 0)),
        ),
        out_shape=jax.ShapeDtypeStruct((count, 2, width), jnp.float32),
        compiler_params=pltpu.CompilerParams(vmem_limit_bytes=12 << 20),
        cost_estimate=light(),
    )(place, grads, layer_inputs)


def back_kernel(
    owners, place_ref, grads_ref, moved_ref, inputs_ref, gain_ref, extra_ref, out_ref
):
    cols = inputs_ref.shape[1] // owners
    values = inputs_ref[...].astype(jnp.float32)
    centred = values - jnp.mean(values, axis=-1, keepdims=True)
    inverse = lax.rsqrt(jnp.mean(centred * centred, axis=-1, keepdims=True) + norm_epsilon)
    grads = grads_ref[...].astype(jnp.float32) + moved_ref[...].astype(jnp.float32)
    back = norm_back(grads, centred * inverse, inverse, gain_ref[...])
    if extra_ref is not None:
        back = back + extra_ref[...]
    for index in range(owners):
        spot = slice(index * cols, (index + 1) * cols)
        out_ref[:, lane_block(place_ref, index, cols)] = back[:, spot].astype(jnp.bfloat16)


def back_share(grads, moved, inputs, gain, extra, place, owners):
    rows, width = grads.shape
    kernel = functools.partial(back_kernel, owners)
    if extra is None:
        kernel = lambda place_ref, grads_ref, moved_ref, inputs_ref, gain_ref, out_ref: back_kernel(
            owners, place_ref, grads_ref, moved_ref, inputs_ref, gain_ref, None, out_ref
        )
    whole = pl.BlockSpec((rows, width), lambda i, place_ref: (0, 0))
    given = [grads, moved, inputs, gain] + ([] if extra is None else [extra])
    return pl.pallas_call(
        kernel,
        grid_spec=pltpu.PrefetchScalarGridSpec(
            num_scalar_prefetch=1,
            grid=(1,),
            in_specs=[whole, whole, whole, pl.BlockSpec((1, width), lambda i, place_ref: (0, 0))]
            + ([] if extra is None else [whole]),
            out_specs=whole,
        ),
        out_shape=jax.ShapeDtypeStruct((rows, width), jnp.bfloat16),
        compiler_params=pltpu.CompilerParams(vmem_limit_bytes=12 << 20),
        cost_estimate=light(),
    )(place, *given)


def body(
    layer_inputs,
    history,
    seq_ids,
    norms_master,
    norms_first,
    norms_second,
    attend_in_master,
    attend_in_first,
    attend_in_second,
    attend_out_master,
    attend_out_first,
    attend_out_second,
    expand_master,
    expand_first,
    expand_second,
    project_master,
    project_first,
    project_second,
    mixer_in_master,
    mixer_in_first,
    mixer_in_second,
    mixer_out_master,
    mixer_out_first,
    mixer_out_second,
    next_cotangent,
    grad_entry,
):
    bf16_type = jnp.bfloat16
    float_type = jnp.float32
    tensor_size = lax.axis_size("tensor")
    owners = lax.axis_size("dp")
    me = lax.axis_index("dp")
    order = feature_order(owners)
    place = jnp.stack([me ^ index for index in order]).astype(jnp.int32)
    tokens_here, width = layer_inputs.shape[1:]
    share_rows = tokens_here // tensor_size
    share_start = share_index("tensor") * share_rows
    cols = norms_master.shape[1]
    mixers = mixer_out_master.shape[0]

    def own_rows(values, axis):
        return lax.dynamic_slice_in_dim(values, share_start, share_rows, axis)

    def reorder(values):
        return jnp.concatenate(
            [
                lax.dynamic_slice_in_dim(values, (me ^ index) * cols, cols, values.ndim - 1)
                for index in order
            ],
            axis=-1,
        )


    near, side_bits, far = stages_of("tensor")
    out_first = (near, side_bits, far)
    in_first = (side_bits, far, near)
    back_order = (far, side_bits, near)
    cross_order = (near, far, side_bits)

    early_rows = [
        jnp.concatenate(
            [
                lax.dynamic_slice_in_dim(
                    values, (me ^ index) * tokens_here + share_start, share_rows, 1
                )
                for values in (history, grad_entry[None])
            ],
            axis=0,
        )
        for index in order
    ]
    early_rows = [
        rows if index == 0 else swap(rows, "dp", index) for rows, index in zip(early_rows, order)
    ]
    norms_half = gather_half(norms_master.astype(bf16_type), "dp", 1)
    attend_low = jnp.concatenate(
        [attend_in_master.astype(bf16_type), attend_out_master.astype(bf16_type).T[None]], axis=0
    )
    norms_half, attend_low, early_rows, expand_late, mixer_in_late, mixer_out_late = sync(
        [norms_half, attend_low, early_rows, expand_master, mixer_in_master, mixer_out_master], []
    )

    attend_kept = gather_half(attend_low, "dp", 1)
    early = join_blocks(early_rows)
    stored_share = early[:-1]
    layer_count = stored_share.shape[0] + 1
    stored_most = Gather(stored_share[:-1], "tensor", back_order, 1)
    stored_last = Gather(stored_share[-1:], "tensor", cross_order, 1)
    stored_most.step(0)
    stored_last.step(0)
    expand_low = expand_late.astype(bf16_type)
    norms_given = swap(norms_half, "dp", 1)
    norm_vals = jnp.concatenate([norms_half, norms_given], axis=1).astype(float_type)
    normed_kept, normed_given = norm_forward(
        layer_inputs, norm_vals[0:4], norm_vals[4:8], place, owners
    )
    attend_kept, normed_kept, normed_given, expand_low, project_late = sync(
        [attend_kept, normed_kept, normed_given, expand_low, project_master],
        [stored_most, stored_last],
    )

    small = jnp.concatenate(
        [mixer_in_late.T, jnp.pad(mixer_out_late, ((0, 0), (0, cols - MIXH)))], axis=0
    ).astype(bf16_type)
    small_half = gather_half(small, "dp", 1)
    expand_kept = gather_half(expand_low, "dp", 0)
    attend_given = swap(attend_kept, "dp", 1)
    stored_most.step(1)
    proj_kept = jnp.einsum(
        "ctd,cde->cte", normed_kept[0:3], attend_kept[0:3], preferred_element_type=float_type
    )
    cosine, sine_table, unused = angles(seq_ids)
    half = ROT // 2
    tables = (
        jnp.concatenate([cosine, cosine, jnp.ones((tokens_here, HDIM - ROT), float_type)], 1),
        jnp.pad(-sine_table, ((0, 0), (0, HDIM - half))),
        jnp.pad(sine_table, ((0, 0), (half, HDIM - ROT))),
    )
    project_low = project_late.astype(bf16_type)
    (
        small_half,
        expand_kept,
        attend_given,
        proj_kept,
        project_low,
        tables,
        layer_late,
        cotangent_late,
    ) = sync(
        [
            small_half,
            expand_kept,
            attend_given,
            proj_kept,
            project_low,
            tables,
            layer_inputs,
            next_cotangent,
        ],
        [stored_most, stored_last],
    )

    small_whole = jnp.concatenate([small_half, swap(small_half, "dp", 1)], axis=1)
    mixer_in_low = small_whole[0:MIXH]
    out_rows = small_whole[MIXH:]
    mixer_out_low = jnp.zeros((owners, mixers, MIXH), bf16_type)
    for spot, index in enumerate(order):
        mixer_out_low = lax.dynamic_update_index_in_dim(
            mixer_out_low, out_rows[:, spot * cols : spot * cols + MIXH], me ^ index, 0
        )
    mixer_out_low = mixer_out_low.reshape(owners * mixers, MIXH)
    project_kept = gather_half(project_low, "dp", 1)
    expand_given = swap(expand_kept, "dp", 1)
    stored_last.step(1)
    stored_most.settle()
    stored_pair = [
        Gather(stored_most.values[index : index + 1], "tensor", back_order, 1)
        for index in range(layer_count - 2)
    ]
    for item in stored_pair:
        item.places = list(stored_most.places)
    for item in stored_pair[:1]:
        item.step(2)
    proj = proj_kept + jnp.einsum(
        "ctd,cde->cte", normed_given[0:3], attend_given[0:3], preferred_element_type=float_type
    )
    turned, heads_out = attend(proj, tables, seq_ids)
    upper_kept = jnp.dot(normed_kept[3], expand_kept, preferred_element_type=float_type)
    valid = (own_rows(seq_ids, 0) >= 0).astype(float_type)[:, None]
    input_share = reorder(own_rows(layer_late, 1))
    cotangent_share = reorder(own_rows(cotangent_late, 1))
    (
        mixer_in_low,
        mixer_out_low,
        project_kept,
        expand_given,
        turned,
        heads_out,
        upper_kept,
        input_share,
        cotangent_share,
    ) = sync(
        [
            mixer_in_low,
            mixer_out_low,
            project_kept,
            expand_given,
            turned,
            heads_out,
            upper_kept,
            input_share,
            cotangent_share,
        ],
        [stored_last] + stored_pair,
    )

    out_kept, out_given = attend_kept[3], attend_given[3]
    project_given = swap(project_kept, "dp", 1)
    upper = upper_kept + jnp.dot(normed_given[3], expand_given, preferred_element_type=float_type)
    phi, density = gelu_parts(upper)
    hidden = exact_gelu(upper).astype(bf16_type)
    slope = phi + upper * density
    branch_kept = Scatter(
        (
            contract_cols(heads_out, out_kept)
            + jnp.dot(hidden, project_kept, preferred_element_type=float_type)
        ).astype(bf16_type),
        "tensor",
        out_first,
    )
    branch_given = Scatter(
        (
            contract_cols(heads_out, out_given)
            + jnp.dot(hidden, project_given, preferred_element_type=float_type)
        ).astype(bf16_type),
        "tensor",
        in_first,
    )
    for stage in range(3):
        branch_kept.step(stage)
        branch_given.step(stage)
    branch = jnp.concatenate([branch_kept.result(), branch_given.result()], axis=-1)
    branch, slope = sync([branch, slope], [])

    newest, grad_newest, sent_kept, sent_given, grad_mixer_in, grad_mixer_out, mixer_gain = mix(
        branch,
        input_share[3],
        stored_share,
        early[-1],
        cotangent_share,
        valid,
        norm_vals[8:9],
        mixer_in_low,
        mixer_out_low,
    )
    grad_kept = Gather(sent_kept, "tensor", back_order)
    grad_given = Gather(sent_given, "tensor", cross_order)
    for stage in range(3):
        grad_kept.step(stage)
        grad_given.step(stage)
    grad_kept = grad_kept.result()
    received = grad_given.result()
    grad_given = received[:, 0 : width // 2]
    mix_low = received[:, width // 2 :]
    mix_total = 4 * layer_count
    mix_weights = mix_low[:, 0:mix_total].astype(float_type) + mix_low[
        :, mix_total : 2 * mix_total
    ].astype(float_type)
    newest_all = Gather(newest, "tensor", back_order)
    grad_kept, grad_given, mix_weights = sync(
        [grad_kept, grad_given, mix_weights], [newest_all, stored_last] + stored_pair
    )

    history_pieces = history_back(mix_weights, cotangent_late, place, owners)
    history_pieces = list(history_pieces)
    history_front, history_last = [], []
    for index in order:
        history_front.append(history_pieces.pop(0))
        history_last.append(history_pieces.pop(0) if index > 1 else None)

    def send_far(pieces, which):
        for spot in which:
            pieces[spot] = swap(pieces[spot], "dp", order[spot])

    far_spots = [spot for spot in range(owners) if order[spot] > 1]
    near_spots = [spot for spot in range(owners) if order[spot] == 1]
    first_far, last_far = far_spots[: len(far_spots) // 2], far_spots[len(far_spots) // 2 :]
    for item in stored_pair[1:]:
        item.step(2)
    stored_last.step(2)
    newest_all.step(0)
    grad_hidden = contract_cols(grad_kept, project_kept) + contract_cols(grad_given, project_given)
    grad_upper = (slope * grad_hidden).astype(bf16_type)
    grad_normed_ffn = jnp.concatenate(
        [
            contract_cols(grad_upper, expand_kept).astype(bf16_type),
            contract_cols(grad_upper, expand_given).astype(bf16_type),
        ],
        axis=-1,
    )
    grad_project = Reduce(*project_grads(hidden, grad_kept, grad_given), "dp", 1)
    (
        history_front,
        history_last,
        grad_normed_ffn,
        grad_upper,
        grad_kept,
        grad_given,
        out_kept,
        out_given,
    ) = sync(
        [
            history_front,
            history_last,
            grad_normed_ffn,
            grad_upper,
            grad_kept,
            grad_given,
            out_kept,
            out_given,
        ],
        [newest_all, stored_last, grad_project] + stored_pair,
    )

    summed = [None, None, None, Scatter(grad_normed_ffn, "tensor", in_first)]
    summed[3].step(0)
    send_far(history_front, first_far)
    send_far(history_front, near_spots)
    grad_project.near()
    grad_heads = (
        jnp.dot(grad_kept, out_kept, preferred_element_type=float_type)
        + jnp.dot(grad_given, out_given, preferred_element_type=float_type)
    ).astype(bf16_type)
    grad_proj = attend_back(turned, grad_heads, tables, seq_ids)
    grad_normed_attend = [
        jnp.concatenate(
            [
                contract_cols(grad_proj[index], weights[index]).astype(bf16_type)
                for weights in (attend_kept, attend_given)
            ],
            axis=-1,
        )
        for index in range(3)
    ]
    grad_proj_late, upper_late, near_pieces = sync(
        [grad_proj, grad_upper, [history_front[spot] for spot in near_spots]], []
    )
    for spot, piece in zip(near_spots, near_pieces):
        history_front[spot] = piece
    grad_attend = Reduce(
        *attend_grads_call(normed_kept, normed_given, grad_proj_late, grad_kept, grad_given, heads_out),
        "dp",
        1,
    )
    grad_expand = Reduce(*expand_grads(normed_kept, normed_given, upper_late), "dp", 0)
    grad_normed_attend, grad_normed_ffn, history_front, history_last, layer_late = sync(
        [grad_normed_attend, grad_normed_ffn, history_front, history_last, layer_late],
        [grad_attend, grad_expand, grad_project, newest_all, summed[3]] + stored_pair,
    )

    for index in range(3):
        summed[index] = Scatter(grad_normed_attend[index], "tensor", out_first)
    summed[0].step(0)
    summed[3].step(1)
    send_far(history_front, last_far)
    grad_expand.near()
    newest_all.step(1)
    (layer_late,) = sync([layer_late], [grad_expand])
    all_grads = list(enumerate(grad_normed_attend + [grad_normed_ffn]))
    sums = [
        norm_sums(grads[None], layer_late, index, place, owners)[0] for index, grads in all_grads[:2]
    ]
    grad_project.prepare()
    sums, all_grads[2:], history_front, history_last = sync(
        [sums, [grads for index, grads in all_grads[2:]], history_front, history_last],
        summed + [newest_all, grad_project, grad_attend, grad_expand],
    )

    sums = sums + [
        norm_sums(grads[None], layer_late, index + 2, place, owners)[0]
        for index, grads in enumerate(all_grads[2:])
    ]
    summed[1].step(0)
    summed[3].step(2)
    summed[0].step(1)
    grad_project.far()
    grad_attend.near()
    sums, history_front, history_last = sync(
        [sums, history_front, history_last], summed + [grad_project, grad_expand, grad_attend]
    )

    def back(index):
        return Gather(
            back_share(
                summed[index].values,
                summed[index].moved,
                input_share[index],
                norm_vals[index][None],
                grad_newest if index == 3 else None,
                place,
                owners,
            ),
            "tensor",
            back_order,
        )

    gathered = [None, None, None, back(3)]
    summed[2].step(0)
    summed[1].step(1)
    step_both(summed[0], 2, gathered[3], 0)
    norm_pack = jnp.stack(sums)
    own_rows_out = jnp.stack(
        [
            lax.dynamic_index_in_dim(
                grad_mixer_out.reshape(owners, mixers * MIXH), me ^ index, 0, False
            )
            for index in order
        ]
    )
    pack = Halves(
        jnp.concatenate(
            [
                norm_pack[:, 0],
                norm_pack[:, 1],
                mixer_gain,
                grad_mixer_in,
                jnp.pad(own_rows_out, ((0, 0), (0, cols - mixers * MIXH))).reshape(1, width),
            ],
            axis=0,
        ),
        "dp",
    )
    send_far(history_last, far_spots)
    grad_expand.prepare()
    project_squares, history_last = sync(
        [grad_project.squares(), history_last],
        summed[0:3] + [gathered[3], grad_expand, grad_project, grad_attend, newest_all, pack],
    )

    gathered[0] = back(0)
    newest_all.step(2)
    step_both(summed[2], 1, gathered[3], 1)
    step_both(summed[1], 2, gathered[0], 0)
    grad_expand.far()
    grad_attend.prepare()
    pack.near()
    pack.far()
    grad_history = jnp.zeros(history.shape, bf16_type)
    for spot, index in enumerate(order):
        first_row = (me ^ index) * tokens_here
        for pieces, layer in ((history_front, 0), (history_last, layer_count - 2)):
            if pieces[spot] is not None:
                grad_history = lax.dynamic_update_slice(
                    grad_history, pieces[spot], (layer, first_row, 0)
                )
    (grad_history,) = sync(
        [grad_history],
        summed[1:3] + [gathered[0], gathered[3], newest_all, grad_attend, grad_expand, pack],
    )

    gathered[1] = back(1)
    gathered[3].step(2)
    step_both(summed[2], 2, gathered[1], 0)
    gathered[0].step(1)
    grad_attend.far()
    pack.rows("tensor", near)
    newest_whole = newest_all.result()
    newest_stored = [item.result()[0] for item in stored_pair] + [stored_last.result()[0]]
    next_inputs = next_layer(mix_weights, newest_stored, newest_whole, place, owners)
    expand_squares, newest_whole, next_inputs = sync(
        [grad_expand.squares(), newest_whole, next_inputs],
        [summed[2], gathered[0], gathered[1], gathered[3], grad_attend, pack],
    )

    gathered[2] = back(2)
    gathered[0].step(2)
    gathered[2].step(0)
    gathered[1].step(1)
    pack.rows("tensor", side_bits)
    pack.rows("tensor", far)
    entry_pieces = [newest_whole[:, spot * cols : (spot + 1) * cols] for spot in range(owners)]
    send_far(entry_pieces, first_far)
    grad_inputs = gathered[3].place_new(4, 3)
    shard_squares = project_squares + expand_squares + grad_attend.squares()
    shard_squares, entry_pieces, grad_inputs = sync(
        [shard_squares, entry_pieces, grad_inputs],
        [gathered[0], gathered[1], gathered[2], pack],
    )

    own_pack = pack.values
    norm_grad = own_pack[0:9]
    grad_mixer_in = own_pack[9 : 9 + MIXH].T
    grad_mixer_out = own_pack[9 + MIXH, 0 : mixers * MIXH].reshape(mixers, MIXH)
    shared_squares = (
        square_sum(norm_grad) + square_sum(grad_mixer_in) + square_sum(grad_mixer_out)
    )
    total_squares = jnp.full((1, 128), shard_squares + shared_squares / tensor_size)
    for axis, bits in (("dp", bits_of(owners)[:1]), ("tensor", side_bits + far)):
        for bit in bits:
            total_squares = total_squares + swap(total_squares, axis, bit)
    (total_squares,) = sync([total_squares], [gathered[2]])
    for axis, bits in (("dp", bits_of(owners)[1:]), ("tensor", near)):
        for bit in bits:
            total_squares = total_squares + swap(total_squares, axis, bit)
    gathered[1].step(2)
    gathered[2].step(1)
    send_far(entry_pieces, last_far)
    send_far(entry_pieces, near_spots)
    grad_inputs = gathered[0].place_last(grad_inputs, 0)
    new_entry = jnp.zeros(grad_entry.shape, bf16_type)
    entry_late = last_far + near_spots
    for spot in range(owners):
        if spot not in entry_late:
            first_row = (me ^ order[spot]) * tokens_here
            new_entry = lax.dynamic_update_slice_in_dim(
                new_entry, entry_pieces[spot], first_row, 0
            )
    total_squares, entry_pieces, grad_inputs, new_entry = sync(
        [total_squares, entry_pieces, grad_inputs, new_entry], [gathered[1], gathered[2]]
    )
    total_squares = total_squares[0, 0]

    gathered[2].step(2)
    grad_norm = jnp.sqrt(total_squares)
    factor = jnp.minimum(1.0, clip_level / grad_norm)
    wide_rate = 2.0 / math.sqrt(D)
    wide = (wide_rate, weight_decay)
    norms_out = adam_step(norms_master, norms_first, norms_second, norm_grad, factor, 1.0, 0.0)
    mixer_in_out = adam_step(
        mixer_in_master,
        mixer_in_first,
        mixer_in_second,
        grad_mixer_in,
        factor,
        wide_rate,
        weight_decay,
    )
    mixer_out_out = adam_step(
        mixer_out_master,
        mixer_out_first,
        mixer_out_second,
        grad_mixer_out,
        factor,
        2.0 / math.sqrt(MIXH),
        weight_decay,
    )
    parts = attend_in_master.shape[0]
    attend_in_out = adam_step(
        attend_in_master,
        attend_in_first,
        attend_in_second,
        grad_attend.own()[0:parts],
        factor,
        wide_rate,
        weight_decay,
    )
    attend_out_out = adam_call(
        grad_attend.terms,
        attend_out_master,
        attend_out_first,
        attend_out_second,
        factor,
        wide,
        (1, 1),
        attend_out_master.shape,
        parts,
    )
    expand_out = adam_step(
        expand_master,
        expand_first,
        expand_second,
        grad_expand.own(),
        factor,
        wide_rate,
        weight_decay,
    )
    project_out = adam_step(
        project_master,
        project_first,
        project_second,
        grad_project.own(),
        factor,
        2.0 / math.sqrt(FF),
        weight_decay,
    )
    for spot in entry_late:
        first_row = (me ^ order[spot]) * tokens_here
        new_entry = lax.dynamic_update_slice_in_dim(new_entry, entry_pieces[spot], first_row, 0)
    for index in (1, 2):
        grad_inputs = gathered[index].place_last(grad_inputs, index)
    grad_inputs = grad_inputs.reshape(layer_inputs.shape)
    return (
        next_inputs,
        new_entry,
        grad_inputs,
        grad_history,
        norms_out[0],
        norms_out[1],
        norms_out[2],
        attend_in_out[0],
        attend_in_out[1],
        attend_in_out[2],
        attend_in_out[0].astype(bf16_type),
        attend_out_out[0],
        attend_out_out[1],
        attend_out_out[2],
        attend_out_out[3],
        expand_out[0],
        expand_out[1],
        expand_out[2],
        expand_out[0].astype(bf16_type),
        project_out[0],
        project_out[1],
        project_out[2],
        project_out[0].astype(bf16_type),
        mixer_in_out[0],
        mixer_in_out[1],
        mixer_in_out[2],
        mixer_in_out[0].astype(bf16_type),
        mixer_out_out[0],
        mixer_out_out[1],
        mixer_out_out[2],
        mixer_out_out[0].astype(bf16_type),
        grad_norm,
    )


def solution(mesh):
    in_specs = (
        P(None, "dp", None),
        P(None, None, "dp"),
        P("dp"),
        P(None, "dp"),
        P(None, "dp"),
        P(None, "dp"),
        P(None, "dp", "tensor"),
        P(None, "dp", "tensor"),
        P(None, "dp", "tensor"),
        P("tensor", "dp"),
        P("tensor", "dp"),
        P("tensor", "dp"),
        P("dp", "tensor"),
        P("dp", "tensor"),
        P("dp", "tensor"),
        P("tensor", "dp"),
        P("tensor", "dp"),
        P("tensor", "dp"),
        P("dp", None),
        P("dp", None),
        P("dp", None),
        P("dp", None),
        P("dp", None),
        P("dp", None),
        P(None, "dp", None),
        P(None, "dp"),
    )
    out_specs = (
        P(None, "dp", None),
        P(None, "dp"),
        P(None, "dp", None),
        P(None, None, "dp"),
        P(None, "dp"),
        P(None, "dp"),
        P(None, "dp"),
        P(None, "dp", "tensor"),
        P(None, "dp", "tensor"),
        P(None, "dp", "tensor"),
        P(None, "dp", "tensor"),
        P("tensor", "dp"),
        P("tensor", "dp"),
        P("tensor", "dp"),
        P("tensor", "dp"),
        P("dp", "tensor"),
        P("dp", "tensor"),
        P("dp", "tensor"),
        P("dp", "tensor"),
        P("tensor", "dp"),
        P("tensor", "dp"),
        P("tensor", "dp"),
        P("tensor", "dp"),
        P("dp", None),
        P("dp", None),
        P("dp", None),
        P("dp", None),
        P("dp", None),
        P("dp", None),
        P("dp", None),
        P("dp", None),
        P(),
    )
    return jax.shard_map(body, mesh=mesh, in_specs=in_specs, out_specs=out_specs, check_vma=False)
```

```python
import functools
import math

import jax
import jax.numpy as jnp
from jax import lax
from jax.experimental import pallas as pl
from jax.experimental.pallas import tpu as pltpu
from jax.sharding import PartitionSpec as P

D = 2048
HDIM = 128
FF = 8192
MIXH = 36
ROT = 32
STEP = 10


norm_epsilon = 1e-05
mixer_epsilon = 1e-06
clip_level = 1.0
beta_first = 0.9
beta_second = 0.95
adam_epsilon = 1e-08
weight_decay = 0.1


def exact_gelu(values):
    return jax.nn.gelu(values, approximate=False)


def gelu_grad(values, upstream):
    unused, pullback = jax.vjp(exact_gelu, values)
    return pullback(upstream)[0]


def rotate(vectors, cosine, sine_table):
    half = ROT // 2
    first_half = vectors[..., :half]
    second_half = vectors[..., half:ROT]
    return jnp.concatenate(
        [
            first_half * cosine - second_half * sine_table,
            second_half * cosine + first_half * sine_table,
            vectors[..., ROT:],
        ],
        axis=-1,
    )


def angles(bucket_ids):
    same_seq = bucket_ids[:, None] == bucket_ids[None, :]
    order = jnp.arange(bucket_ids.shape[0])
    earlier = order[None, :] < order[:, None]
    position = jnp.sum(jnp.where(same_seq & earlier, 1, 0), axis=1).astype(jnp.float32)
    freqs = 10000.0 ** (-2.0 * jnp.arange(ROT // 2).astype(jnp.float32) / ROT)
    angle = position[:, None] * freqs[None, :]
    allowed = same_seq & (order[None, :] <= order[:, None])
    return (jnp.cos(angle), jnp.sin(angle), allowed)


def score_block(query, key_rows, allowed):
    head_scale = HDIM ** (-0.5)
    scores = (
        jnp.einsum("hqd,hkd->hqk", query, key_rows, preferred_element_type=jnp.float32) * head_scale
    )
    return jnp.where(allowed[None], scores, -1e30)


def norm_back(grad_rows, unit_rows, inverse_rows, gain_rows):
    scaled = grad_rows * gain_rows
    mean_scaled = jnp.mean(scaled, axis=-1, keepdims=True)
    mean_cross = jnp.mean(scaled * unit_rows, axis=-1, keepdims=True)
    return inverse_rows * (scaled - mean_scaled - unit_rows * mean_cross)


def contract_rows(left, right):
    return lax.dot_general(
        left, right, (((0,), (0,)), ((), ())), preferred_element_type=jnp.float32
    )


def contract_cols(left, right):
    return lax.dot_general(
        left, right, (((1,), (1,)), ((), ())), preferred_element_type=jnp.float32
    )


def adam_step(master, first_moment, second_moment, gradient, factor, step_rate, decay_rate):
    scaled = gradient * factor
    first_new = beta_first * first_moment + (1.0 - beta_first) * scaled
    second_new = beta_second * second_moment + (1.0 - beta_second) * scaled * scaled
    first_hat = first_new / (1.0 - beta_first**STEP)
    second_hat = second_new / (1.0 - beta_second**STEP)
    master_new = master - step_rate * (
        first_hat / (jnp.sqrt(second_hat) + adam_epsilon) + decay_rate * master
    )
    return (master_new, first_new, second_new)


def gelu_parts(values):
    upper_share = 0.5 * (1.0 + lax.erf(values * math.sqrt(0.5)))
    density = jnp.exp(-0.5 * values * values) * (1.0 / math.sqrt(2.0 * math.pi))
    return upper_share, density


def bits_of(size):
    return [1 << index for index in range(size.bit_length() - 1)]


def feature_order(owners):
    order = [0]
    for bit in reversed(bits_of(owners)):
        order = order + [index | bit for index in order]
    return order


def swap(values, axis, mask):
    size = lax.axis_size(axis)
    return lax.ppermute(values, axis, [(source, source ^ mask) for source in range(size)])


def sync(plain, steps):
    held = [vars(item) for item in steps]
    names = [
        [name for name in ("values", "terms", "given", "moved") if item.get(name) is not None]
        for item in held
    ]
    plain, inner = lax.optimization_barrier(
        (
            list(plain),
            [[item[name] for name in kinds] for item, kinds in zip(held, names)],
        )
    )
    for item, kinds, values in zip(steps, names, inner):
        for name, value in zip(kinds, values):
            setattr(item, name, value)
    return plain


def gather_half(piece, axis, dim):
    for bit in reversed(bits_of(lax.axis_size(axis))[1:]):
        piece = jnp.concatenate([piece, swap(piece, axis, bit)], axis=dim)
    return piece


def halve(values, dim):
    half = values.shape[dim] // 2
    return (
        lax.slice_in_dim(values, 0, half, axis=dim),
        lax.slice_in_dim(values, half, 2 * half, axis=dim),
    )


class Reduce:
    def __init__(self, kept, given, axis, dim):
        self.terms, self.given, self.axis, self.dim = [kept], given, axis, dim

    def near(self):
        self.terms.append(swap(self.given, self.axis, 1))
        self.given = None

    def prepare(self):
        half = self.terms[-1].shape[self.dim] // 2
        self.given = sum(
            lax.slice_in_dim(term, half, 2 * half, axis=self.dim).astype(jnp.float32)
            for term in self.terms
        ).astype(jnp.bfloat16)

    def far(self):
        for bit in bits_of(lax.axis_size(self.axis))[1:]:
            if self.given is None:
                self.prepare()
            self.terms.append(swap(self.given, self.axis, bit))
            self.given = None

    def own(self):
        own = self.terms[-1].shape[self.dim]
        return sum(
            lax.slice_in_dim(term, 0, own, axis=self.dim).astype(jnp.float32)
            for term in self.terms
        )

    def squares(self):
        return square_sum(self.own())


class Halves:
    def __init__(self, values, axis):
        self.values, self.axis = values, axis

    def hop(self, bit):
        kept, given = halve(self.values, 1)
        self.values = kept + swap(given, self.axis, bit)

    def near(self):
        self.hop(1)

    def far(self):
        for bit in bits_of(lax.axis_size(self.axis))[1:]:
            self.hop(bit)

    def rows(self, axis, bits):
        for bit in bits:
            self.values = self.values + swap(self.values, axis, bit)


def step_both(scatter, stage, gather, gather_stage):
    for bit in scatter.order[stage]:
        given = scatter.split(bit)
        gather.settle()
        moved = swap(jnp.stack([given, gather.values]), scatter.axis, bit)
        scatter.moved, gather.moved, gather.bit = moved[0], moved[1], bit


def square_sum(values):
    return jnp.sum(values * values)


def share_index(axis):
    here = lax.axis_index(axis)
    place = 0
    for bit in bits_of(lax.axis_size(axis)):
        place = place * 2 + (here & bit) // bit
    return place


def unfold_rows(values, axis, dim):
    count = len(bits_of(lax.axis_size(axis)))
    shape = values.shape
    return values.reshape(
        shape[:dim] + (2,) * count + (shape[dim] >> count,) + shape[dim + 1 :]
    )


def fold_rows(values, axis, dim):
    count = len(bits_of(lax.axis_size(axis)))
    shape = values.shape
    return values.reshape(shape[:dim] + (-1,) + shape[dim + count + 1 :])


class Scatter:
    def __init__(self, values, axis, order):
        self.values, self.axis, self.order = unfold_rows(values, axis, 0), axis, list(order)
        self.places = bits_of(lax.axis_size(axis))
        self.moved = None

    def split(self, bit):
        self.settle()
        dim = self.places.index(bit)
        self.places = [place for place in self.places if place != bit]
        side = (lax.axis_index(self.axis) & bit) // bit
        given = lax.dynamic_index_in_dim(self.values, 1 - side, dim, False)
        self.values = lax.dynamic_index_in_dim(self.values, side, dim, False)
        return given

    def settle(self):
        if self.moved is not None:
            values = self.values.astype(jnp.float32) + self.moved.astype(jnp.float32)
            self.values = values.astype(jnp.bfloat16) if self.places else values
            self.moved = None

    def step(self, stage):
        for bit in self.order[stage]:
            self.moved = swap(self.split(bit), self.axis, bit)

    def result(self):
        self.settle()
        return self.values


class Gather:
    def __init__(self, values, axis, order, dim=0):
        self.values, self.axis, self.order, self.dim = values, axis, list(order), dim
        self.places, self.moved, self.bit = [], None, None

    def step(self, stage):
        for bit in self.order[stage]:
            self.settle()
            self.moved, self.bit = swap(self.values, self.axis, bit), bit

    def settle(self):
        if self.moved is None:
            return
        known = self.places + [self.bit]
        self.places = [place for place in bits_of(lax.axis_size(self.axis)) if place in known]
        dim = self.dim + self.places.index(self.bit)
        side = (lax.axis_index(self.axis) & self.bit) // self.bit
        shape = list(self.moved.shape)
        shape.insert(dim, 2)
        self.values = jnp.where(
            lax.broadcasted_iota(jnp.int32, shape, dim) == side,
            jnp.expand_dims(self.values, dim),
            jnp.expand_dims(self.moved, dim),
        )
        self.moved = None

    def place_new(self, count, index):
        spot = bits_of(lax.axis_size(self.axis)).index(self.bit)
        side = (lax.axis_index(self.axis) & self.bit) // self.bit
        whole = place_first(self.values, self.moved, side, spot, count, index)
        shape = self.values.shape[:spot] + (2,) + self.values.shape[spot:]
        return whole.reshape((count,) + shape)

    def place_last(self, whole, index):
        spot = bits_of(lax.axis_size(self.axis)).index(self.bit)
        side = (lax.axis_index(self.axis) & self.bit) // self.bit
        for values, at in ((self.values, side), (self.moved, 1 - side)):
            block = jnp.expand_dims(values, spot)[None]
            starts = [0] * block.ndim
            starts[0], starts[spot + 1] = index, at
            whole = lax.dynamic_update_slice(whole, block, starts)
        return whole

    def result(self):
        self.settle()
        return fold_rows(self.values, self.axis, self.dim)


def stages_of(axis):
    bits = bits_of(lax.axis_size(axis))
    near = len(bits) - 2
    return bits[:near], bits[near : near + 1], bits[near + 1 :]


def light():
    return pl.CostEstimate(flops=1, bytes_accessed=1, transcendentals=0)


def join_kernel(*refs):
    out_ref = refs[-1]
    cols = refs[0].shape[-1]
    for index, ref in enumerate(refs[:-1]):
        out_ref[:, :, index * cols : (index + 1) * cols] = ref[...]


def join_blocks(blocks):
    shape = blocks[0].shape
    return pl.pallas_call(
        join_kernel,
        out_shape=jax.ShapeDtypeStruct(
            shape[:-1] + (shape[-1] * len(blocks),), blocks[0].dtype
        ),
        cost_estimate=light(),
    )(*blocks)


def place_kernel(side_ref, values_ref, moved_ref, out_ref):
    @pl.when(pl.program_id(1) == 0)
    def own():
        out_ref[0, 0, 0] = values_ref[0]

    @pl.when(pl.program_id(1) == 1)
    def other():
        out_ref[0, 0, 0] = moved_ref[0]


def place_first(values, moved, side, spot, count, index):
    front = 2**spot
    rows, width = values.size // values.shape[-1] // front, values.shape[-1]
    part = pl.BlockSpec((1, rows, width), lambda a, g, side_ref: (a, 0, 0))
    return pl.pallas_call(
        place_kernel,
        grid_spec=pltpu.PrefetchScalarGridSpec(
            num_scalar_prefetch=1,
            grid=(front, 2),
            in_specs=[part, part],
            out_specs=pl.BlockSpec(
                (1, 1, 1, rows, width),
                lambda a, g, side_ref: (index, a, (side_ref[0] + g) % 2, 0, 0),
            ),
        ),
        out_shape=jax.ShapeDtypeStruct((count, front, 2, rows, width), values.dtype),
        compiler_params=pltpu.CompilerParams(vmem_limit_bytes=12 << 20),
        cost_estimate=light(),
    )(
        side.reshape(1).astype(jnp.int32),
        values.reshape(front, rows, width),
        moved.reshape(front, rows, width),
    )


def outer_kernel(pairs, *refs):
    for left, right, target in pairs:
        left_ref, right_ref = refs[left], refs[right]
        value = contract_rows(left_ref[...].reshape(left_ref.shape[-2:]), right_ref[...])
        refs[target][...] = value.astype(jnp.bfloat16)


def outer_call(operands, specs, pairs, grid, out_rows, out_cols, tile):
    out = pl.BlockSpec((tile, out_cols), lambda i: (i, 0))
    shape = jax.ShapeDtypeStruct((out_rows, out_cols), jnp.bfloat16)
    return pl.pallas_call(
        functools.partial(outer_kernel, pairs),
        grid=grid,
        in_specs=specs,
        out_specs=[out, out],
        out_shape=[shape, shape],
        compiler_params=pltpu.CompilerParams(vmem_limit_bytes=16 << 20),
        cost_estimate=light(),
    )(*operands)


def project_grads(hidden, kept, given):
    tokens, units = hidden.shape
    tile = 256
    whole = pl.BlockSpec(kept.shape, lambda i: (0, 0))
    return outer_call(
        (hidden, kept, given),
        [pl.BlockSpec((tokens, tile), lambda i: (0, i)), whole, whole],
        ((0, 1, 3), (0, 2, 4)),
        (units // tile,),
        units,
        kept.shape[1],
        tile,
    )


def expand_grads(kept, given, upper):
    count, tokens, width = kept.shape
    tile = 256
    part = pl.BlockSpec((1, tokens, tile), lambda i: (count - 1, 0, i))
    return outer_call(
        (kept, given, upper),
        [part, part, pl.BlockSpec(upper.shape, lambda i: (0, 0))],
        ((0, 2, 3), (1, 2, 4)),
        (width // tile,),
        width,
        upper.shape[1],
        tile,
    )


def attend_grads_kernel(
    kept_ref, given_ref, back_ref, out_kept_ref, out_given_ref, heads_ref, *outs
):
    last = pl.program_id(0) == pl.num_programs(0) - 1
    for left_ref, other_ref, target_ref in (
        (kept_ref, out_kept_ref, outs[0]),
        (given_ref, out_given_ref, outs[1]),
    ):

        @pl.when(jnp.logical_not(last))
        def inner(left_ref=left_ref, target_ref=target_ref):
            target_ref[0] = contract_rows(left_ref[0], back_ref[0]).astype(jnp.bfloat16)

        @pl.when(last)
        def outer(other_ref=other_ref, target_ref=target_ref):
            target_ref[0] = contract_rows(other_ref[...], heads_ref[...]).astype(jnp.bfloat16)


def attend_grads_call(kept, given, back, out_kept, out_given, heads):
    count, tokens, width = kept.shape
    units = heads.shape[1]
    part = pl.BlockSpec((1, tokens, width), lambda c: (jnp.minimum(c, count - 2), 0, 0))
    whole = pl.BlockSpec((tokens, width), lambda c: (0, 0))
    out = pl.BlockSpec((1, width, units), lambda c: (c, 0, 0))
    shape = jax.ShapeDtypeStruct((count, width, units), jnp.bfloat16)
    return pl.pallas_call(
        attend_grads_kernel,
        grid=(count,),
        in_specs=[
            part,
            part,
            pl.BlockSpec((1, tokens, units), lambda c: (jnp.minimum(c, count - 2), 0, 0)),
            whole,
            whole,
            pl.BlockSpec((tokens, units), lambda c: (0, 0)),
        ],
        out_specs=[out, out],
        out_shape=[shape, shape],
        compiler_params=pltpu.CompilerParams(vmem_limit_bytes=20 << 20),
        cost_estimate=light(),
    )(kept, given, back, out_kept, out_given, heads)


def adam_kernel(rates, count, flip, factor_ref, *refs):
    term_refs, (master_ref, first_ref, second_ref) = refs[:count], refs[count : count + 3]
    new_ref, first_new_ref, second_new_ref, copy_ref = refs[count + 3 :]
    gradient = sum(term_ref[...].astype(jnp.float32) for term_ref in term_refs)
    if flip:
        gradient = gradient[0].T
    master_new, first_new, second_new = adam_step(
        master_ref[...], first_ref[...], second_ref[...], gradient, factor_ref[0], *rates
    )
    new_ref[...] = master_new
    first_new_ref[...] = first_new
    second_new_ref[...] = second_new
    copy_ref[...] = master_new.astype(jnp.bfloat16)


def adam_call(terms, master, first_moment, second_moment, factor, rates, grid, block, spot):
    flip = spot is not None
    own = pl.BlockSpec(block, lambda *steps: steps[: len(grid)])
    if flip:
        term_specs = [
            pl.BlockSpec((1,) + block[::-1], lambda *steps: (spot, steps[1], 0)) for term in terms
        ]
    else:
        term_specs = [own] * len(terms)
    wide = jax.ShapeDtypeStruct(master.shape, jnp.float32)
    return pl.pallas_call(
        functools.partial(adam_kernel, rates, len(terms), flip),
        grid=grid,
        in_specs=[pl.BlockSpec(memory_space=pltpu.SMEM)] + term_specs + [own] * 3,
        out_specs=[own] * 4,
        out_shape=[wide, wide, wide, jax.ShapeDtypeStruct(master.shape, jnp.bfloat16)],
        compiler_params=pltpu.CompilerParams(vmem_limit_bytes=20 << 20),
        cost_estimate=light(),
    )(factor.reshape(1), *terms, master, first_moment, second_moment)


def lane_block(place_ref, index, cols):
    return pl.ds(pl.multiple_of(place_ref[index] * cols, cols), cols)


def norm_kernel(owners, place_ref, inputs_ref, gains_ref, biases_ref, kept_ref, given_ref):
    cols = inputs_ref.shape[2] // owners
    values = inputs_ref[0].astype(jnp.float32)
    mean_vals = jnp.mean(values, axis=-1, keepdims=True)
    centred = values - mean_vals
    inverse = lax.rsqrt(jnp.mean(centred * centred, axis=-1, keepdims=True) + norm_epsilon)
    for index in range(owners):
        block = inputs_ref[0, :, lane_block(place_ref, index, cols)].astype(jnp.float32)
        spot = slice(index * cols, (index + 1) * cols)
        normed = (block - mean_vals) * inverse * gains_ref[0, :, spot] + biases_ref[0, :, spot]
        target = kept_ref if index < owners // 2 else given_ref
        near = index % (owners // 2)
        target[0, :, near * cols : (near + 1) * cols] = normed.astype(jnp.bfloat16)


def norm_forward(layer_inputs, gains, biases, place, owners):
    count, tokens, width = layer_inputs.shape
    tile = 128
    half = pl.BlockSpec((1, tile, width // 2), lambda c, i, place_ref: (c, i, 0))
    row = pl.BlockSpec((1, 1, width), lambda c, i, place_ref: (c, 0, 0))
    shape = jax.ShapeDtypeStruct((count, tokens, width // 2), jnp.bfloat16)
    return pl.pallas_call(
        functools.partial(norm_kernel, owners),
        grid_spec=pltpu.PrefetchScalarGridSpec(
            num_scalar_prefetch=1,
            grid=(count, tokens // tile),
            in_specs=[
                pl.BlockSpec((1, tile, width), lambda c, i, place_ref: (c, i, 0)),
                row,
                row,
            ],
            out_specs=[half, half],
        ),
        out_shape=[shape, shape],
        compiler_params=pltpu.CompilerParams(vmem_limit_bytes=14 << 20),
        cost_estimate=light(),
    )(place, layer_inputs, gains[:, None, :], biases[:, None, :])


def turn(values, cosine, sine_low, sine_high):
    width = values.shape[-1]
    return (
        values * cosine
        + pltpu.roll(values, width - ROT // 2, 1) * sine_low
        + pltpu.roll(values, ROT // 2, 1) * sine_high
    )


def masked_probs(query, key_rows, ids_col, ids_row):
    tokens = query.shape[0]
    scores = lax.dot_general(
        query, key_rows, (((1,), (1,)), ((), ())), preferred_element_type=jnp.float32
    ) * (HDIM ** (-0.5))
    here = lax.broadcasted_iota(jnp.int32, (tokens, tokens), 0)
    there = lax.broadcasted_iota(jnp.int32, (tokens, tokens), 1)
    scores = jnp.where((ids_col == ids_row) & (there <= here), scores, -1e30)
    row_max = jnp.max(scores, axis=-1, keepdims=True)
    log_total = jnp.log(jnp.sum(jnp.exp(scores - row_max), axis=-1, keepdims=True)) + row_max
    return jnp.exp(scores - log_total)


def attend_kernel(proj_ref, cos_ref, low_ref, high_ref, col_ref, row_ref, turned_ref, heads_ref):
    tables = (cos_ref[...], low_ref[...], high_ref[...])
    query = turn(proj_ref[0], *tables).astype(jnp.bfloat16)
    key_rows = turn(proj_ref[1], *tables).astype(jnp.bfloat16)
    value_rows = proj_ref[2].astype(jnp.bfloat16)
    turned_ref[0] = query
    turned_ref[1] = key_rows
    turned_ref[2] = value_rows
    prob = masked_probs(query, key_rows, col_ref[...], row_ref[...]).astype(jnp.bfloat16)
    heads_ref[...] = jnp.dot(prob, value_rows, preferred_element_type=jnp.float32).astype(
        jnp.bfloat16
    )


def attend_back_kernel(
    turned_ref, grads_ref, cos_ref, low_ref, high_ref, col_ref, row_ref, back_ref
):
    query, key_rows, value_rows = turned_ref[0], turned_ref[1], turned_ref[2]
    grads = grads_ref[...]
    prob = masked_probs(query, key_rows, col_ref[...], row_ref[...])
    grad_prob = contract_cols(grads, value_rows)
    row_delta = jnp.sum(prob * grad_prob, axis=-1, keepdims=True)
    grad_scores = (prob * (grad_prob - row_delta)).astype(jnp.bfloat16)
    tables = (cos_ref[...], -low_ref[...], -high_ref[...])
    head_scale = HDIM ** (-0.5)
    grad_query = jnp.dot(grad_scores, key_rows, preferred_element_type=jnp.float32) * head_scale
    grad_key = contract_rows(grad_scores, query) * head_scale
    back_ref[0] = turn(grad_query, *tables).astype(jnp.bfloat16)
    back_ref[1] = turn(grad_key, *tables).astype(jnp.bfloat16)
    back_ref[2] = contract_rows(prob.astype(jnp.bfloat16), grads).astype(jnp.bfloat16)


def attend_specs(tokens):
    table = pl.BlockSpec((tokens, HDIM), lambda head: (0, 0))
    heads = pl.BlockSpec((tokens, HDIM), lambda head: (0, head))
    triple = pl.BlockSpec((3, tokens, HDIM), lambda head: (0, 0, head))
    shared = [
        table,
        table,
        table,
        pl.BlockSpec((tokens, 1), lambda head: (0, 0)),
        pl.BlockSpec((1, tokens), lambda head: (0, 0)),
    ]
    return heads, triple, shared


def attend(proj, tables, ids):
    tokens, width = proj.shape[1:]
    heads, triple, shared = attend_specs(tokens)
    return pl.pallas_call(
        attend_kernel,
        grid=(width // HDIM,),
        in_specs=[triple] + shared,
        out_specs=[triple, heads],
        out_shape=[
            jax.ShapeDtypeStruct((3, tokens, width), jnp.bfloat16),
            jax.ShapeDtypeStruct((tokens, width), jnp.bfloat16),
        ],
        compiler_params=pltpu.CompilerParams(vmem_limit_bytes=16 << 20),
        cost_estimate=light(),
    )(proj, *tables, ids[:, None], ids[None, :])


def attend_back(turned, grads, tables, ids):
    tokens, width = grads.shape
    heads, triple, shared = attend_specs(tokens)
    return pl.pallas_call(
        attend_back_kernel,
        grid=(width // HDIM,),
        in_specs=[triple, heads] + shared,
        out_specs=triple,
        out_shape=jax.ShapeDtypeStruct((3, tokens, width), jnp.bfloat16),
        compiler_params=pltpu.CompilerParams(vmem_limit_bytes=20 << 20),
        cost_estimate=light(),
    )(turned, grads, *tables, ids[:, None], ids[None, :])


def mix_kernel(
    branch_ref,
    inputs_ref,
    stored_ref,
    entry_ref,
    cotangent_ref,
    valid_ref,
    gain_ref,
    mixer_in_ref,
    mixer_out_ref,
    newest_ref,
    grad_newest_ref,
    sent_kept_ref,
    sent_given_ref,
    mixer_in_grad_ref,
    mixer_out_grad_ref,
    gain_grad_ref,
):
    valid = valid_ref[...]
    gain = gain_ref[...]
    newest = inputs_ref[...].astype(jnp.float32) + valid * branch_ref[...]
    newest_ref[...] = newest.astype(jnp.bfloat16)
    rows, width = newest.shape
    scale = lax.rsqrt(jnp.mean(newest * newest, axis=-1, keepdims=True) + mixer_epsilon)
    normed = (newest * scale * gain).astype(jnp.bfloat16)
    mix_pre = contract_cols(normed, mixer_in_ref[...])
    phi, density = gelu_parts(mix_pre)
    mix_act = (mix_pre * phi).astype(jnp.bfloat16)
    weights = contract_cols(mix_act, mixer_out_ref[...])
    count = stored_ref.shape[0] + 1
    total = weights.shape[1]
    lane = lax.broadcasted_iota(jnp.int32, (rows, total), 1)
    grad_weights = jnp.zeros((rows, total), jnp.float32)
    newest_back = jnp.zeros((rows, width), jnp.float32)
    for outer in range(total // count):
        upstream = cotangent_ref[outer].astype(jnp.float32)
        for inner in range(count):
            layer = newest if inner == count - 1 else stored_ref[inner].astype(jnp.float32)
            dots = jnp.sum(upstream * layer, axis=-1, keepdims=True)
            grad_weights = jnp.where(lane == outer * count + inner, dots, grad_weights)
        last = outer * count + count - 1
        newest_back = newest_back + weights[:, last : last + 1] * upstream
    grad_weights = grad_weights.astype(jnp.bfloat16)
    mixer_out_grad_ref[...] = contract_rows(grad_weights, mix_act)
    grad_act = jnp.dot(grad_weights, mixer_out_ref[...], preferred_element_type=jnp.float32)
    grad_pre = ((phi + mix_pre * density) * grad_act).astype(jnp.bfloat16)
    mixer_in_grad_ref[...] = contract_rows(grad_pre, normed)
    grad_normed = jnp.dot(grad_pre, mixer_in_ref[...], preferred_element_type=jnp.float32)
    gain_grad_ref[...] = jnp.sum(grad_normed * newest * scale, axis=0, keepdims=True)
    scaled = grad_normed * gain
    grad_newest = (
        newest_back
        + entry_ref[...].astype(jnp.float32)
        + scale * scaled
        - newest * (scale * scale * scale) * jnp.mean(scaled * newest, axis=-1, keepdims=True)
    )
    grad_newest_ref[...] = grad_newest
    sent = (valid * grad_newest).astype(jnp.bfloat16)
    sent_kept_ref[...] = sent[:, 0 : width // 2]
    sent_given_ref[:, 0 : width // 2] = sent[:, width // 2 :]
    high = weights.astype(jnp.bfloat16)
    rest = (weights - high.astype(jnp.float32)).astype(jnp.bfloat16)
    blank = jnp.zeros((rows, 128 - 2 * total), jnp.bfloat16)
    sent_given_ref[:, width // 2 :] = jnp.concatenate([high, rest, blank], axis=1)


def mix(branch, inputs, stored, entry, cotangent, valid, gain, mixer_in, mixer_out):
    rows, width = branch.shape
    hidden_units = mixer_in.shape[0]
    total = mixer_out.shape[0]
    return pl.pallas_call(
        mix_kernel,
        out_shape=[
            jax.ShapeDtypeStruct((rows, width), jnp.bfloat16),
            jax.ShapeDtypeStruct((rows, width), jnp.float32),
            jax.ShapeDtypeStruct((rows, width // 2), jnp.bfloat16),
            jax.ShapeDtypeStruct((rows, width // 2 + 128), jnp.bfloat16),
            jax.ShapeDtypeStruct((hidden_units, width), jnp.float32),
            jax.ShapeDtypeStruct((total, hidden_units), jnp.float32),
            jax.ShapeDtypeStruct((1, width), jnp.float32),
        ],
        compiler_params=pltpu.CompilerParams(vmem_limit_bytes=32 << 20),
        cost_estimate=light(),
    )(branch, inputs, stored, entry, cotangent, valid, gain, mixer_in, mixer_out)


def history_kernel(owners, count, place_ref, weights_ref, cotangent_ref, *back_refs):
    cols = back_refs[0].shape[2]
    spots = [
        (target_ref, layer)
        for target_ref in back_refs
        for layer in range(target_ref.shape[0])
    ]
    weights = weights_ref[...]
    for index in range(owners):
        spot = lane_block(place_ref, index, cols)
        upstream = [
            cotangent_ref[outer, :, spot].astype(jnp.float32)
            for outer in range(cotangent_ref.shape[0])
        ]
        for layer in range(count - 1):
            target_ref, near = spots[index * (count - 1) + layer]
            target_ref[near] = sum(
                weights[:, outer * count + layer : outer * count + layer + 1] * upstream[outer]
                for outer in range(len(upstream))
            ).astype(jnp.bfloat16)


def history_back(weights, cotangent, place, owners):
    outer, tokens, width = cotangent.shape
    total = weights.shape[1]
    count = total // outer
    cuts = []
    for index in feature_order(owners):
        cuts += [count - 2, 1] if index > 1 else [count - 1]
    tile = 128
    return pl.pallas_call(
        functools.partial(history_kernel, owners, count),
        grid_spec=pltpu.PrefetchScalarGridSpec(
            num_scalar_prefetch=1,
            grid=(tokens // tile,),
            in_specs=[
                pl.BlockSpec((tile, total), lambda i, place_ref: (i, 0)),
                pl.BlockSpec((outer, tile, width), lambda i, place_ref: (0, i, 0)),
            ],
            out_specs=[
                pl.BlockSpec((layers, tile, width // owners), lambda i, place_ref: (0, i, 0))
                for layers in cuts
            ],
        ),
        out_shape=[
            jax.ShapeDtypeStruct((layers, tokens, width // owners), jnp.bfloat16)
            for layers in cuts
        ],
        compiler_params=pltpu.CompilerParams(vmem_limit_bytes=20 << 20),
        cost_estimate=light(),
    )(place, weights, cotangent)


def next_kernel(owners, place_ref, weights_ref, newest_ref, *refs):
    stored_refs, next_ref = refs[:-1], refs[-1]
    cols = newest_ref.shape[1] // owners
    weights = weights_ref[...]
    count = len(stored_refs) + 1
    for index in range(owners):
        spot = slice(index * cols, (index + 1) * cols)
        layers = [stored_ref[:, spot].astype(jnp.float32) for stored_ref in stored_refs]
        layers.append(newest_ref[:, spot].astype(jnp.float32))
        for outer in range(next_ref.shape[0]):
            next_ref[outer, :, lane_block(place_ref, index, cols)] = sum(
                weights[:, outer * count + layer : outer * count + layer + 1] * layers[layer]
                for layer in range(count)
            ).astype(jnp.bfloat16)


def next_layer(weights, stored, newest, place, owners):
    tokens, width = newest.shape
    total = weights.shape[1]
    count = len(stored) + 1
    outer = total // count
    tile = 128
    return pl.pallas_call(
        functools.partial(next_kernel, owners),
        grid_spec=pltpu.PrefetchScalarGridSpec(
            num_scalar_prefetch=1,
            grid=(tokens // tile,),
            in_specs=[
                pl.BlockSpec((tile, total), lambda i, place_ref: (i, 0)),
            ]
            + [pl.BlockSpec((tile, width), lambda i, place_ref: (i, 0))] * count,
            out_specs=pl.BlockSpec((outer, tile, width), lambda i, place_ref: (0, i, 0)),
        ),
        out_shape=jax.ShapeDtypeStruct((outer, tokens, width), jnp.bfloat16),
        compiler_params=pltpu.CompilerParams(vmem_limit_bytes=24 << 20),
        cost_estimate=light(),
    )(place, weights, newest, *stored)


def sums_kernel(owners, place_ref, grads_ref, inputs_ref, sums_ref):
    cols = inputs_ref.shape[2] // owners
    values = inputs_ref[0].astype(jnp.float32)
    mean_vals = jnp.mean(values, axis=-1, keepdims=True)
    centred = values - mean_vals
    inverse = lax.rsqrt(jnp.mean(centred * centred, axis=-1, keepdims=True) + norm_epsilon)

    @pl.when(pl.program_id(1) == 0)
    def clear():
        sums_ref[...] = jnp.zeros_like(sums_ref)

    for index in range(owners):
        spot = lane_block(place_ref, index, cols)
        unit = (inputs_ref[0, :, spot].astype(jnp.float32) - mean_vals) * inverse
        grads = grads_ref[0, :, index * cols : (index + 1) * cols].astype(jnp.float32)
        near = slice(index * cols, (index + 1) * cols)
        sums_ref[0, 0:1, near] += jnp.sum(grads * unit, axis=0, keepdims=True)
        sums_ref[0, 1:2, near] += jnp.sum(grads, axis=0, keepdims=True)


def norm_sums(grads, layer_inputs, first, place, owners):
    count, tokens, width = grads.shape
    tile = 128
    return pl.pallas_call(
        functools.partial(sums_kernel, owners),
        grid_spec=pltpu.PrefetchScalarGridSpec(
            num_scalar_prefetch=1,
            grid=(count, tokens // tile),
            in_specs=[
                pl.BlockSpec((1, tile, width), lambda c, i, place_ref: (c, i, 0)),
                pl.BlockSpec((1, tile, width), lambda c, i, place_ref: (c + first, i, 0)),
            ],
            out_specs=pl.BlockSpec((1, 2, width), lambda c, i, place_ref: (c, 0, 0)),
        ),
        out_shape=jax.ShapeDtypeStruct((count, 2, width), jnp.float32),
        compiler_params=pltpu.CompilerParams(vmem_limit_bytes=12 << 20),
        cost_estimate=light(),
    )(place, grads, layer_inputs)


def back_kernel(
    owners, place_ref, grads_ref, moved_ref, inputs_ref, gain_ref, extra_ref, out_ref
):
    cols = inputs_ref.shape[1] // owners
    values = inputs_ref[...].astype(jnp.float32)
    centred = values - jnp.mean(values, axis=-1, keepdims=True)
    inverse = lax.rsqrt(jnp.mean(centred * centred, axis=-1, keepdims=True) + norm_epsilon)
    grads = grads_ref[...].astype(jnp.float32) + moved_ref[...].astype(jnp.float32)
    back = norm_back(grads, centred * inverse, inverse, gain_ref[...])
    if extra_ref is not None:
        back = back + extra_ref[...]
    for index in range(owners):
        spot = slice(index * cols, (index + 1) * cols)
        out_ref[:, lane_block(place_ref, index, cols)] = back[:, spot].astype(jnp.bfloat16)


def back_share(grads, moved, inputs, gain, extra, place, owners):
    rows, width = grads.shape
    kernel = functools.partial(back_kernel, owners)
    if extra is None:
        kernel = lambda place_ref, grads_ref, moved_ref, inputs_ref, gain_ref, out_ref: back_kernel(
            owners, place_ref, grads_ref, moved_ref, inputs_ref, gain_ref, None, out_ref
        )
    whole = pl.BlockSpec((rows, width), lambda i, place_ref: (0, 0))
    given = [grads, moved, inputs, gain] + ([] if extra is None else [extra])
    return pl.pallas_call(
        kernel,
        grid_spec=pltpu.PrefetchScalarGridSpec(
            num_scalar_prefetch=1,
            grid=(1,),
            in_specs=[whole, whole, whole, pl.BlockSpec((1, width), lambda i, place_ref: (0, 0))]
            + ([] if extra is None else [whole]),
            out_specs=whole,
        ),
        out_shape=jax.ShapeDtypeStruct((rows, width), jnp.bfloat16),
        compiler_params=pltpu.CompilerParams(vmem_limit_bytes=12 << 20),
        cost_estimate=light(),
    )(place, *given)


def body(
    layer_inputs,
    history,
    seq_ids,
    norms_master,
    norms_first,
    norms_second,
    attend_in_master,
    attend_in_first,
    attend_in_second,
    attend_out_master,
    attend_out_first,
    attend_out_second,
    expand_master,
    expand_first,
    expand_second,
    project_master,
    project_first,
    project_second,
    mixer_in_master,
    mixer_in_first,
    mixer_in_second,
    mixer_out_master,
    mixer_out_first,
    mixer_out_second,
    next_cotangent,
    grad_entry,
):
    bf16_type = jnp.bfloat16
    float_type = jnp.float32
    tensor_size = lax.axis_size("tensor")
    owners = lax.axis_size("dp")
    me = lax.axis_index("dp")
    order = feature_order(owners)
    place = jnp.stack([me ^ index for index in order]).astype(jnp.int32)
    tokens_here, width = layer_inputs.shape[1:]
    share_rows = tokens_here // tensor_size
    share_start = share_index("tensor") * share_rows
    cols = norms_master.shape[1]
    mixers = mixer_out_master.shape[0]

    def own_rows(values, axis):
        return lax.dynamic_slice_in_dim(values, share_start, share_rows, axis)

    def reorder(values):
        return jnp.concatenate(
            [
                lax.dynamic_slice_in_dim(values, (me ^ index) * cols, cols, values.ndim - 1)
                for index in order
            ],
            axis=-1,
        )


    near, side_bits, far = stages_of("tensor")
    out_first = (near, side_bits, far)
    in_first = (side_bits, far, near)
    back_order = (far, side_bits, near)
    cross_order = (near, far, side_bits)

    early_rows = [
        jnp.concatenate(
            [
                lax.dynamic_slice_in_dim(
                    values, (me ^ index) * tokens_here + share_start, share_rows, 1
                )
                for values in (history, grad_entry[None])
            ],
            axis=0,
        )
        for index in order
    ]
    early_rows = [
        rows if index == 0 else swap(rows, "dp", index) for rows, index in zip(early_rows, order)
    ]
    norms_half = gather_half(norms_master.astype(bf16_type), "dp", 1)
    attend_low = jnp.concatenate(
        [attend_in_master.astype(bf16_type), attend_out_master.astype(bf16_type).T[None]], axis=0
    )
    norms_half, attend_low, early_rows, expand_late, mixer_in_late, mixer_out_late = sync(
        [norms_half, attend_low, early_rows, expand_master, mixer_in_master, mixer_out_master], []
    )

    attend_kept = gather_half(attend_low, "dp", 1)
    early = join_blocks(early_rows)
    stored_share = early[:-1]
    layer_count = stored_share.shape[0] + 1
    stored_most = Gather(stored_share[:-1], "tensor", back_order, 1)
    stored_last = Gather(stored_share[-1:], "tensor", cross_order, 1)
    stored_most.step(0)
    stored_last.step(0)
    expand_low = expand_late.astype(bf16_type)
    norms_given = swap(norms_half, "dp", 1)
    norm_vals = jnp.concatenate([norms_half, norms_given], axis=1).astype(float_type)
    normed_kept, normed_given = norm_forward(
        layer_inputs, norm_vals[0:4], norm_vals[4:8], place, owners
    )
    attend_kept, normed_kept, normed_given, expand_low, project_late = sync(
        [attend_kept, normed_kept, normed_given, expand_low, project_master],
        [stored_most, stored_last],
    )

    small = jnp.concatenate(
        [mixer_in_late.T, jnp.pad(mixer_out_late, ((0, 0), (0, cols - MIXH)))], axis=0
    ).astype(bf16_type)
    small_half = gather_half(small, "dp", 1)
    expand_kept = gather_half(expand_low, "dp", 0)
    attend_given = swap(attend_kept, "dp", 1)
    stored_most.step(1)
    proj_kept = jnp.einsum(
        "ctd,cde->cte", normed_kept[0:3], attend_kept[0:3], preferred_element_type=float_type
    )
    cosine, sine_table, unused = angles(seq_ids)
    half = ROT // 2
    tables = (
        jnp.concatenate([cosine, cosine, jnp.ones((tokens_here, HDIM - ROT), float_type)], 1),
        jnp.pad(-sine_table, ((0, 0), (0, HDIM - half))),
        jnp.pad(sine_table, ((0, 0), (half, HDIM - ROT))),
    )
    project_low = project_late.astype(bf16_type)
    (
        small_half,
        expand_kept,
        attend_given,
        proj_kept,
        project_low,
        tables,
        layer_late,
        cotangent_late,
    ) = sync(
        [
            small_half,
            expand_kept,
            attend_given,
            proj_kept,
            project_low,
            tables,
            layer_inputs,
            next_cotangent,
        ],
        [stored_most, stored_last],
    )

    small_whole = jnp.concatenate([small_half, swap(small_half, "dp", 1)], axis=1)
    mixer_in_low = small_whole[0:MIXH]
    out_rows = small_whole[MIXH:]
    mixer_out_low = jnp.zeros((owners, mixers, MIXH), bf16_type)
    for spot, index in enumerate(order):
        mixer_out_low = lax.dynamic_update_index_in_dim(
            mixer_out_low, out_rows[:, spot * cols : spot * cols + MIXH], me ^ index, 0
        )
    mixer_out_low = mixer_out_low.reshape(owners * mixers, MIXH)
    project_kept = gather_half(project_low, "dp", 1)
    expand_given = swap(expand_kept, "dp", 1)
    stored_last.step(1)
    stored_most.settle()
    stored_pair = [
        Gather(stored_most.values[index : index + 1], "tensor", back_order, 1)
        for index in range(layer_count - 2)
    ]
    for item in stored_pair:
        item.places = list(stored_most.places)
    for item in stored_pair[:1]:
        item.step(2)
    proj = proj_kept + jnp.einsum(
        "ctd,cde->cte", normed_given[0:3], attend_given[0:3], preferred_element_type=float_type
    )
    turned, heads_out = attend(proj, tables, seq_ids)
    upper_kept = jnp.dot(normed_kept[3], expand_kept, preferred_element_type=float_type)
    valid = (own_rows(seq_ids, 0) >= 0).astype(float_type)[:, None]
    input_share = reorder(own_rows(layer_late, 1))
    cotangent_share = reorder(own_rows(cotangent_late, 1))
    (
        mixer_in_low,
        mixer_out_low,
        project_kept,
        expand_given,
        turned,
        heads_out,
        upper_kept,
        input_share,
        cotangent_share,
    ) = sync(
        [
            mixer_in_low,
            mixer_out_low,
            project_kept,
            expand_given,
            turned,
            heads_out,
            upper_kept,
            input_share,
            cotangent_share,
        ],
        [stored_last] + stored_pair,
    )

    out_kept, out_given = attend_kept[3], attend_given[3]
    project_given = swap(project_kept, "dp", 1)
    upper = upper_kept + jnp.dot(normed_given[3], expand_given, preferred_element_type=float_type)
    phi, density = gelu_parts(upper)
    hidden = exact_gelu(upper).astype(bf16_type)
    slope = phi + upper * density
    branch_kept = Scatter(
        (
            contract_cols(heads_out, out_kept)
            + jnp.dot(hidden, project_kept, preferred_element_type=float_type)
        ).astype(bf16_type),
        "tensor",
        out_first,
    )
    branch_given = Scatter(
        (
            contract_cols(heads_out, out_given)
            + jnp.dot(hidden, project_given, preferred_element_type=float_type)
        ).astype(bf16_type),
        "tensor",
        in_first,
    )
    for stage in range(3):
        branch_kept.step(stage)
        branch_given.step(stage)
    branch = jnp.concatenate([branch_kept.result(), branch_given.result()], axis=-1)
    branch, slope = sync([branch, slope], [])

    newest, grad_newest, sent_kept, sent_given, grad_mixer_in, grad_mixer_out, mixer_gain = mix(
        branch,
        input_share[3],
        stored_share,
        early[-1],
        cotangent_share,
        valid,
        norm_vals[8:9],
        mixer_in_low,
        mixer_out_low,
    )
    grad_kept = Gather(sent_kept, "tensor", back_order)
    grad_given = Gather(sent_given, "tensor", cross_order)
    for stage in range(3):
        grad_kept.step(stage)
        grad_given.step(stage)
    grad_kept = grad_kept.result()
    received = grad_given.result()
    grad_given = received[:, 0 : width // 2]
    mix_low = received[:, width // 2 :]
    mix_total = 4 * layer_count
    mix_weights = mix_low[:, 0:mix_total].astype(float_type) + mix_low[
        :, mix_total : 2 * mix_total
    ].astype(float_type)
    newest_all = Gather(newest, "tensor", back_order)
    grad_kept, grad_given, mix_weights = sync(
        [grad_kept, grad_given, mix_weights], [newest_all, stored_last] + stored_pair
    )

    history_pieces = history_back(mix_weights, cotangent_late, place, owners)
    history_pieces = list(history_pieces)
    history_front, history_last = [], []
    for index in order:
        history_front.append(history_pieces.pop(0))
        history_last.append(history_pieces.pop(0) if index > 1 else None)

    def send_far(pieces, which):
        for spot in which:
            pieces[spot] = swap(pieces[spot], "dp", order[spot])

    far_spots = [spot for spot in range(owners) if order[spot] > 1]
    near_spots = [spot for spot in range(owners) if order[spot] == 1]
    first_far, last_far = far_spots[: len(far_spots) // 2], far_spots[len(far_spots) // 2 :]
    for item in stored_pair[1:]:
        item.step(2)
    stored_last.step(2)
    newest_all.step(0)
    grad_hidden = contract_cols(grad_kept, project_kept) + contract_cols(grad_given, project_given)
    grad_upper = (slope * grad_hidden).astype(bf16_type)
    grad_normed_ffn = jnp.concatenate(
        [
            contract_cols(grad_upper, expand_kept).astype(bf16_type),
            contract_cols(grad_upper, expand_given).astype(bf16_type),
        ],
        axis=-1,
    )
    grad_project = Reduce(*project_grads(hidden, grad_kept, grad_given), "dp", 1)
    (
        history_front,
        history_last,
        grad_normed_ffn,
        grad_upper,
        grad_kept,
        grad_given,
        out_kept,
        out_given,
    ) = sync(
        [
            history_front,
            history_last,
            grad_normed_ffn,
            grad_upper,
            grad_kept,
            grad_given,
            out_kept,
            out_given,
        ],
        [newest_all, stored_last, grad_project] + stored_pair,
    )

    summed = [None, None, None, Scatter(grad_normed_ffn, "tensor", in_first)]
    summed[3].step(0)
    send_far(history_front, first_far)
    send_far(history_front, near_spots)
    grad_project.near()
    grad_heads = (
        jnp.dot(grad_kept, out_kept, preferred_element_type=float_type)
        + jnp.dot(grad_given, out_given, preferred_element_type=float_type)
    ).astype(bf16_type)
    grad_proj = attend_back(turned, grad_heads, tables, seq_ids)
    grad_normed_attend = [
        jnp.concatenate(
            [
                contract_cols(grad_proj[index], weights[index]).astype(bf16_type)
                for weights in (attend_kept, attend_given)
            ],
            axis=-1,
        )
        for index in range(3)
    ]
    grad_proj_late, upper_late, near_pieces = sync(
        [grad_proj, grad_upper, [history_front[spot] for spot in near_spots]], []
    )
    for spot, piece in zip(near_spots, near_pieces):
        history_front[spot] = piece
    grad_attend = Reduce(
        *attend_grads_call(normed_kept, normed_given, grad_proj_late, grad_kept, grad_given, heads_out),
        "dp",
        1,
    )
    grad_expand = Reduce(*expand_grads(normed_kept, normed_given, upper_late), "dp", 0)
    grad_normed_attend, grad_normed_ffn, history_front, history_last, layer_late = sync(
        [grad_normed_attend, grad_normed_ffn, history_front, history_last, layer_late],
        [grad_attend, grad_expand, grad_project, newest_all, summed[3]] + stored_pair,
    )

    for index in range(3):
        summed[index] = Scatter(grad_normed_attend[index], "tensor", out_first)
    summed[0].step(0)
    summed[3].step(1)
    send_far(history_front, last_far)
    grad_expand.near()
    newest_all.step(1)
    (layer_late,) = sync([layer_late], [grad_expand])
    all_grads = list(enumerate(grad_normed_attend + [grad_normed_ffn]))
    sums = [
        norm_sums(grads[None], layer_late, index, place, owners)[0] for index, grads in all_grads[:2]
    ]
    grad_project.prepare()
    sums, all_grads[2:], history_front, history_last = sync(
        [sums, [grads for index, grads in all_grads[2:]], history_front, history_last],
        summed + [newest_all, grad_project, grad_attend, grad_expand],
    )

    sums = sums + [
        norm_sums(grads[None], layer_late, index + 2, place, owners)[0]
        for index, grads in enumerate(all_grads[2:])
    ]
    summed[1].step(0)
    summed[3].step(2)
    summed[0].step(1)
    grad_project.far()
    grad_attend.near()
    sums, history_front, history_last = sync(
        [sums, history_front, history_last], summed + [grad_project, grad_expand, grad_attend]
    )

    def back(index):
        return Gather(
            back_share(
                summed[index].values,
                summed[index].moved,
                input_share[index],
                norm_vals[index][None],
                grad_newest if index == 3 else None,
                place,
                owners,
            ),
            "tensor",
            back_order,
        )

    gathered = [None, None, None, back(3)]
    summed[2].step(0)
    summed[1].step(1)
    step_both(summed[0], 2, gathered[3], 0)
    norm_pack = jnp.stack(sums)
    own_rows_out = jnp.stack(
        [
            lax.dynamic_index_in_dim(
                grad_mixer_out.reshape(owners, mixers * MIXH), me ^ index, 0, False
            )
            for index in order
        ]
    )
    pack = Halves(
        jnp.concatenate(
            [
                norm_pack[:, 0],
                norm_pack[:, 1],
                mixer_gain,
                grad_mixer_in,
                jnp.pad(own_rows_out, ((0, 0), (0, cols - mixers * MIXH))).reshape(1, width),
            ],
            axis=0,
        ),
        "dp",
    )
    send_far(history_last, far_spots)
    grad_expand.prepare()
    project_squares, history_last = sync(
        [grad_project.squares(), history_last],
        summed[0:3] + [gathered[3], grad_expand, grad_project, grad_attend, newest_all, pack],
    )

    gathered[0] = back(0)
    newest_all.step(2)
    step_both(summed[2], 1, gathered[3], 1)
    step_both(summed[1], 2, gathered[0], 0)
    grad_expand.far()
    grad_attend.prepare()
    pack.near()
    pack.far()
    grad_history = jnp.zeros(history.shape, bf16_type)
    for spot, index in enumerate(order):
        first_row = (me ^ index) * tokens_here
        for pieces, layer in ((history_front, 0), (history_last, layer_count - 2)):
            if pieces[spot] is not None:
                grad_history = lax.dynamic_update_slice(
                    grad_history, pieces[spot], (layer, first_row, 0)
                )
    (grad_history,) = sync(
        [grad_history],
        summed[1:3] + [gathered[0], gathered[3], newest_all, grad_attend, grad_expand, pack],
    )

    gathered[1] = back(1)
    gathered[3].step(2)
    step_both(summed[2], 2, gathered[1], 0)
    gathered[0].step(1)
    grad_attend.far()
    pack.rows("tensor", near)
    newest_whole = newest_all.result()
    newest_stored = [item.result()[0] for item in stored_pair] + [stored_last.result()[0]]
    next_inputs = next_layer(mix_weights, newest_stored, newest_whole, place, owners)
    expand_squares, newest_whole, next_inputs = sync(
        [grad_expand.squares(), newest_whole, next_inputs],
        [summed[2], gathered[0], gathered[1], gathered[3], grad_attend, pack],
    )

    gathered[2] = back(2)
    gathered[0].step(2)
    gathered[2].step(0)
    gathered[1].step(1)
    pack.rows("tensor", side_bits)
    pack.rows("tensor", far)
    entry_pieces = [newest_whole[:, spot * cols : (spot + 1) * cols] for spot in range(owners)]
    send_far(entry_pieces, first_far)
    grad_inputs = gathered[3].place_new(4, 3)
    shard_squares = project_squares + expand_squares + grad_attend.squares()
    shard_squares, entry_pieces, grad_inputs = sync(
        [shard_squares, entry_pieces, grad_inputs],
        [gathered[0], gathered[1], gathered[2], pack],
    )

    own_pack = pack.values
    norm_grad = own_pack[0:9]
    grad_mixer_in = own_pack[9 : 9 + MIXH].T
    grad_mixer_out = own_pack[9 + MIXH, 0 : mixers * MIXH].reshape(mixers, MIXH)
    shared_squares = (
        square_sum(norm_grad) + square_sum(grad_mixer_in) + square_sum(grad_mixer_out)
    )
    total_squares = jnp.full((1, 128), shard_squares + shared_squares / tensor_size)
    for axis, bits in (("dp", bits_of(owners)[:1]), ("tensor", side_bits + far)):
        for bit in bits:
            total_squares = total_squares + swap(total_squares, axis, bit)
    (total_squares,) = sync([total_squares], [gathered[2]])
    for axis, bits in (("dp", bits_of(owners)[1:]), ("tensor", near)):
        for bit in bits:
            total_squares = total_squares + swap(total_squares, axis, bit)
    gathered[1].step(2)
    gathered[2].step(1)
    send_far(entry_pieces, last_far)
    send_far(entry_pieces, near_spots)
    grad_inputs = gathered[0].place_last(grad_inputs, 0)
    new_entry = jnp.zeros(grad_entry.shape, bf16_type)
    entry_late = last_far + near_spots
    for spot in range(owners):
        if spot not in entry_late:
            first_row = (me ^ order[spot]) * tokens_here
            new_entry = lax.dynamic_update_slice_in_dim(
                new_entry, entry_pieces[spot], first_row, 0
            )
    total_squares, entry_pieces, grad_inputs, new_entry = sync(
        [total_squares, entry_pieces, grad_inputs, new_entry], [gathered[1], gathered[2]]
    )
    total_squares = total_squares[0, 0]

    gathered[2].step(2)
    grad_norm = jnp.sqrt(total_squares)
    factor = jnp.minimum(1.0, clip_level / grad_norm)
    wide_rate = 2.0 / math.sqrt(D)
    wide = (wide_rate, weight_decay)
    norms_out = adam_step(norms_master, norms_first, norms_second, norm_grad, factor, 1.0, 0.0)
    mixer_in_out = adam_step(
        mixer_in_master,
        mixer_in_first,
        mixer_in_second,
        grad_mixer_in,
        factor,
        wide_rate,
        weight_decay,
    )
    mixer_out_out = adam_step(
        mixer_out_master,
        mixer_out_first,
        mixer_out_second,
        grad_mixer_out,
        factor,
        2.0 / math.sqrt(MIXH),
        weight_decay,
    )
    parts = attend_in_master.shape[0]
    attend_in_out = adam_step(
        attend_in_master,
        attend_in_first,
        attend_in_second,
        grad_attend.own()[0:parts],
        factor,
        wide_rate,
        weight_decay,
    )
    attend_out_out = adam_call(
        grad_attend.terms,
        attend_out_master,
        attend_out_first,
        attend_out_second,
        factor,
        wide,
        (1, attend_out_master.shape[1] // 128),
        (attend_out_master.shape[0], 128),
        parts,
    )
    expand_out = adam_step(
        expand_master,
        expand_first,
        expand_second,
        grad_expand.own(),
        factor,
        wide_rate,
        weight_decay,
    )
    project_out = adam_step(
        project_master,
        project_first,
        project_second,
        grad_project.own(),
        factor,
        2.0 / math.sqrt(FF),
        weight_decay,
    )
    for spot in entry_late:
        first_row = (me ^ order[spot]) * tokens_here
        new_entry = lax.dynamic_update_slice_in_dim(new_entry, entry_pieces[spot], first_row, 0)
    for index in (1, 2):
        grad_inputs = gathered[index].place_last(grad_inputs, index)
    grad_inputs = grad_inputs.reshape(layer_inputs.shape)
    return (
        next_inputs,
        new_entry,
        grad_inputs,
        grad_history,
        norms_out[0],
        norms_out[1],
        norms_out[2],
        attend_in_out[0],
        attend_in_out[1],
        attend_in_out[2],
        attend_in_out[0].astype(bf16_type),
        attend_out_out[0],
        attend_out_out[1],
        attend_out_out[2],
        attend_out_out[3],
        expand_out[0],
        expand_out[1],
        expand_out[2],
        expand_out[0].astype(bf16_type),
        project_out[0],
        project_out[1],
        project_out[2],
        project_out[0].astype(bf16_type),
        mixer_in_out[0],
        mixer_in_out[1],
        mixer_in_out[2],
        mixer_in_out[0].astype(bf16_type),
        mixer_out_out[0],
        mixer_out_out[1],
        mixer_out_out[2],
        mixer_out_out[0].astype(bf16_type),
        grad_norm,
    )


def solution(mesh):
    in_specs = (
        P(None, "dp", None),
        P(None, None, "dp"),
        P("dp"),
        P(None, "dp"),
        P(None, "dp"),
        P(None, "dp"),
        P(None, "dp", "tensor"),
        P(None, "dp", "tensor"),
        P(None, "dp", "tensor"),
        P("tensor", "dp"),
        P("tensor", "dp"),
        P("tensor", "dp"),
        P("dp", "tensor"),
        P("dp", "tensor"),
        P("dp", "tensor"),
        P("tensor", "dp"),
        P("tensor", "dp"),
        P("tensor", "dp"),
        P("dp", None),
        P("dp", None),
        P("dp", None),
        P("dp", None),
        P("dp", None),
        P("dp", None),
        P(None, "dp", None),
        P(None, "dp"),
    )
    out_specs = (
        P(None, "dp", None),
        P(None, "dp"),
        P(None, "dp", None),
        P(None, None, "dp"),
        P(None, "dp"),
        P(None, "dp"),
        P(None, "dp"),
        P(None, "dp", "tensor"),
        P(None, "dp", "tensor"),
        P(None, "dp", "tensor"),
        P(None, "dp", "tensor"),
        P("tensor", "dp"),
        P("tensor", "dp"),
        P("tensor", "dp"),
        P("tensor", "dp"),
        P("dp", "tensor"),
        P("dp", "tensor"),
        P("dp", "tensor"),
        P("dp", "tensor"),
        P("tensor", "dp"),
        P("tensor", "dp"),
        P("tensor", "dp"),
        P("tensor", "dp"),
        P("dp", None),
        P("dp", None),
        P("dp", None),
        P("dp", None),
        P("dp", None),
        P("dp", None),
        P("dp", None),
        P("dp", None),
        P(),
    )
    return jax.shard_map(body, mesh=mesh, in_specs=in_specs, out_specs=out_specs, check_vma=False)
```
